256 devices in a mesh: table: 32 (over x, y, core), fsdp: 8 (over z).
Axes of the slice: x: 4, y: 4, z: 8, core: 2. Of those that a mesh axis runs over, the one named last changes fastest.
Arguments:
- item_table: bfloat16 [65536, 1024], P('table'), may hold values from -36 to 36
- item_row: int32 [32768], P(('table', 'fsdp')), may hold values from 0 to 2047
- item_owner: int32 [32768, 1], P(('table', 'fsdp')), may hold values from 0 to 31; in each aligned block of 128 rows (0 to 127, 128 to 255, ...) at most 6 rows name the same one
- user_lengths: int32 [256, 8], P(('table', 'fsdp')), may hold values from 1 to 64, 128 in all within a row
- w_mix: bfloat16 [1024, 2048], P('fsdp'), may hold values from -0.1875 to 0.1875
- w_out: bfloat16 [512, 1024], P('fsdp'), may hold values from -0.25 to 0.25
- gain_in: float32 [1024], replicated, may hold values from 0.4 to 7.2
- gain_attn: float32 [512], replicated, may hold values from 0.4 to 7.2
- cotangent: bfloat16 [32768, 1024], P(('table', 'fsdp')), may hold values from -6 to 6
Outputs:
- layer_out: bfloat16 [32768, 1024], P(('table', 'fsdp'))
- table_grad: float32 [65536, 1024], P(('table', 'fsdp'))
- mix_grad: float32 [1024, 2048], P('fsdp')
- out_grad: float32 [512, 1024], P('fsdp')
The draws below stay inside these ranges and needn't reach their ends.
Inputs may be any that keep to these rules, and one draw needn't show every extreme that they name: `item_owner`: among the 128 actions of one device, at most 6 name one owner, and in every draw some owner is named by exactly 6 actions of some device. `user_lengths`: each row sums to 128 and its longest history has 64 actions.
All inputs are finite; a program needn't handle non-finite values.
Results may differ from the reference program's by a relative error of at most 0.025.
Values may be sent and summed in bfloat16 or wider, within the bound.
No kernel may reach another device: no remote copies, remote signals or barrier semaphores. Data moves between devices by JAX's collectives and lax.ppermute only.
A program may use at most 128 MiB of HBM per device.

```python
import math
import jax
import jax.numpy as jnp
import numpy as np
from jax import lax

D = 1024
H = 4
DH = 128
TOK_DEV = 128
USERS_DEV = 8
TROWS = 2048
MAXLEN = 64
CAP = 6
TOKENS = 32768
ITEMS = 65536
N_TABLE = 32
N_FSDP = 8


def ramped_gain(key, count, base, lower, upper):
    position = jnp.arange(count, dtype=jnp.float32) / count
    noise = jax.random.uniform(key, (count,), jnp.float32, lower, upper)
    return jnp.power(base, position) * noise


def draw_item_table(key, part):
    key = jax.random.fold_in(key, 3)
    key_rows, key_cols, key_body = jax.random.split(key, 3)
    row_scale = jnp.exp(jax.random.uniform(key_rows, (ITEMS, 1), jnp.float32, jnp.log(0.3), jnp.log(3.0)))
    col_scale = jnp.exp(jax.random.uniform(key_cols, (1, D), jnp.float32, jnp.log(0.3), jnp.log(3.0)))
    base = jax.random.truncated_normal(key_body, -4.0, 4.0, (ITEMS, D), jnp.float32)
    return (base * row_scale * col_scale).astype(jnp.bfloat16)


def draw_gain_in(key, part):
    key = jax.random.fold_in(key, 5)
    return ramped_gain(key, D, 3.0, 0.5, 1.6)


def draw_gain_attn(key, part):
    key = jax.random.fold_in(key, 7)
    return ramped_gain(key, H * DH, 3.0, 0.5, 1.6)


def with_ends(drawn, key, low, high):
    longest = drawn.shape.index(max(drawn.shape))
    spots = []
    for shift in (0, 1):
        where = [jax.random.randint(jax.random.fold_in(key, axis), (), 0, length) for axis, length in enumerate(drawn.shape)]
        where[longest] = (where[longest] + shift) % drawn.shape[longest]
        spots.append(tuple(where))
    return drawn.at[spots[0]].set(low).at[spots[1]].set(high)


def block_scale(own_key, dims, cuts, low, high):
    factor_of, own = 1.0, jax.random.fold_in(own_key, 6)
    for dim, blocks in cuts:
        steps = jnp.exp(jax.random.uniform(jax.random.fold_in(own, dim), (blocks,), jnp.float32, low / len(cuts), high / len(cuts)))
        factor_of = factor_of * jnp.repeat(steps, dims[dim] // blocks).reshape([-1 if axis == dim else 1 for axis in range(len(dims))])
    return factor_of


def cumulative_ranks(number_of, slope):
    weights = [(1 << 20) // math.isqrt(rank ** slope) + 1 for rank in range(1, number_of + 1)]
    deviation = 1 + sum(weights) // (1 << 30)
    return np.cumsum(np.array([max(1, weight // deviation) for weight in weights]))


def skewed_ids(stream_key, dims, amount, skew):
    grid = cumulative_ranks(amount, skew)
    ticket = jax.random.randint(jax.random.fold_in(stream_key, 1), dims, 0, int(grid[amount - 1]))
    rank = jnp.searchsorted(jnp.asarray(grid, jnp.int32), ticket, side="right")
    return jax.random.permutation(jax.random.fold_in(stream_key, 2), amount)[rank].astype(jnp.int32)


def length_profile(count, total, limit, slope):
    weights = [(1 << 20) // math.isqrt(rank ** slope) + 1 for rank in range(2, count + 1)]
    spare, holding = total - limit - (count - 1), [1] * (count - 1)
    while spare > 0:
        movable = [i for i in range(count - 1) if holding[i] < limit]
        pool, remaining = sum([weights[i] for i in movable]), spare
        for i in movable:
            addition = min(limit - holding[i], max(1, remaining * weights[i] // pool), spare)
            holding[i] = holding[i] + addition
            spare = spare - addition
    return np.array([limit] + holding)


def ragged(rng, count, total, limit, skew):
    if count == 2:
        one = jax.random.randint(rng, (), max(1, total - limit), min(limit, total - 1) + 1)
        return jnp.stack([one, total - one])
    tallies = jnp.asarray(length_profile(count, total, limit, skew), jnp.int32)
    couples = (count - 1) // 2
    giver, sink = tallies[1:1 + 2 * couples:2], tallies[2:2 + 2 * couples:2]
    slack = jnp.minimum(giver - 1, limit - sink)
    passed = jax.random.randint(jax.random.fold_in(rng, 1), (couples,), 0, 1 << 20) % (slack + 1)
    tallies = tallies.at[1:1 + 2 * couples:2].set(giver - passed).at[2:2 + 2 * couples:2].set(sink + passed)
    return tallies[jax.random.permutation(jax.random.fold_in(rng, 2), count)]


def routed_block(rng, own, number, rows, number_of, top, limit, skew):
    order = jax.random.permutation(rng, number_of)
    crowded, usual = portions_of(number_of, rows * top, limit, skew, True), portions_of(number_of, rows * top, limit, skew, False)
    places = jnp.arange(number_of)

    def named(sizes, rotation):
        used = int((sizes > 0).sum())
        fixed = max(1, used // 4)
        moved = fixed + (places - fixed + rotation * (used - fixed)) % max(1, number_of - fixed)
        return jnp.zeros((number_of,), jnp.int32).at[order[jnp.where(places < fixed, places, moved)]].set(jnp.asarray(sizes, jnp.int32))

    sizes = jnp.where(number % 4 == 0, named(crowded, number // 4), named(usual, number - number // 4 - 1))
    mixed = jax.random.permutation(jax.random.fold_in(own, 3), number_of)
    giver, taker = mixed[0:number_of // 2 * 2:2], mixed[1:number_of // 2 * 2:2]
    margin = jnp.minimum(sizes[giver] - 1, limit - sizes[taker]) // 2
    margin = jnp.where((giver == order[0]) | (taker == order[0]) | (sizes[taker] == 0), 0, jnp.maximum(margin, 0))
    moved = jax.random.randint(jax.random.fold_in(own, 4), (number_of // 2,), 0, 1 << 20) % (margin + 1)
    sizes = sizes.at[giver].add(-moved).at[taker].add(moved)
    members = jnp.searchsorted(jnp.cumsum(sizes), jnp.arange(rows * top), side="right").astype(jnp.int32)
    grid = members.reshape(top, rows).T
    grid = grid[jax.random.permutation(jax.random.fold_in(own, 1), rows)]
    rotation = jax.random.randint(jax.random.fold_in(own, 2), (rows, 1), 0, top)
    return jnp.take_along_axis(grid, (jnp.arange(top)[None, :] + rotation) % top, axis=1)


def portions_of(number_of, total, bound, skew, full):
    loads = [(1 << 20) // math.isqrt(grade ** skew) + 1 for grade in range(1, number_of + 1)]
    largest = bound if full else min(bound, max(-(-total // number_of), total * loads[0] // sum(loads)))
    least = 1 if total - largest >= number_of - 1 else 0
    given, rest = [largest] + [least] * (number_of - 1), total - largest - least * (number_of - 1)
    while rest > 0:
        free = [i for i in range(1, number_of) if given[i] < largest] or [i for i in range(1, number_of) if given[i] < bound]
        whole, remaining = sum([loads[i] for i in free]), rest
        for i in free:
            extra = min(bound - given[i], max(1, remaining * loads[i] // whole), rest)
            given[i] = given[i] + extra
            rest = rest - extra
    return np.array(given)


def scatter_about(stream_key, shape, spread, reach, pieces=(), kind=jnp.bfloat16):
    gain = block_scale(stream_key, shape, pieces, -0.22, 0.18) if pieces else 1.0
    entries = jax.random.normal(stream_key, shape, jnp.float32) * spread * gain
    return jnp.minimum(jnp.maximum(entries, -reach), reach).astype(kind)


def setup_inputs(seed: int = 0) -> dict:
    splits = jax.random.split(jax.random.key(seed), 10)
    item_table = draw_item_table(jax.random.fold_in(splits[9], 71), 0)
    item_row = with_ends(skewed_ids(splits[1], (TOKENS,), TROWS, 2), jax.random.fold_in(splits[1], 3), 0, TROWS - 1).astype(jnp.int32)
    item_owner_keys = jax.random.split(jax.random.fold_in(splits[2], 1), TOKENS // TOK_DEV)
    item_owner_turns = jax.random.permutation(jax.random.fold_in(splits[2], 3), TOKENS // TOK_DEV)
    item_owner = jax.vmap(lambda own, number: routed_block(jax.random.fold_in(splits[2], 2), own, number, TOK_DEV, N_TABLE, 1, CAP, 2))(item_owner_keys, item_owner_turns).reshape((TOKENS, 1))
    user_lengths = jax.vmap(lambda own: ragged(own, USERS_DEV, TOK_DEV, MAXLEN, 2))(jax.random.split(splits[3], (N_TABLE * N_FSDP))).reshape((N_TABLE * N_FSDP, USERS_DEV)).astype(jnp.int32)
    w_mix = scatter_about(splits[4], (D, 4 * H * DH), D ** -0.5, 0.1875, ((0, 8),))
    w_out = scatter_about(splits[5], (H * DH, D), (H * DH) ** -0.5, 0.25, ((0, 8),))
    gain_in = draw_gain_in(jax.random.fold_in(splits[9], 71), 0)
    gain_attn = draw_gain_attn(jax.random.fold_in(splits[9], 71), 0)
    cotangent = scatter_about(splits[8], (TOKENS, D), 1.0, 6.0, ((0, 256),))
    return dict(item_table=item_table, item_row=item_row, item_owner=item_owner, user_lengths=user_lengths, w_mix=w_mix, w_out=w_out, gain_in=gain_in, gain_attn=gain_attn, cotangent=cotangent)


def segment_mask(lengths_row, row_count):
    seg_ends = jnp.cumsum(lengths_row).astype(jnp.int32)
    position = jnp.arange(row_count, dtype=jnp.int32)
    segment = lax.optimization_barrier(jnp.sum((position[:, None] >= seg_ends[None, :]).astype(jnp.int32), axis=1))
    same_user = segment[:, None] == segment[None, :]
    causal = position[None, :] <= position[:, None]
    return same_user & causal

def layer_norm(inputs, scales):
    average = lax.optimization_barrier(jnp.mean(inputs, axis=-1, keepdims=True))
    centered = inputs - average
    variance = lax.optimization_barrier(jnp.mean(centered * centered, axis=-1, keepdims=True))
    return centered * lax.rsqrt(variance + 1e-05) * scales

def layer_forward(embedded, w_mix, w_out, gain_in, gain_attn, allowed):
    row_count = embedded.shape[0]
    attn_width = H * DH
    widened = embedded.astype(jnp.float32)
    normed = layer_norm(widened, gain_in).astype(jnp.bfloat16)
    mixture = jnp.dot(normed, w_mix, preferred_element_type=jnp.float32)
    activated = jax.nn.silu(mixture).astype(jnp.bfloat16)
    gate_u = activated[:, :attn_width]
    value_heads = activated[:, attn_width:2 * attn_width].reshape(row_count, H, DH)
    query_heads = activated[:, 2 * attn_width:3 * attn_width].reshape(row_count, H, DH)
    key_heads = activated[:, 3 * attn_width:].reshape(row_count, H, DH)
    scores = jnp.einsum('ihd,jhd->hij', query_heads, key_heads, preferred_element_type=jnp.float32) * DH ** (-0.5)
    weights = (jnp.where(allowed[None], jax.nn.silu(scores), 0.0) / MAXLEN).astype(jnp.bfloat16)
    attended = jnp.einsum('hij,jhd->ihd', weights, value_heads, preferred_element_type=jnp.float32)
    attended = attended.reshape(row_count, attn_width).astype(jnp.bfloat16)
    gated_rows = (layer_norm(attended.astype(jnp.float32), gain_attn) * gate_u.astype(jnp.float32)).astype(jnp.bfloat16)
    layer_out = widened + jnp.dot(gated_rows, w_out, preferred_element_type=jnp.float32)
    return layer_out.astype(jnp.bfloat16)

def reference(item_table, item_row, item_owner, user_lengths, w_mix, w_out, gain_in, gain_attn, cotangent):
    flat_index = (item_owner[:, 0] * TROWS + item_row).astype(jnp.int32)
    embedded = jnp.take(item_table, flat_index, axis=0)
    block_count = user_lengths.shape[0]

    def block_step(sums_so_far, inputs):
        emb_block, len_row, cot_block = inputs
        allowed = segment_mask(len_row, TOK_DEV)

        def apply_layer(emb_rows, mix_full, out_full):
            return layer_forward(emb_rows, mix_full, out_full, gain_in, gain_attn, allowed)
        result, pullback = jax.vjp(apply_layer, emb_block, w_mix, w_out)
        d_emb, d_mix, d_out = pullback(cot_block)
        return ((sums_so_far[0] + d_mix.astype(jnp.float32), sums_so_far[1] + d_out.astype(jnp.float32)), (result, d_emb))
    start_sums = (jnp.zeros(w_mix.shape, jnp.float32), jnp.zeros(w_out.shape, jnp.float32))
    (mix_sum, out_sum), (results, d_embs) = lax.scan(block_step, start_sums, (embedded.reshape(block_count, TOK_DEV, D), user_lengths, cotangent.reshape(block_count, TOK_DEV, D)))
    layer_out = results.reshape(TOKENS, D)
    d_embedded = d_embs.reshape(TOKENS, D)
    table_grad = jnp.zeros((ITEMS, D), jnp.float32).at[flat_index].add(d_embedded.astype(jnp.float32))
    mix_root = jnp.sqrt(jnp.mean(mix_sum * mix_sum) + 1e-06)
    out_root = jnp.sqrt(jnp.mean(out_sum * out_sum) + 1e-06)
    mix_grad = mix_sum * jnp.minimum(1.0, 1.0 / mix_root)
    out_grad = out_sum * jnp.minimum(1.0, 1.0 / out_root)
    return (layer_out, table_grad, mix_grad, out_grad)
```

```python
import jax
import jax.numpy as jnp
from jax import lax
from jax.experimental import pallas as pl
from jax.experimental.pallas import tpu as pltpu
from jax.sharding import Mesh
from jax.sharding import PartitionSpec as P

H = 4
DH = 128
MAXLEN = 64
TOK = 128
D = 1024
AW = H * DH
OWNERS = 32
CAP = 6
SLOTS = 8
NZ = 8
XY = 16
PROWS = 16
PCOLS = 640
GROWS = OWNERS * CAP + 16
TABLE = ("x", "y", "core")
ALL = ("x", "y", "core", "z")
F32 = jnp.float32
BF16 = jnp.bfloat16
MB = 1024 * 1024


def mm(a, b):
    return lax.dot_general(a, b, (((1,), (0,)), ((), ())), preferred_element_type=F32)


def mm_nt(a, b):
    return lax.dot_general(a, b, (((1,), (1,)), ((), ())), preferred_element_type=F32)


def mm_tn(a, b):
    return lax.dot_general(a, b, (((0,), (0,)), ((), ())), preferred_element_type=F32)


def iota(shape, dim):
    return lax.broadcasted_iota(jnp.int32, shape, dim)


def plan_kernel(owner_ref, row_ref, req_ref, tgt_ref):
    square = (TOK, TOK)
    lane = iota(square, 1)

    def column(values):
        return jnp.broadcast_to(values.astype(F32), square).T

    row = row_ref[...]
    owner = column(owner_ref[...])
    low, high = column(row & 127), column(row >> 7)
    onehot = owner == lane.astype(F32)
    onehot_f = onehot.astype(F32)
    onehot_b = onehot_f.astype(BF16)
    earlier = (lane < iota(square, 0)).astype(F32).astype(BF16)
    before = mm(earlier, onehot_b)
    slot = jnp.sum(before * onehot_f, axis=1, keepdims=True)
    tgt_ref[...] = (owner * SLOTS + slot).astype(jnp.int32)
    here = slot == lane.astype(F32)
    low = jnp.where(here, low, 0.0).astype(BF16)
    high = jnp.where(here, high, 0.0).astype(BF16)
    requests = mm_tn(onehot_b, low) + 128.0 * mm_tn(onehot_b, high)
    req_ref[...] = requests[:OWNERS].astype(jnp.int32)


def layer_kernel(
    lens_ref, got_ref, tgt_ref, weights_ref, gin_ref, gat_ref, ct_ref,
    out_ref, slots_ref, keep_ref, send_ref,
    wm, wo, dmx, sems,
):
    core = lax.axis_index("core")
    copies = []
    for half in range(2):
        copies.append(
            pltpu.make_async_copy(
                weights_ref.at[half, :, pl.ds(0, TOK), :], wm.at[half], sems.at[half]
            )
        )
    for half in range(2):
        copies.append(
            pltpu.make_async_copy(
                weights_ref.at[half, :, pl.ds(TOK, 32), :], wo.at[:, half], sems.at[2 + half]
            )
        )
    for copy in copies:
        copy.start()

    pick = (tgt_ref[:, :1] == iota((TOK, OWNERS * SLOTS), 1)).astype(F32).astype(BF16)
    emb = mm(pick, got_ref[...])
    gin = gin_ref[...]
    gat = gat_ref[...]
    centered = emb - jnp.mean(emb, axis=1, keepdims=True)
    rstd = lax.rsqrt(jnp.mean(centered * centered, axis=1, keepdims=True) + 1e-05)
    xhat = centered * rstd
    normed = (xhat * gin).astype(BF16)

    position, other = iota((TOK, TOK), 0), iota((TOK, TOK), 1)
    seg_row = jnp.zeros((TOK, TOK), jnp.int32)
    seg_col = jnp.zeros((TOK, TOK), jnp.int32)
    end = 0
    for user in range(lens_ref.shape[1]):
        end = end + lens_ref[0, user]
        seg_row = seg_row + (position >= end).astype(jnp.int32)
        seg_col = seg_col + (other >= end).astype(jnp.int32)
    allowed = (seg_row == seg_col) & (other <= position)

    copies[0].wait()
    wm0 = wm[0].reshape(D, D)
    mix0 = mm(normed, wm0)
    copies[1].wait()
    wm1 = wm[1].reshape(D, D)
    mix1 = mm(normed, wm1)

    sig0, sig1 = jax.nn.sigmoid(mix0), jax.nn.sigmoid(mix1)
    act0, act1 = (mix0 * sig0).astype(BF16), (mix1 * sig1).astype(BF16)
    slope0 = sig0 * (1.0 + mix0 * (1.0 - sig0))
    slope1 = sig1 * (1.0 + mix1 * (1.0 - sig1))
    gate_u = act0[:, :AW].astype(F32)

    heads = []
    attended = []
    for h in range(H):
        val = act0[:, AW + h * DH : AW + (h + 1) * DH]
        qry = act1[:, h * DH : (h + 1) * DH]
        key = act1[:, AW + h * DH : AW + (h + 1) * DH]
        score = mm_nt(qry, key) * DH ** (-0.5)
        sig = jax.nn.sigmoid(score)
        wgt = (jnp.where(allowed, score * sig, 0.0) / MAXLEN).astype(BF16)
        attended.append(mm(wgt, val).astype(BF16))
        slope = jnp.where(allowed, sig * (1.0 + score * (1.0 - sig)), 0.0) * (
            DH ** (-0.5) / MAXLEN
        )
        heads.append((val, qry, key, wgt, slope))
    att = jnp.concatenate(attended, axis=1).astype(F32)
    acent = att - jnp.mean(att, axis=1, keepdims=True)
    arstd = lax.rsqrt(jnp.mean(acent * acent, axis=1, keepdims=True) + 1e-05)
    ahat = acent * arstd
    scaled = ahat * gat
    gated = (scaled * gate_u).astype(BF16)

    copies[2].wait()
    copies[3].wait()
    w_out = wo[...].reshape(AW, D)
    ct = ct_ref[...]
    out_ref[...] = (emb + mm(gated, w_out)).astype(BF16)

    d_gated = mm_nt(ct, w_out).astype(BF16).astype(F32)
    d_gate = (d_gated * scaled).astype(BF16).astype(F32)
    d_ahat = d_gated * gate_u * gat
    d_att = arstd * (
        d_ahat
        - jnp.mean(d_ahat, axis=1, keepdims=True)
        - ahat * jnp.mean(d_ahat * ahat, axis=1, keepdims=True)
    )
    d_att = d_att.astype(BF16)
    d_val, d_qry, d_key = [], [], []
    for h in range(H):
        val, qry, key, wgt, slope = heads[h]
        d_head = d_att[:, h * DH : (h + 1) * DH]
        d_wgt = mm_nt(d_head, val).astype(BF16).astype(F32)
        d_val.append(mm_tn(wgt, d_head).astype(BF16))
        d_score = (d_wgt * slope).astype(BF16)
        d_qry.append(mm(d_score, key).astype(BF16))
        d_key.append(mm_tn(d_score, qry).astype(BF16))
    d_act0 = jnp.concatenate([d_gate] + [v.astype(F32) for v in d_val], axis=1)
    d_act1 = jnp.concatenate([v.astype(F32) for v in d_qry + d_key], axis=1)
    d_mix0 = (d_act0 * slope0).astype(BF16)
    d_mix1 = (d_act1 * slope1).astype(BF16)
    dmx[0] = d_mix0
    dmx[1] = d_mix1
    d_normed = (mm_nt(d_mix0, wm0) + mm_nt(d_mix1, wm1)).astype(BF16).astype(F32)
    d_xhat = d_normed * gin
    d_emb = (
        rstd
        * (
            d_xhat
            - jnp.mean(d_xhat, axis=1, keepdims=True)
            - xhat * jnp.mean(d_xhat * xhat, axis=1, keepdims=True)
        )
        + ct.astype(F32)
    ).astype(BF16)
    slots_ref[...] = mm_tn(pick, d_emb).astype(BF16)

    for side, dst in ((1 - core, send_ref), (core, keep_ref)):
        d_mix = dmx[side]
        ct_half = ct_ref[:, pl.ds(pl.multiple_of(side * AW, AW), AW)]
        for z in range(NZ):
            grad = mm_tn(normed[:, z * TOK : (z + 1) * TOK], d_mix).astype(BF16)
            for g in range(8):
                for c in range(2):
                    dst[g * 2 + c, z, :, 0:512] = grad[
                        g * PROWS : (g + 1) * PROWS, c * 512 : (c + 1) * 512
                    ]
        for pair in range(NZ // 2):
            grad = mm_tn(gated[:, pair * TOK : (pair + 1) * TOK], ct_half).astype(BF16)
            for sub in range(2):
                for r in range(4):
                    for c in range(4):
                        dst[r * 4 + c, pair * 2 + sub, :, 512:PCOLS] = grad[
                            sub * 64 + r * PROWS : sub * 64 + (r + 1) * PROWS,
                            c * 128 : (c + 1) * 128,
                        ]


def pack_kernel(rows_ref, asked_ref, out_ref):
    used = OWNERS * CAP
    r, k = iota((used, OWNERS * SLOTS), 0), iota((used, OWNERS * SLOTS), 1)
    take = (r // CAP == k // SLOTS) & (r % CAP == k % SLOTS)
    out_ref[:used] = mm(take.astype(F32).astype(BF16), rows_ref[...]).astype(BF16)
    asked = asked_ref[...]
    owner = (iota((256, OWNERS), 0) // CAP == iota((256, OWNERS), 1)).astype(F32).astype(BF16)
    slot = iota((256, 128), 0) % CAP == iota((256, 128), 1)
    parts = []
    for part in (asked & 127, asked >> 7):
        spread = mm(owner, part.astype(F32).astype(BF16))
        column = jnp.sum(jnp.where(slot, spread, 0.0), axis=1, keepdims=True)
        parts.append(jnp.broadcast_to(column, (256, 128)).T[:PROWS])
    which = iota((PROWS, 256), 0)
    numbers = jnp.where(which == 0, parts[0], jnp.where(which == 1, parts[1], 0.0))
    out_ref[used:] = jnp.concatenate(
        [numbers.astype(BF16), jnp.zeros((PROWS, D - 256), BF16)], axis=1
    )


def table_kernel(rows_ref, out_ref):
    used = OWNERS * CAP
    first = lax.axis_index("z") * 256
    total = jnp.zeros((256, D), F32)
    for z in range(NZ):
        low = rows_ref[z, used : used + PROWS, :256].astype(F32)
        number = (low[0:1] + 128.0 * low[1:2]).astype(jnp.int32)[:, :used] - first
        here = (iota((256, used), 0) == number).astype(F32).astype(BF16)
        total = total + mm(here, rows_ref[z, :used])
    out_ref[...] = total


def square_kernel(sums_ref, out_ref):
    sums = sums_ref[...].astype(F32)
    sq = sums * sums
    mix = jnp.sum(sq[:, :, :512])
    out = jnp.sum(sq[:, :, 512:])
    lane = iota((NZ, 8, 128), 2)
    out_ref[...] = jnp.where(lane == 0, mix, jnp.where(lane == 1, out, 0.0))


def scale_kernel(sums_ref, squares_ref, mix_ref, out_ref):
    total = jnp.sum(squares_ref[...], axis=0)[0:1]
    mix_sq, out_sq = total[:, 0:1], total[:, 1:2]
    mix_scale = jnp.minimum(1.0, 1.0 / jnp.sqrt(mix_sq / float(D * 4 * AW) + 1e-06))
    out_scale = jnp.minimum(1.0, 1.0 / jnp.sqrt(out_sq / float(D * AW) + 1e-06))
    for core in range(2):
        for g in range(8):
            for c in range(2):
                mix_ref[
                    g * PROWS : (g + 1) * PROWS, core * D + c * 512 : core * D + (c + 1) * 512
                ] = sums_ref[(g * 2 + c) * 2 + core, :, 0:512].astype(F32) * mix_scale
        for r in range(4):
            for c in range(4):
                out_ref[
                    r * PROWS : (r + 1) * PROWS, core * AW + c * 128 : core * AW + (c + 1) * 128
                ] = sums_ref[(r * 4 + c) * 2 + core, :, 512:PCOLS].astype(F32) * out_scale


def vmem():
    return pl.BlockSpec(memory_space=pltpu.VMEM)


def call(body, outs, args, specs=None, **kwargs):
    shapes = [jax.ShapeDtypeStruct(s, t) for s, t in outs]
    one = len(shapes) == 1
    return pl.pallas_call(
        body,
        out_shape=shapes[0] if one else shapes,
        in_specs=specs or [vmem()] * len(args),
        out_specs=vmem() if one else [vmem()] * len(shapes),
        **kwargs,
    )(*args)


def exchange(array, axes):
    return lax.all_to_all(array, axes, split_axis=0, concat_axis=0, tiled=True)


def shards(
    item_table, item_row, item_owner, user_lengths, w_mix, w_out, gain_in, gain_attn, cotangent
):
    core = lax.axis_index("core")
    share = jnp.concatenate(
        [
            lax.dynamic_slice(w_mix, (0, core * D), (TOK, D)),
            lax.dynamic_slice(w_out, (core * 32, 0), (32, D)),
        ],
        axis=0,
    )
    weights = lax.all_gather(share, ("core", "z"), axis=0, tiled=True).reshape(2, NZ, 160, D)

    requests, target = call(
        plan_kernel,
        [((OWNERS, 128), jnp.int32), ((TOK, TOK), jnp.int32)],
        (item_owner.reshape(1, TOK), item_row.reshape(1, TOK)),
    )
    asked = exchange(requests, TABLE)
    wanted = asked[:, :SLOTS].reshape(OWNERS * SLOTS)
    found = item_table.at[wanted].get(mode="promise_in_bounds")
    got = exchange(found.reshape(OWNERS, SLOTS, D), TABLE)

    smem = pl.BlockSpec(memory_space=pltpu.SMEM)
    anywhere = pl.BlockSpec(memory_space=pl.ANY)
    piece = (XY, NZ, PROWS, PCOLS)
    layer_out, grad_slots, keep, send = call(
        layer_kernel,
        [((TOK, D), BF16), ((OWNERS * SLOTS, D), BF16), (piece, BF16), (piece, BF16)],
        (
            user_lengths,
            got.reshape(OWNERS * SLOTS, D),
            target,
            weights,
            gain_in.reshape(1, D),
            gain_attn.reshape(1, AW),
            cotangent,
        ),
        specs=[smem, vmem(), vmem(), anywhere, vmem(), vmem(), vmem()],
        scratch_shapes=[
            pltpu.VMEM((2, NZ, TOK, D), BF16),
            pltpu.VMEM((NZ, 2, 32, D), BF16),
            pltpu.VMEM((2, TOK, D), BF16),
            pltpu.SemaphoreType.DMA((4,)),
        ],
        compiler_params=pltpu.CompilerParams(vmem_limit_bytes=40 * MB),
    )

    theirs = lax.ppermute(send, "core", [(0, 1), (1, 0)])
    pair_sum = (keep.astype(F32) + theirs.astype(F32)).astype(BF16)
    plane = exchange(pair_sum, ("x", "y"))
    plane_sum = jnp.sum(plane.astype(F32), axis=0).astype(BF16)
    column = exchange(plane_sum, "z")
    whole = jnp.sum(column.astype(F32), axis=0).astype(BF16)
    sums = exchange(jnp.broadcast_to(whole[None], (OWNERS, PROWS, PCOLS)), TABLE)
    squares = call(square_kernel, [((NZ, 8, 128), F32)], (sums,))
    squares = exchange(squares, "z")
    mix_grad, out_grad = call(
        scale_kernel, [((TOK, 4 * AW), F32), ((64, D), F32)], (sums, squares)
    )

    received = exchange(grad_slots.reshape(OWNERS, SLOTS, D), TABLE)
    packed = call(
        pack_kernel, [((GROWS, D), BF16)], (received.reshape(OWNERS * SLOTS, D), asked)
    )
    gathered = lax.all_gather(packed, "z", axis=0, tiled=True).reshape(NZ, GROWS, D)
    table_grad = call(
        table_kernel,
        [((256, D), F32)],
        (gathered,),
        compiler_params=pltpu.CompilerParams(vmem_limit_bytes=40 * MB),
    )
    return (layer_out, table_grad, mix_grad, out_grad)


def solution(mesh):
    cube = Mesh(mesh.devices.reshape(4, 4, 2, 8), ALL)
    in_specs = (
        P(TABLE, None),
        P(ALL),
        P(ALL, None),
        P(ALL, None),
        P("z", None),
        P("z", None),
        P(),
        P(),
        P(ALL, None),
    )
    out_specs = (
        P(ALL, None),
        P(ALL, None),
        P("z", None),
        P("z", None),
    )
    return jax.shard_map(shards, mesh=cube, in_specs=in_specs, out_specs=out_specs, check_vma=False)
```

```python
import jax
import jax.numpy as jnp
from jax import lax
from jax.experimental import pallas as pl
from jax.experimental.pallas import tpu as pltpu
from jax.sharding import Mesh
from jax.sharding import PartitionSpec as P

H = 4
DH = 128
MAXLEN = 64
TOK = 128
D = 1024
AW = H * DH
OWNERS = 32
CAP = 6
SLOTS = 8
NZ = 8
XY = 16
PROWS = 16
PCOLS = 640
GROWS = OWNERS * CAP + 16
TABLE = ("x", "y", "core")
ALL = ("x", "y", "core", "z")
F32 = jnp.float32
BF16 = jnp.bfloat16
MB = 1024 * 1024


def mm(a, b):
    return lax.dot_general(a, b, (((1,), (0,)), ((), ())), preferred_element_type=F32)


def mm_nt(a, b):
    return lax.dot_general(a, b, (((1,), (1,)), ((), ())), preferred_element_type=F32)


def mm_tn(a, b):
    return lax.dot_general(a, b, (((0,), (0,)), ((), ())), preferred_element_type=F32)


def iota(shape, dim):
    return lax.broadcasted_iota(jnp.int32, shape, dim)


def plan_kernel(owner_ref, row_ref, req_ref, tgt_ref):
    square = (TOK, TOK)
    lane = iota(square, 1)

    def column(values):
        return jnp.broadcast_to(values.astype(F32), square).T

    row = row_ref[...]
    owner = column(owner_ref[...])
    low, high = column(row & 127), column(row >> 7)
    onehot = owner == lane.astype(F32)
    onehot_f = onehot.astype(F32)
    onehot_b = onehot_f.astype(BF16)
    earlier = (lane < iota(square, 0)).astype(F32).astype(BF16)
    before = mm(earlier, onehot_b)
    slot = jnp.sum(before * onehot_f, axis=1, keepdims=True)
    tgt_ref[...] = (owner * SLOTS + slot).astype(jnp.int32)
    here = slot == lane.astype(F32)
    low = jnp.where(here, low, 0.0).astype(BF16)
    high = jnp.where(here, high, 0.0).astype(BF16)
    requests = mm_tn(onehot_b, low) + 128.0 * mm_tn(onehot_b, high)
    req_ref[...] = requests[:OWNERS].astype(jnp.int32)


def layer_kernel(
    lens_ref, got_ref, tgt_ref, weights_ref, gin_ref, gat_ref, ct_ref,
    out_ref, slots_ref, keep_ref, send_ref,
    wm, wo, dmx, sems,
):
    core = lax.axis_index("core")
    copies = []
    for half in range(2):
        copies.append(
            pltpu.make_async_copy(
                weights_ref.at[half, :, pl.ds(0, TOK), :], wm.at[half], sems.at[half]
            )
        )
    for half in range(2):
        copies.append(
            pltpu.make_async_copy(
                weights_ref.at[half, :, pl.ds(TOK, 32), :], wo.at[:, half], sems.at[2 + half]
            )
        )
    for copy in copies:
        copy.start()

    pick = (tgt_ref[:, :1] == iota((TOK, OWNERS * SLOTS), 1)).astype(F32).astype(BF16)
    emb = mm(pick, got_ref[...])
    gin = gin_ref[...]
    gat = gat_ref[...]
    centered = emb - jnp.mean(emb, axis=1, keepdims=True)
    rstd = lax.rsqrt(jnp.mean(centered * centered, axis=1, keepdims=True) + 1e-05)
    xhat = centered * rstd
    normed = (xhat * gin).astype(BF16)

    position, other = iota((TOK, TOK), 0), iota((TOK, TOK), 1)
    seg_row = jnp.zeros((TOK, TOK), jnp.int32)
    seg_col = jnp.zeros((TOK, TOK), jnp.int32)
    end = 0
    for user in range(lens_ref.shape[1]):
        end = end + lens_ref[0, user]
        seg_row = seg_row + (position >= end).astype(jnp.int32)
        seg_col = seg_col + (other >= end).astype(jnp.int32)
    allowed = (seg_row == seg_col) & (other <= position)

    copies[0].wait()
    wm0 = wm[0].reshape(D, D)
    mix0 = mm(normed, wm0)
    copies[1].wait()
    wm1 = wm[1].reshape(D, D)
    mix1 = mm(normed, wm1)

    sig0, sig1 = jax.nn.sigmoid(mix0), jax.nn.sigmoid(mix1)
    act0, act1 = (mix0 * sig0).astype(BF16), (mix1 * sig1).astype(BF16)
    slope0 = sig0 * (1.0 + mix0 * (1.0 - sig0))
    slope1 = sig1 * (1.0 + mix1 * (1.0 - sig1))
    gate_u = act0[:, :AW].astype(F32)

    heads = []
    attended = []
    for h in range(H):
        val = act0[:, AW + h * DH : AW + (h + 1) * DH]
        qry = act1[:, h * DH : (h + 1) * DH]
        key = act1[:, AW + h * DH : AW + (h + 1) * DH]
        score = mm_nt(qry, key) * DH ** (-0.5)
        sig = jax.nn.sigmoid(score)
        wgt = (jnp.where(allowed, score * sig, 0.0) / MAXLEN).astype(BF16)
        attended.append(mm(wgt, val).astype(BF16))
        slope = jnp.where(allowed, sig * (1.0 + score * (1.0 - sig)), 0.0) * (
            DH ** (-0.5) / MAXLEN
        )
        heads.append((val, qry, key, wgt, slope))
    att = jnp.concatenate(attended, axis=1).astype(F32)
    acent = att - jnp.mean(att, axis=1, keepdims=True)
    arstd = lax.rsqrt(jnp.mean(acent * acent, axis=1, keepdims=True) + 1e-05)
    ahat = acent * arstd
    scaled = ahat * gat
    gated = (scaled * gate_u).astype(BF16)

    copies[2].wait()
    copies[3].wait()
    w_out = wo[...].reshape(AW, D)
    ct = ct_ref[...]
    out_ref[...] = (emb + mm(gated, w_out)).astype(BF16)

    d_gated = mm_nt(ct, w_out).astype(BF16).astype(F32)
    d_gate = (d_gated * scaled).astype(BF16).astype(F32)
    d_ahat = d_gated * gate_u * gat
    d_att = arstd * (
        d_ahat
        - jnp.mean(d_ahat, axis=1, keepdims=True)
        - ahat * jnp.mean(d_ahat * ahat, axis=1, keepdims=True)
    )
    d_att = d_att.astype(BF16)
    d_val, d_qry, d_key = [], [], []
    for h in range(H):
        val, qry, key, wgt, slope = heads[h]
        d_head = d_att[:, h * DH : (h + 1) * DH]
        d_wgt = mm_nt(d_head, val).astype(BF16).astype(F32)
        d_val.append(mm_tn(wgt, d_head).astype(BF16))
        d_score = (d_wgt * slope).astype(BF16)
        d_qry.append(mm(d_score, key).astype(BF16))
        d_key.append(mm_tn(d_score, qry).astype(BF16))
    d_act0 = jnp.concatenate([d_gate] + [v.astype(F32) for v in d_val], axis=1)
    d_act1 = jnp.concatenate([v.astype(F32) for v in d_qry + d_key], axis=1)
    d_mix0 = (d_act0 * slope0).astype(BF16)
    d_mix1 = (d_act1 * slope1).astype(BF16)
    dmx[0] = d_mix0
    dmx[1] = d_mix1
    d_normed = (mm_nt(d_mix0, wm0) + mm_nt(d_mix1, wm1)).astype(BF16).astype(F32)
    d_xhat = d_normed * gin
    d_emb = (
        rstd
        * (
            d_xhat
            - jnp.mean(d_xhat, axis=1, keepdims=True)
            - xhat * jnp.mean(d_xhat * xhat, axis=1, keepdims=True)
        )
        + ct.astype(F32)
    ).astype(BF16)
    slots_ref[...] = mm_tn(pick, d_emb).astype(BF16)

    for side, dst in ((1 - core, send_ref), (core, keep_ref)):
        d_mix = dmx[side]
        ct_half = ct_ref[:, pl.ds(pl.multiple_of(side * AW, AW), AW)]
        for z in range(NZ):
            grad = mm_tn(normed[:, z * TOK : (z + 1) * TOK], d_mix).astype(BF16)
            for g in range(8):
                for c in range(2):
                    dst[g * 2 + c, z, :, 0:512] = grad[
                        g * PROWS : (g + 1) * PROWS, c * 512 : (c + 1) * 512
                    ]
        for pair in range(NZ // 2):
            grad = mm_tn(gated[:, pair * TOK : (pair + 1) * TOK], ct_half).astype(BF16)
            for sub in range(2):
                for r in range(4):
                    for c in range(4):
                        dst[r * 4 + c, pair * 2 + sub, :, 512:PCOLS] = grad[
                            sub * 64 + r * PROWS : sub * 64 + (r + 1) * PROWS,
                            c * 128 : (c + 1) * 128,
                        ]


def pack_kernel(rows_ref, asked_ref, after_ref, out_ref):
    used = OWNERS * CAP
    r, k = iota((used, OWNERS * SLOTS), 0), iota((used, OWNERS * SLOTS), 1)
    take = (r // CAP == k // SLOTS) & (r % CAP == k % SLOTS)
    out_ref[:used] = mm(take.astype(F32).astype(BF16), rows_ref[...]).astype(BF16)
    asked = asked_ref[...]
    owner = (iota((256, OWNERS), 0) // CAP == iota((256, OWNERS), 1)).astype(F32).astype(BF16)
    slot = iota((256, 128), 0) % CAP == iota((256, 128), 1)
    parts = []
    for part in (asked & 127, asked >> 7):
        spread = mm(owner, part.astype(F32).astype(BF16))
        column = jnp.sum(jnp.where(slot, spread, 0.0), axis=1, keepdims=True)
        parts.append(jnp.broadcast_to(column, (256, 128)).T[:PROWS])
    which = iota((PROWS, 256), 0)
    numbers = jnp.where(which == 0, parts[0], jnp.where(which == 1, parts[1], 0.0))
    out_ref[used:] = jnp.concatenate(
        [numbers.astype(BF16), jnp.zeros((PROWS, D - 256), BF16)], axis=1
    )


def table_kernel(rows_ref, out_ref):
    used = OWNERS * CAP
    first = lax.axis_index("z") * 256
    total = jnp.zeros((256, D), F32)
    for z in range(NZ):
        low = rows_ref[z, used : used + PROWS, :256].astype(F32)
        number = (low[0:1] + 128.0 * low[1:2]).astype(jnp.int32)[:, :used] - first
        here = (iota((256, used), 0) == number).astype(F32).astype(BF16)
        total = total + mm(here, rows_ref[z, :used])
    out_ref[...] = total


def square_kernel(sums_ref, out_ref):
    sums = sums_ref[...].astype(F32)
    sq = sums * sums
    mix = jnp.sum(sq[:, :, :512])
    out = jnp.sum(sq[:, :, 512:])
    lane = iota((NZ, 8, 128), 2)
    out_ref[...] = jnp.where(lane == 0, mix, jnp.where(lane == 1, out, 0.0))


def scale_kernel(sums_ref, squares_ref, after_ref, mix_ref, out_ref):
    total = jnp.sum(squares_ref[...], axis=0)[0:1]
    mix_sq, out_sq = total[:, 0:1], total[:, 1:2]
    mix_scale = jnp.minimum(1.0, 1.0 / jnp.sqrt(mix_sq / float(D * 4 * AW) + 1e-06))
    out_scale = jnp.minimum(1.0, 1.0 / jnp.sqrt(out_sq / float(D * AW) + 1e-06))
    for core in range(2):
        for g in range(8):
            for c in range(2):
                mix_ref[
                    g * PROWS : (g + 1) * PROWS, core * D + c * 512 : core * D + (c + 1) * 512
                ] = sums_ref[(g * 2 + c) * 2 + core, :, 0:512].astype(F32) * mix_scale
        for r in range(4):
            for c in range(4):
                out_ref[
                    r * PROWS : (r + 1) * PROWS, core * AW + c * 128 : core * AW + (c + 1) * 128
                ] = sums_ref[(r * 4 + c) * 2 + core, :, 512:PCOLS].astype(F32) * out_scale


def vmem():
    return pl.BlockSpec(memory_space=pltpu.VMEM)


def call(body, outs, args, specs=None, **kwargs):
    shapes = [jax.ShapeDtypeStruct(s, t) for s, t in outs]
    one = len(shapes) == 1
    return pl.pallas_call(
        body,
        out_shape=shapes[0] if one else shapes,
        in_specs=specs or [vmem()] * len(args),
        out_specs=vmem() if one else [vmem()] * len(shapes),
        **kwargs,
    )(*args)


def cost(us):
    return pl.CostEstimate(flops=0, bytes_accessed=int(us * 3.0e6), transcendentals=0)


def exchange(array, axes):
    return lax.all_to_all(array, axes, split_axis=0, concat_axis=0, tiled=True)


def shards(
    item_table, item_row, item_owner, user_lengths, w_mix, w_out, gain_in, gain_attn, cotangent
):
    core = lax.axis_index("core")
    share = jnp.concatenate(
        [
            lax.dynamic_slice(w_mix, (0, core * D), (TOK, D)),
            lax.dynamic_slice(w_out, (core * 32, 0), (32, D)),
        ],
        axis=0,
    )
    weights = lax.all_gather(share, ("core", "z"), axis=0, tiled=True).reshape(2, NZ, 160, D)

    requests, target = call(
        plan_kernel,
        [((OWNERS, 128), jnp.int32), ((TOK, TOK), jnp.int32)],
        (item_owner.reshape(1, TOK), item_row.reshape(1, TOK)),
    )
    asked = exchange(requests, TABLE)
    wanted = asked[:, :SLOTS].reshape(OWNERS * SLOTS)
    found = item_table.at[wanted].get(mode="promise_in_bounds")
    got = exchange(found.reshape(OWNERS, SLOTS, D), TABLE)

    smem = pl.BlockSpec(memory_space=pltpu.SMEM)
    anywhere = pl.BlockSpec(memory_space=pl.ANY)
    piece = (XY, NZ, PROWS, PCOLS)
    layer_out, grad_slots, keep, send = call(
        layer_kernel,
        [((TOK, D), BF16), ((OWNERS * SLOTS, D), BF16), (piece, BF16), (piece, BF16)],
        (
            user_lengths,
            got.reshape(OWNERS * SLOTS, D),
            target,
            weights,
            gain_in.reshape(1, D),
            gain_attn.reshape(1, AW),
            cotangent,
        ),
        specs=[smem, vmem(), vmem(), anywhere, vmem(), vmem(), vmem()],
        scratch_shapes=[
            pltpu.VMEM((2, NZ, TOK, D), BF16),
            pltpu.VMEM((NZ, 2, 32, D), BF16),
            pltpu.VMEM((2, TOK, D), BF16),
            pltpu.SemaphoreType.DMA((4,)),
        ],
        cost_estimate=cost(9),
        compiler_params=pltpu.CompilerParams(vmem_limit_bytes=60 * MB),
    )

    theirs = lax.ppermute(send, "core", [(0, 1), (1, 0)])
    pair_sum = (keep.astype(F32) + theirs.astype(F32)).astype(BF16)
    added = pair_sum[0, 0, :, :128]
    plane = exchange(pair_sum, ("x", "y"))
    plane_sum = jnp.sum(plane.astype(F32), axis=0).astype(BF16)
    column = exchange(plane_sum, "z")
    whole = jnp.sum(column.astype(F32), axis=0).astype(BF16)
    sums = exchange(jnp.broadcast_to(whole[None], (OWNERS, PROWS, PCOLS)), TABLE)
    received = exchange(grad_slots.reshape(OWNERS, SLOTS, D), TABLE)
    packed = call(
        pack_kernel,
        [((GROWS, D), BF16)],
        (received.reshape(OWNERS * SLOTS, D), asked, added),
        specs=[vmem(), vmem(), anywhere],
        cost_estimate=cost(2),
        compiler_params=pltpu.CompilerParams(vmem_limit_bytes=16 * MB),
    )
    gathered = lax.all_gather(packed, "z", axis=0, tiled=True).reshape(NZ, GROWS, D)
    table_grad = call(
        table_kernel,
        [((256, D), F32)],
        (gathered,),
        cost_estimate=cost(2),
        compiler_params=pltpu.CompilerParams(vmem_limit_bytes=60 * MB),
    )
    squares = call(square_kernel, [((NZ, 8, 128), F32)], (sums,))
    squares = exchange(squares, "z")
    mix_grad, out_grad = call(
        scale_kernel,
        [((TOK, 4 * AW), F32), ((64, D), F32)],
        (sums, squares, table_grad),
        specs=[vmem(), vmem(), anywhere],
        cost_estimate=cost(2),
    )

    return (layer_out, table_grad, mix_grad, out_grad)


def solution(mesh):
    cube = Mesh(mesh.devices.reshape(4, 4, 2, 8), ALL)
    in_specs = (
        P(TABLE, None),
        P(ALL),
        P(ALL, None),
        P(ALL, None),
        P("z", None),
        P("z", None),
        P(),
        P(),
        P(ALL, None),
    )
    out_specs = (
        P(ALL, None),
        P(ALL, None),
        P("z", None),
        P("z", None),
    )
    return jax.shard_map(shards, mesh=cube, in_specs=in_specs, out_specs=out_specs, check_vma=False)
```

```python
import jax
import jax.numpy as jnp
from jax import lax
from jax.experimental import pallas as pl
from jax.experimental.pallas import tpu as pltpu
from jax.sharding import Mesh
from jax.sharding import PartitionSpec as P

H = 4
DH = 128
MAXLEN = 64
TOK = 128
D = 1024
AW = H * DH
OWNERS = 32
CAP = 6
SLOTS = 8
NZ = 8
XY = 16
PROWS = 16
PCOLS = 640
PEER = 96
FACT = 4224
GROWS = OWNERS * CAP + 16
TABLE = ("x", "y", "core")
ALL = ("x", "y", "core", "z")
F32 = jnp.float32
BF16 = jnp.bfloat16
MB = 1024 * 1024


def mm(a, b):
    return lax.dot_general(a, b, (((1,), (0,)), ((), ())), preferred_element_type=F32)


def mm_nt(a, b):
    return lax.dot_general(a, b, (((1,), (1,)), ((), ())), preferred_element_type=F32)


def mm_tn(a, b):
    return lax.dot_general(a, b, (((0,), (0,)), ((), ())), preferred_element_type=F32)


def iota(shape, dim):
    return lax.broadcasted_iota(jnp.int32, shape, dim)


def plan_kernel(owner_ref, row_ref, req_ref, tgt_ref, num_ref):
    square = (TOK, TOK)
    lane = iota(square, 1)

    def column(values):
        return jnp.broadcast_to(values.astype(F32), square).T

    row = row_ref[...]
    owner = column(owner_ref[...])
    low, high = column(row & 127), column(row >> 7)
    onehot = owner == lane.astype(F32)
    onehot_f = onehot.astype(F32)
    onehot_b = onehot_f.astype(BF16)
    earlier = (lane < iota(square, 0)).astype(F32).astype(BF16)
    before = mm(earlier, onehot_b)
    slot = jnp.sum(before * onehot_f, axis=1, keepdims=True)
    tgt_ref[...] = (owner * SLOTS + slot).astype(jnp.int32)
    num_ref[...] = jnp.where(lane == 0, low, jnp.where(lane == 1, high, 0.0)).astype(BF16)
    here = slot == lane.astype(F32)
    low = jnp.where(here, low, 0.0).astype(BF16)
    high = jnp.where(here, high, 0.0).astype(BF16)
    requests = mm_tn(onehot_b, low) + 128.0 * mm_tn(onehot_b, high)
    req_ref[...] = requests[:OWNERS].astype(jnp.int32)


def layer_kernel(
    lens_ref, got_ref, tgt_ref, num_ref, weights_ref, gin_ref, gat_ref, ct_ref,
    out_ref, keep_ref, send_ref,
    wm, wo, dmx, sems,
):
    core = lax.axis_index("core")
    copies = []
    for half in range(2):
        copies.append(
            pltpu.make_async_copy(
                weights_ref.at[half, :, pl.ds(0, TOK), :], wm.at[half], sems.at[half]
            )
        )
    for half in range(2):
        copies.append(
            pltpu.make_async_copy(
                weights_ref.at[half, :, pl.ds(TOK, 32), :], wo.at[:, half], sems.at[2 + half]
            )
        )
    for copy in copies:
        copy.start()

    pick = (tgt_ref[:, :1] == iota((TOK, OWNERS * SLOTS), 1)).astype(F32).astype(BF16)
    emb = mm(pick, got_ref[...])
    gin = gin_ref[...]
    gat = gat_ref[...]
    centered = emb - jnp.mean(emb, axis=1, keepdims=True)
    rstd = lax.rsqrt(jnp.mean(centered * centered, axis=1, keepdims=True) + 1e-05)
    xhat = centered * rstd
    normed = (xhat * gin).astype(BF16)

    position, other = iota((TOK, TOK), 0), iota((TOK, TOK), 1)
    seg_row = jnp.zeros((TOK, TOK), jnp.int32)
    seg_col = jnp.zeros((TOK, TOK), jnp.int32)
    end = 0
    for user in range(lens_ref.shape[1]):
        end = end + lens_ref[0, user]
        seg_row = seg_row + (position >= end).astype(jnp.int32)
        seg_col = seg_col + (other >= end).astype(jnp.int32)
    allowed = (seg_row == seg_col) & (other <= position)

    copies[0].wait()
    wm0 = wm[0].reshape(D, D)
    mix0 = mm(normed, wm0)
    copies[1].wait()
    wm1 = wm[1].reshape(D, D)
    mix1 = mm(normed, wm1)

    sig0, sig1 = jax.nn.sigmoid(mix0), jax.nn.sigmoid(mix1)
    act0, act1 = (mix0 * sig0).astype(BF16), (mix1 * sig1).astype(BF16)
    slope0 = sig0 * (1.0 + mix0 * (1.0 - sig0))
    slope1 = sig1 * (1.0 + mix1 * (1.0 - sig1))
    gate_u = act0[:, :AW].astype(F32)

    heads = []
    attended = []
    for h in range(H):
        val = act0[:, AW + h * DH : AW + (h + 1) * DH]
        qry = act1[:, h * DH : (h + 1) * DH]
        key = act1[:, AW + h * DH : AW + (h + 1) * DH]
        score = mm_nt(qry, key) * DH ** (-0.5)
        sig = jax.nn.sigmoid(score)
        wgt = (jnp.where(allowed, score * sig, 0.0) / MAXLEN).astype(BF16)
        attended.append(mm(wgt, val).astype(BF16))
        slope = jnp.where(allowed, sig * (1.0 + score * (1.0 - sig)), 0.0) * (
            DH ** (-0.5) / MAXLEN
        )
        heads.append((val, qry, key, wgt, slope))
    att = jnp.concatenate(attended, axis=1).astype(F32)
    acent = att - jnp.mean(att, axis=1, keepdims=True)
    arstd = lax.rsqrt(jnp.mean(acent * acent, axis=1, keepdims=True) + 1e-05)
    ahat = acent * arstd
    scaled = ahat * gat
    gated = (scaled * gate_u).astype(BF16)

    copies[2].wait()
    copies[3].wait()
    w_out = wo[...].reshape(AW, D)
    ct = ct_ref[...]
    out_ref[...] = (emb + mm(gated, w_out)).astype(BF16)

    d_gated = mm_nt(ct, w_out).astype(BF16).astype(F32)
    d_gate = (d_gated * scaled).astype(BF16).astype(F32)
    d_ahat = d_gated * gate_u * gat
    d_att = arstd * (
        d_ahat
        - jnp.mean(d_ahat, axis=1, keepdims=True)
        - ahat * jnp.mean(d_ahat * ahat, axis=1, keepdims=True)
    )
    d_att = d_att.astype(BF16)
    d_val, d_qry, d_key = [], [], []
    for h in range(H):
        val, qry, key, wgt, slope = heads[h]
        d_head = d_att[:, h * DH : (h + 1) * DH]
        d_wgt = mm_nt(d_head, val).astype(BF16).astype(F32)
        d_val.append(mm_tn(wgt, d_head).astype(BF16))
        d_score = (d_wgt * slope).astype(BF16)
        d_qry.append(mm(d_score, key).astype(BF16))
        d_key.append(mm_tn(d_score, qry).astype(BF16))
    d_act0 = jnp.concatenate([d_gate] + [v.astype(F32) for v in d_val], axis=1)
    d_act1 = jnp.concatenate([v.astype(F32) for v in d_qry + d_key], axis=1)
    d_mix0 = (d_act0 * slope0).astype(BF16)
    d_mix1 = (d_act1 * slope1).astype(BF16)
    dmx[0] = d_mix0
    dmx[1] = d_mix1
    d_normed = (mm_nt(d_mix0, wm0) + mm_nt(d_mix1, wm1)).astype(BF16).astype(F32)
    d_xhat = d_normed * gin
    d_emb = (
        rstd
        * (
            d_xhat
            - jnp.mean(d_xhat, axis=1, keepdims=True)
            - xhat * jnp.mean(d_xhat * xhat, axis=1, keepdims=True)
        )
        + ct.astype(F32)
    ).astype(BF16)
    lane = iota((TOK, TOK), 1)
    rows = jnp.concatenate([d_emb, num_ref[...]], axis=1)
    for side, dst in ((1 - core, send_ref), (core, keep_ref)):
        dst[:, 0:1024] = normed
        dst[:, 1024:2048] = dmx[side]
        dst[:, 2048:2560] = gated
        dst[:, 2560:3072] = ct_ref[:, pl.ds(pl.multiple_of(side * AW, AW), AW)]
        slot = ((lane >> 3) * 2 + side) * SLOTS + (lane & 7)
        chosen = (tgt_ref[...] == slot).astype(F32).astype(BF16)
        dst[:, 3072:FACT] = mm_tn(chosen, rows).astype(BF16)


def grads_kernel(keep_ref, theirs_ref, out_ref, buf, sems):
    def both(first, last):
        return jnp.concatenate([keep_ref[:, first:last], theirs_ref[:, first:last]], axis=0)

    copies = []

    def send(first, count):
        block = pl.ds(first, count)
        copies.append(
            pltpu.make_async_copy(buf.at[:, block, :], out_ref.at[:, block, :], sems.at[len(copies)])
        )
        copies[-1].start()

    d_mix = both(1024, 2048)
    for pair in range(NZ // 2):
        one, two = (
            mm_tn(both(z * TOK, (z + 1) * TOK), d_mix) for z in (2 * pair, 2 * pair + 1)
        )
        for p in range(XY):
            buf[p, 16 * pair : 16 * pair + 16, :] = jnp.concatenate(
                [one[8 * p : 8 * p + 8], two[8 * p : 8 * p + 8]], axis=0
            ).astype(BF16)
        send(16 * pair, 16)

    grad = mm_tn(both(2048, 2560), both(2560, 3072))
    for p in range(XY):
        r, c = (p // 2) * 8, (p % 2) * 256
        halves = [
            jnp.concatenate(
                [grad[z * 64 + r : z * 64 + r + 8, c : c + 256] for z in range(first, first + 4)],
                axis=1,
            )
            for first in (0, 4)
        ]
        buf[p, 64:80, :] = jnp.concatenate(halves, axis=0).astype(BF16)
    send(64, 16)

    r, k = iota((256, 256), 0), iota((256, 256), 1)
    j = r & 15
    source = jnp.where(j < CAP, 0, 128) + (r >> 4) * SLOTS + jnp.where(j < CAP, j, j - CAP)
    take = ((k == source) & (j < 2 * CAP)).astype(F32).astype(BF16)
    rows = mm(take, both(3072, 4096))
    names = mm(take, both(4096, FACT)).T
    place = iota((256, 256), 0) & 15
    names = jnp.where(
        place == 2 * CAP, names[0:1], jnp.where(place == 2 * CAP + 1, names[1:2], 0.0)
    )
    rows = jnp.concatenate([rows[:, :256] + names, rows[:, 256:]], axis=1).astype(BF16)
    for p in range(XY):
        buf[p, 80:PEER, :] = rows[16 * p : 16 * p + 16]
    send(80, 16)
    for copy in copies:
        copy.wait()


def plane_kernel(block_ref, out_ref):
    step = pl.program_id(0)
    total = jnp.sum(block_ref[...].astype(F32), axis=0)

    @pl.when(step < 4)
    def _():
        for sub in range(2):
            part = total[8 * sub : 8 * sub + 8]
            out_ref[step * 2 + sub, :, 0:512] = jnp.concatenate(
                [part[:, :512], part[:, 512:]], axis=0
            ).astype(BF16)

    @pl.when(step == 4)
    def _():
        for z in range(NZ):
            part = total[(z // 4) * 8 : (z // 4) * 8 + 8, (z % 4) * 256 : (z % 4) * 256 + 256]
            out_ref[z, :, 512:PCOLS] = jnp.concatenate(
                [part[:, :128], part[:, 128:]], axis=0
            ).astype(BF16)


def pack_kernel(rows_ref, out_ref):
    used = OWNERS * CAP
    me = lax.axis_index("x") * 4 + lax.axis_index("y")
    rows = rows_ref[...].reshape(256, D)
    r, k = iota((used, 256), 0), iota((used, 256), 1)
    src, j = r // (2 * CAP), r % (2 * CAP)
    out_ref[:used] = mm((k == src * 16 + j).astype(F32).astype(BF16), rows).astype(BF16)
    r, k = iota((256, 256), 0), iota((256, 256), 1)
    src, j = r // (2 * CAP), r % (2 * CAP)
    mine = k == me * 16 + j
    parts = []
    for place in (2 * CAP, 2 * CAP + 1):
        take = (k == src * 16 + place).astype(F32).astype(BF16)
        column = jnp.sum(jnp.where(mine, mm(take, rows[:, :256]), 0.0), axis=1, keepdims=True)
        parts.append(jnp.broadcast_to(column, (256, 128)).T[:PROWS])
    which = iota((PROWS, 256), 0)
    numbers = jnp.where(which == 0, parts[0], jnp.where(which == 1, parts[1], 0.0))
    out_ref[used:] = jnp.concatenate(
        [numbers.astype(BF16), jnp.zeros((PROWS, D - 256), BF16)], axis=1
    )


def table_kernel(rows_ref, out_ref):
    used = OWNERS * CAP
    first = lax.axis_index("z") * 256
    names = rows_ref[0, used : used + PROWS, :256].astype(F32)
    number = (names[0:1] + 128.0 * names[1:2]).astype(jnp.int32)[:, :used] - first
    here = (iota((256, used), 0) == number).astype(F32).astype(BF16)
    part = mm(here, rows_ref[0, :used])

    @pl.when(pl.program_id(0) == 0)
    def _():
        out_ref[...] = part

    @pl.when(pl.program_id(0) > 0)
    def _():
        out_ref[...] += part


def square_kernel(sums_ref, out_ref):
    total = jnp.zeros((PROWS, PCOLS), F32)
    for i in range(OWNERS):
        part = sums_ref[i].astype(F32)
        total = total + part * part
    mix = jnp.sum(total[:, :512])
    out = jnp.sum(total[:, 512:])
    lane = iota((NZ, 8, 128), 2)
    out_ref[...] = jnp.where(lane == 0, mix, jnp.where(lane == 1, out, 0.0))


def scale_kernel(sums_ref, squares_ref, mix_ref, out_ref):
    total = jnp.sum(squares_ref[...], axis=0)[0:1]
    mix_sq, out_sq = total[:, 0:1], total[:, 1:2]
    mix_scale = jnp.minimum(1.0, 1.0 / jnp.sqrt(mix_sq / float(D * 4 * AW) + 1e-06))
    out_scale = jnp.minimum(1.0, 1.0 / jnp.sqrt(out_sq / float(D * AW) + 1e-06))
    for p in range(XY):
        for core in range(2):
            sums = sums_ref[p * 2 + core].astype(F32)
            mix, out = sums[:, :512] * mix_scale, sums[:, 512:] * out_scale
            r, c = p * 8, core * D
            mix_ref[r : r + 8, c : c + 512] = mix[:8]
            mix_ref[r : r + 8, c + 512 : c + 1024] = mix[8:]
            r, c = (p // 2) * 8, core * AW + (p % 2) * 256
            out_ref[r : r + 8, c : c + 128] = out[:8]
            out_ref[r : r + 8, c + 128 : c + 256] = out[8:]


def vmem():
    return pl.BlockSpec(memory_space=pltpu.VMEM)


def call(body, outs, args, specs=None, **kwargs):
    shapes = [jax.ShapeDtypeStruct(s, t) for s, t in outs]
    one = len(shapes) == 1
    return pl.pallas_call(
        body,
        out_shape=shapes[0] if one else shapes,
        in_specs=specs or [vmem()] * len(args),
        out_specs=vmem() if one else [vmem()] * len(shapes),
        **kwargs,
    )(*args)


def cost(us):
    return pl.CostEstimate(flops=0, bytes_accessed=int(us * 3.0e6), transcendentals=0)


def exchange(array, axes):
    return lax.all_to_all(array, axes, split_axis=0, concat_axis=0, tiled=True)


def shards(
    item_table, item_row, item_owner, user_lengths, w_mix, w_out, gain_in, gain_attn, cotangent
):
    core = lax.axis_index("core")
    share = jnp.concatenate(
        [
            lax.dynamic_slice(w_mix, (0, core * D), (TOK, D)),
            lax.dynamic_slice(w_out, (core * 32, 0), (32, D)),
        ],
        axis=0,
    )
    weights = lax.all_gather(share, ("core", "z"), axis=0, tiled=True).reshape(2, NZ, 160, D)

    requests, target, numbers = call(
        plan_kernel,
        [((OWNERS, 128), jnp.int32), ((TOK, TOK), jnp.int32), ((TOK, TOK), BF16)],
        (item_owner.reshape(1, TOK), item_row.reshape(1, TOK)),
    )
    asked = exchange(requests, TABLE)
    wanted = asked[:, :SLOTS].reshape(OWNERS * SLOTS)
    found = item_table.at[wanted].get(mode="promise_in_bounds")
    got = exchange(found.reshape(OWNERS, SLOTS, D), TABLE)

    smem = pl.BlockSpec(memory_space=pltpu.SMEM)
    anywhere = pl.BlockSpec(memory_space=pl.ANY)
    layer_out, keep, send = call(
        layer_kernel,
        [((TOK, D), BF16), ((TOK, FACT), BF16), ((TOK, FACT), BF16)],
        (
            user_lengths,
            got.reshape(OWNERS * SLOTS, D),
            target,
            numbers,
            weights,
            gain_in.reshape(1, D),
            gain_attn.reshape(1, AW),
            cotangent,
        ),
        specs=[smem, vmem(), vmem(), vmem(), anywhere, vmem(), vmem(), vmem()],
        scratch_shapes=[
            pltpu.VMEM((2, NZ, TOK, D), BF16),
            pltpu.VMEM((NZ, 2, 32, D), BF16),
            pltpu.VMEM((2, TOK, D), BF16),
            pltpu.SemaphoreType.DMA((4,)),
        ],
        cost_estimate=cost(9),
        compiler_params=pltpu.CompilerParams(vmem_limit_bytes=60 * MB),
    )

    theirs = lax.ppermute(send, "core", [(0, 1), (1, 0)])
    grads = pl.pallas_call(
        grads_kernel,
        out_shape=jax.ShapeDtypeStruct((XY, PEER, D), BF16),
        in_specs=[vmem(), vmem()],
        out_specs=anywhere,
        scratch_shapes=[
            pltpu.VMEM((XY, PEER, D), BF16),
            pltpu.SemaphoreType.DMA((6,)),
        ],
        cost_estimate=cost(3),
        compiler_params=pltpu.CompilerParams(vmem_limit_bytes=30 * MB),
    )(keep, theirs)
    plane = exchange(grads, ("x", "y"))

    packed = pl.pallas_call(
        pack_kernel,
        grid=(1,),
        out_shape=jax.ShapeDtypeStruct((GROWS, D), BF16),
        in_specs=[pl.BlockSpec((XY, 16, D), lambda i: (0, 5, 0))],
        out_specs=pl.BlockSpec((GROWS, D), lambda i: (0, 0)),
        cost_estimate=cost(2),
        compiler_params=pltpu.CompilerParams(vmem_limit_bytes=60 * MB),
    )(plane)
    gathered = lax.all_gather(packed, "z", axis=0, tiled=True).reshape(NZ, GROWS, D)
    table_grad = pl.pallas_call(
        table_kernel,
        grid=(NZ,),
        out_shape=jax.ShapeDtypeStruct((256, D), F32),
        in_specs=[pl.BlockSpec((1, GROWS, D), lambda i: (i, 0, 0))],
        out_specs=pl.BlockSpec((256, D), lambda i: (0, 0)),
        cost_estimate=cost(3),
        compiler_params=pltpu.CompilerParams(vmem_limit_bytes=60 * MB),
    )(gathered)

    plane_sum = pl.pallas_call(
        plane_kernel,
        grid=(5,),
        out_shape=jax.ShapeDtypeStruct((NZ, PROWS, PCOLS), BF16),
        in_specs=[pl.BlockSpec((XY, 16, D), lambda i: (0, i, 0))],
        out_specs=pl.BlockSpec((NZ, PROWS, PCOLS), lambda i: (0, 0, 0)),
        cost_estimate=cost(2),
        compiler_params=pltpu.CompilerParams(vmem_limit_bytes=60 * MB),
    )(plane)
    column = exchange(plane_sum, "z")
    whole = jnp.sum(column.astype(F32), axis=0).astype(BF16)
    sums = exchange(jnp.broadcast_to(whole[None], (OWNERS, PROWS, PCOLS)), TABLE)
    squares = call(
        square_kernel,
        [((NZ, 8, 128), F32)],
        (sums,),
        cost_estimate=cost(1),
        compiler_params=pltpu.CompilerParams(vmem_limit_bytes=16 * MB),
    )
    squares = exchange(squares, "z")
    mix_grad, out_grad = call(
        scale_kernel,
        [((TOK, 4 * AW), F32), ((64, D), F32)],
        (sums, squares),
        cost_estimate=cost(2),
        compiler_params=pltpu.CompilerParams(vmem_limit_bytes=16 * MB),
    )
    return (layer_out, table_grad, mix_grad, out_grad)


def solution(mesh):
    cube = Mesh(mesh.devices.reshape(4, 4, 2, 8), ALL)
    in_specs = (
        P(TABLE, None),
        P(ALL),
        P(ALL, None),
        P(ALL, None),
        P("z", None),
        P("z", None),
        P(),
        P(),
        P(ALL, None),
    )
    out_specs = (
        P(ALL, None),
        P(ALL, None),
        P("z", None),
        P("z", None),
    )
    return jax.shard_map(shards, mesh=cube, in_specs=in_specs, out_specs=out_specs, check_vma=False)
```

```python
import jax
import jax.numpy as jnp
from jax import lax
from jax.experimental import pallas as pl
from jax.experimental.pallas import tpu as pltpu
from jax.sharding import Mesh
from jax.sharding import PartitionSpec as P

H = 4
DH = 128
MAXLEN = 64
TOK = 128
D = 1024
AW = H * DH
OWNERS = 32
CAP = 6
SLOTS = 8
NZ = 8
XY = 16
PROWS = 16
PCOLS = 640
FACT = 3072
GROWS = OWNERS * CAP + 16
TABLE = ("x", "y", "core")
ALL = ("x", "y", "core", "z")
F32 = jnp.float32
BF16 = jnp.bfloat16
MB = 1024 * 1024


def mm(a, b):
    return lax.dot_general(a, b, (((1,), (0,)), ((), ())), preferred_element_type=F32)


def mm_nt(a, b):
    return lax.dot_general(a, b, (((1,), (1,)), ((), ())), preferred_element_type=F32)


def mm_tn(a, b):
    return lax.dot_general(a, b, (((0,), (0,)), ((), ())), preferred_element_type=F32)


def iota(shape, dim):
    return lax.broadcasted_iota(jnp.int32, shape, dim)


def plan_kernel(owner_ref, row_ref, req_ref, tgt_ref):
    square = (TOK, TOK)
    lane = iota(square, 1)

    def column(values):
        return jnp.broadcast_to(values.astype(F32), square).T

    row = row_ref[...]
    owner = column(owner_ref[...])
    low, high = column(row & 127), column(row >> 7)
    onehot = owner == lane.astype(F32)
    onehot_f = onehot.astype(F32)
    onehot_b = onehot_f.astype(BF16)
    earlier = (lane < iota(square, 0)).astype(F32).astype(BF16)
    before = mm(earlier, onehot_b)
    slot = jnp.sum(before * onehot_f, axis=1, keepdims=True)
    tgt_ref[...] = (owner * SLOTS + slot).astype(jnp.int32)
    here = slot == lane.astype(F32)
    low = jnp.where(here, low, 0.0).astype(BF16)
    high = jnp.where(here, high, 0.0).astype(BF16)
    requests = mm_tn(onehot_b, low) + 128.0 * mm_tn(onehot_b, high)
    req_ref[...] = requests[:OWNERS].astype(jnp.int32)


def layer_kernel(
    lens_ref, got_ref, tgt_ref, weights_ref, gin_ref, gat_ref, ct_ref,
    out_ref, slots_ref, keep_ref, send_ref,
    wm, wo, dmx, sems,
):
    core = lax.axis_index("core")
    copies = []
    for half in range(2):
        copies.append(
            pltpu.make_async_copy(
                weights_ref.at[half, :, pl.ds(0, TOK), :], wm.at[half], sems.at[half]
            )
        )
    for half in range(2):
        copies.append(
            pltpu.make_async_copy(
                weights_ref.at[half, :, pl.ds(TOK, 32), :], wo.at[:, half], sems.at[2 + half]
            )
        )
    for copy in copies:
        copy.start()

    pick = (tgt_ref[:, :1] == iota((TOK, OWNERS * SLOTS), 1)).astype(F32).astype(BF16)
    emb = mm(pick, got_ref[...])
    gin = gin_ref[...]
    gat = gat_ref[...]
    centered = emb - jnp.mean(emb, axis=1, keepdims=True)
    rstd = lax.rsqrt(jnp.mean(centered * centered, axis=1, keepdims=True) + 1e-05)
    xhat = centered * rstd
    normed = (xhat * gin).astype(BF16)

    position, other = iota((TOK, TOK), 0), iota((TOK, TOK), 1)
    seg_row = jnp.zeros((TOK, TOK), jnp.int32)
    seg_col = jnp.zeros((TOK, TOK), jnp.int32)
    end = 0
    for user in range(lens_ref.shape[1]):
        end = end + lens_ref[0, user]
        seg_row = seg_row + (position >= end).astype(jnp.int32)
        seg_col = seg_col + (other >= end).astype(jnp.int32)
    allowed = (seg_row == seg_col) & (other <= position)

    copies[0].wait()
    wm0 = wm[0].reshape(D, D)
    mix0 = mm(normed, wm0)
    copies[1].wait()
    wm1 = wm[1].reshape(D, D)
    mix1 = mm(normed, wm1)

    sig0, sig1 = jax.nn.sigmoid(mix0), jax.nn.sigmoid(mix1)
    act0, act1 = (mix0 * sig0).astype(BF16), (mix1 * sig1).astype(BF16)
    slope0 = sig0 * (1.0 + mix0 * (1.0 - sig0))
    slope1 = sig1 * (1.0 + mix1 * (1.0 - sig1))
    gate_u = act0[:, :AW].astype(F32)

    heads = []
    attended = []
    for h in range(H):
        val = act0[:, AW + h * DH : AW + (h + 1) * DH]
        qry = act1[:, h * DH : (h + 1) * DH]
        key = act1[:, AW + h * DH : AW + (h + 1) * DH]
        score = mm_nt(qry, key) * DH ** (-0.5)
        sig = jax.nn.sigmoid(score)
        wgt = (jnp.where(allowed, score * sig, 0.0) / MAXLEN).astype(BF16)
        attended.append(mm(wgt, val).astype(BF16))
        slope = jnp.where(allowed, sig * (1.0 + score * (1.0 - sig)), 0.0) * (
            DH ** (-0.5) / MAXLEN
        )
        heads.append((val, qry, key, wgt, slope))
    att = jnp.concatenate(attended, axis=1).astype(F32)
    acent = att - jnp.mean(att, axis=1, keepdims=True)
    arstd = lax.rsqrt(jnp.mean(acent * acent, axis=1, keepdims=True) + 1e-05)
    ahat = acent * arstd
    scaled = ahat * gat
    gated = (scaled * gate_u).astype(BF16)

    copies[2].wait()
    copies[3].wait()
    w_out = wo[...].reshape(AW, D)
    ct = ct_ref[...]
    out_ref[...] = (emb + mm(gated, w_out)).astype(BF16)

    d_gated = mm_nt(ct, w_out).astype(BF16).astype(F32)
    d_gate = (d_gated * scaled).astype(BF16).astype(F32)
    d_ahat = d_gated * gate_u * gat
    d_att = arstd * (
        d_ahat
        - jnp.mean(d_ahat, axis=1, keepdims=True)
        - ahat * jnp.mean(d_ahat * ahat, axis=1, keepdims=True)
    )
    d_att = d_att.astype(BF16)
    d_val, d_qry, d_key = [], [], []
    for h in range(H):
        val, qry, key, wgt, slope = heads[h]
        d_head = d_att[:, h * DH : (h + 1) * DH]
        d_wgt = mm_nt(d_head, val).astype(BF16).astype(F32)
        d_val.append(mm_tn(wgt, d_head).astype(BF16))
        d_score = (d_wgt * slope).astype(BF16)
        d_qry.append(mm(d_score, key).astype(BF16))
        d_key.append(mm_tn(d_score, qry).astype(BF16))
    d_act0 = jnp.concatenate([d_gate] + [v.astype(F32) for v in d_val], axis=1)
    d_act1 = jnp.concatenate([v.astype(F32) for v in d_qry + d_key], axis=1)
    d_mix0 = (d_act0 * slope0).astype(BF16)
    d_mix1 = (d_act1 * slope1).astype(BF16)
    dmx[0] = d_mix0
    dmx[1] = d_mix1
    d_normed = (mm_nt(d_mix0, wm0) + mm_nt(d_mix1, wm1)).astype(BF16).astype(F32)
    d_xhat = d_normed * gin
    d_emb = (
        rstd
        * (
            d_xhat
            - jnp.mean(d_xhat, axis=1, keepdims=True)
            - xhat * jnp.mean(d_xhat * xhat, axis=1, keepdims=True)
        )
        + ct.astype(F32)
    ).astype(BF16)
    slots_ref[...] = mm_tn(pick, d_emb).astype(BF16)
    for side, dst in ((1 - core, send_ref), (core, keep_ref)):
        dst[:, 0:1024] = normed
        dst[:, 1024:2048] = dmx[side]
        dst[:, 2048:2560] = gated
        dst[:, 2560:FACT] = ct_ref[:, pl.ds(pl.multiple_of(side * AW, AW), AW)]


def grads_kernel(keep_ref, theirs_ref, out_ref, buf, sems):
    def both(first, last):
        return jnp.concatenate([keep_ref[:, first:last], theirs_ref[:, first:last]], axis=0)

    grad = mm_tn(both(2048, 2560), both(2560, FACT))
    for z in range(NZ):
        for p in range(XY):
            r, c = z * 64 + (p // 2) * 8, (p % 2) * 256
            part = grad[r : r + 8, c : c + 256]
            buf[p, z, :, 512:PCOLS] = jnp.concatenate(
                [part[:, :128], part[:, 128:]], axis=0
            ).astype(BF16)

    copies = []
    d_mix = both(1024, 2048)
    for z in range(NZ):
        grad = mm_tn(both(z * TOK, (z + 1) * TOK), d_mix)
        for p in range(XY):
            part = grad[8 * p : 8 * p + 8]
            buf[p, z, :, 0:512] = jnp.concatenate(
                [part[:, :512], part[:, 512:]], axis=0
            ).astype(BF16)
        copies.append(pltpu.make_async_copy(buf.at[:, z], out_ref.at[:, z], sems.at[z]))
        copies[-1].start()
    for copy in copies:
        copy.wait()


def pack_kernel(rows_ref, asked_ref, out_ref):
    used = OWNERS * CAP
    r, k = iota((used, OWNERS * SLOTS), 0), iota((used, OWNERS * SLOTS), 1)
    take = (r // CAP == k // SLOTS) & (r % CAP == k % SLOTS)
    out_ref[:used] = mm(take.astype(F32).astype(BF16), rows_ref[...]).astype(BF16)
    asked = asked_ref[...]
    owner = (iota((256, OWNERS), 0) // CAP == iota((256, OWNERS), 1)).astype(F32).astype(BF16)
    slot = iota((256, 128), 0) % CAP == iota((256, 128), 1)
    parts = []
    for part in (asked & 127, asked >> 7):
        spread = mm(owner, part.astype(F32).astype(BF16))
        column = jnp.sum(jnp.where(slot, spread, 0.0), axis=1, keepdims=True)
        parts.append(jnp.broadcast_to(column, (256, 128)).T[:PROWS])
    which = iota((PROWS, 256), 0)
    numbers = jnp.where(which == 0, parts[0], jnp.where(which == 1, parts[1], 0.0))
    out_ref[used:] = jnp.concatenate(
        [numbers.astype(BF16), jnp.zeros((PROWS, D - 256), BF16)], axis=1
    )


def table_kernel(rows_ref, out_ref, buf, sems):
    used = OWNERS * CAP
    first = lax.axis_index("z") * 256
    copies = [
        pltpu.make_async_copy(rows_ref.at[z], buf.at[z], sems.at[z]) for z in range(NZ)
    ]
    for copy in copies:
        copy.start()
    total = jnp.zeros((256, D), F32)
    for z in range(NZ):
        copies[z].wait()
        names = buf[z, used : used + PROWS, :256].astype(F32)
        number = (names[0:1] + 128.0 * names[1:2]).astype(jnp.int32)[:, :used] - first
        here = (iota((256, used), 0) == number).astype(F32).astype(BF16)
        total = total + mm(here, buf[z, :used])
    out_ref[...] = total


def square_kernel(sums_ref, out_ref):
    total = jnp.zeros((PROWS, PCOLS), F32)
    for i in range(OWNERS):
        part = sums_ref[i].astype(F32)
        total = total + part * part
    mix = jnp.sum(total[:, :512])
    out = jnp.sum(total[:, 512:])
    lane = iota((NZ, 8, 128), 2)
    out_ref[...] = jnp.where(lane == 0, mix, jnp.where(lane == 1, out, 0.0))


def scale_kernel(sums_ref, squares_ref, mix_ref, out_ref):
    total = jnp.sum(squares_ref[...], axis=0)[0:1]
    mix_sq, out_sq = total[:, 0:1], total[:, 1:2]
    mix_scale = jnp.minimum(1.0, 1.0 / jnp.sqrt(mix_sq / float(D * 4 * AW) + 1e-06))
    out_scale = jnp.minimum(1.0, 1.0 / jnp.sqrt(out_sq / float(D * AW) + 1e-06))
    for p in range(XY):
        for core in range(2):
            sums = sums_ref[p * 2 + core].astype(F32)
            mix, out = sums[:, :512] * mix_scale, sums[:, 512:] * out_scale
            r, c = p * 8, core * D
            mix_ref[r : r + 8, c : c + 512] = mix[:8]
            mix_ref[r : r + 8, c + 512 : c + 1024] = mix[8:]
            r, c = (p // 2) * 8, core * AW + (p % 2) * 256
            out_ref[r : r + 8, c : c + 128] = out[:8]
            out_ref[r : r + 8, c + 128 : c + 256] = out[8:]


def vmem():
    return pl.BlockSpec(memory_space=pltpu.VMEM)


def call(body, outs, args, specs=None, **kwargs):
    shapes = [jax.ShapeDtypeStruct(s, t) for s, t in outs]
    one = len(shapes) == 1
    return pl.pallas_call(
        body,
        out_shape=shapes[0] if one else shapes,
        in_specs=specs or [vmem()] * len(args),
        out_specs=vmem() if one else [vmem()] * len(shapes),
        **kwargs,
    )(*args)


def cost(us):
    return pl.CostEstimate(flops=0, bytes_accessed=int(us * 3.0e6), transcendentals=0)


def exchange(array, axes):
    return lax.all_to_all(array, axes, split_axis=0, concat_axis=0, tiled=True)


def shards(
    item_table, item_row, item_owner, user_lengths, w_mix, w_out, gain_in, gain_attn, cotangent
):
    core = lax.axis_index("core")
    share = jnp.concatenate(
        [
            lax.dynamic_slice(w_mix, (0, core * D), (TOK, D)),
            lax.dynamic_slice(w_out, (core * 32, 0), (32, D)),
        ],
        axis=0,
    )
    weights = lax.all_gather(share, ("core", "z"), axis=0, tiled=True).reshape(2, NZ, 160, D)

    requests, target = call(
        plan_kernel,
        [((OWNERS, 128), jnp.int32), ((TOK, TOK), jnp.int32)],
        (item_owner.reshape(1, TOK), item_row.reshape(1, TOK)),
    )
    asked = exchange(requests, TABLE)
    wanted = asked[:, :SLOTS].reshape(OWNERS * SLOTS)
    found = item_table.at[wanted].get(mode="promise_in_bounds")
    got = exchange(found.reshape(OWNERS, SLOTS, D), TABLE)

    smem = pl.BlockSpec(memory_space=pltpu.SMEM)
    anywhere = pl.BlockSpec(memory_space=pl.ANY)
    layer_out, grad_slots, keep, send = call(
        layer_kernel,
        [
            ((TOK, D), BF16),
            ((OWNERS * SLOTS, D), BF16),
            ((TOK, FACT), BF16),
            ((TOK, FACT), BF16),
        ],
        (
            user_lengths,
            got.reshape(OWNERS * SLOTS, D),
            target,
            weights,
            gain_in.reshape(1, D),
            gain_attn.reshape(1, AW),
            cotangent,
        ),
        specs=[smem, vmem(), vmem(), anywhere, vmem(), vmem(), vmem()],
        scratch_shapes=[
            pltpu.VMEM((2, NZ, TOK, D), BF16),
            pltpu.VMEM((NZ, 2, 32, D), BF16),
            pltpu.VMEM((2, TOK, D), BF16),
            pltpu.SemaphoreType.DMA((4,)),
        ],
        cost_estimate=cost(9),
        compiler_params=pltpu.CompilerParams(vmem_limit_bytes=60 * MB),
    )

    theirs = lax.ppermute(send, "core", [(0, 1), (1, 0)])
    grads = pl.pallas_call(
        grads_kernel,
        out_shape=jax.ShapeDtypeStruct((XY, NZ, PROWS, PCOLS), BF16),
        in_specs=[vmem(), vmem()],
        out_specs=anywhere,
        scratch_shapes=[
            pltpu.VMEM((XY, NZ, PROWS, PCOLS), BF16),
            pltpu.SemaphoreType.DMA((NZ,)),
        ],
        cost_estimate=cost(3),
        compiler_params=pltpu.CompilerParams(vmem_limit_bytes=30 * MB),
    )(keep, theirs)
    row_sum = lax.psum_scatter(
        grads.reshape(XY * NZ * PROWS, PCOLS), "x", scatter_dimension=0, tiled=True
    )
    column = exchange(row_sum.reshape(4 * NZ, PROWS, PCOLS), ("y", "z"))
    whole = jnp.sum(column.astype(F32), axis=0).astype(BF16)
    sums = exchange(jnp.broadcast_to(whole[None], (OWNERS, PROWS, PCOLS)), TABLE)

    received = exchange(grad_slots.reshape(OWNERS, SLOTS, D), TABLE)
    packed = call(
        pack_kernel,
        [((GROWS, D), BF16)],
        (received.reshape(OWNERS * SLOTS, D), asked),
        cost_estimate=cost(2),
        compiler_params=pltpu.CompilerParams(vmem_limit_bytes=16 * MB),
    )
    gathered = lax.all_gather(packed, "z", axis=0, tiled=True).reshape(NZ, GROWS, D)
    table_grad = call(
        table_kernel,
        [((256, D), F32)],
        (gathered,),
        specs=[anywhere],
        scratch_shapes=[pltpu.VMEM((NZ, GROWS, D), BF16), pltpu.SemaphoreType.DMA((NZ,))],
        cost_estimate=cost(3),
        compiler_params=pltpu.CompilerParams(vmem_limit_bytes=60 * MB),
    )

    squares = call(
        square_kernel,
        [((NZ, 8, 128), F32)],
        (sums,),
        cost_estimate=cost(1),
        compiler_params=pltpu.CompilerParams(vmem_limit_bytes=16 * MB),
    )
    squares = exchange(squares, "z")
    mix_grad, out_grad = call(
        scale_kernel,
        [((TOK, 4 * AW), F32), ((64, D), F32)],
        (sums, squares),
        cost_estimate=cost(2),
        compiler_params=pltpu.CompilerParams(vmem_limit_bytes=16 * MB),
    )
    return (layer_out, table_grad, mix_grad, out_grad)


def solution(mesh):
    cube = Mesh(mesh.devices.reshape(4, 4, 2, 8), ALL)
    in_specs = (
        P(TABLE, None),
        P(ALL),
        P(ALL, None),
        P(ALL, None),
        P("z", None),
        P("z", None),
        P(),
        P(),
        P(ALL, None),
    )
    out_specs = (
        P(ALL, None),
        P(ALL, None),
        P("z", None),
        P("z", None),
    )
    return jax.shard_map(shards, mesh=cube, in_specs=in_specs, out_specs=out_specs, check_vma=False)
```

```python
import jax
import jax.numpy as jnp
from jax import lax
from jax.experimental import pallas as pl
from jax.experimental.pallas import tpu as pltpu
from jax.sharding import Mesh
from jax.sharding import PartitionSpec as P

H = 4
DH = 128
MAXLEN = 64
TOK = 128
D = 1024
AW = H * DH
OWNERS = 32
CAP = 6
SLOTS = 8
NZ = 8
XY = 16
PROWS = 16
PCOLS = 640
FACT = 3072
GROWS = OWNERS * CAP + 16
TABLE = ("x", "y", "core")
ALL = ("x", "y", "core", "z")
F32 = jnp.float32
BF16 = jnp.bfloat16
MB = 1024 * 1024


def mm(a, b):
    return lax.dot_general(a, b, (((1,), (0,)), ((), ())), preferred_element_type=F32)


def mm_nt(a, b):
    return lax.dot_general(a, b, (((1,), (1,)), ((), ())), preferred_element_type=F32)


def mm_tn(a, b):
    return lax.dot_general(a, b, (((0,), (0,)), ((), ())), preferred_element_type=F32)


def iota(shape, dim):
    return lax.broadcasted_iota(jnp.int32, shape, dim)


def share_kernel(mix_ref, out_ref, share_ref, sems):
    core = lax.axis_index("core")
    copies = [
        pltpu.make_async_copy(
            mix_ref.at[:, pl.ds(pl.multiple_of(core * D, D), D)],
            share_ref.at[pl.ds(0, TOK), :],
            sems.at[0],
        ),
        pltpu.make_async_copy(
            out_ref.at[pl.ds(pl.multiple_of(core * 32, 32), 32), :],
            share_ref.at[pl.ds(TOK, 32), :],
            sems.at[1],
        ),
    ]
    for copy in copies:
        copy.start()
    for copy in copies:
        copy.wait()


def plan_kernel(owner_ref, row_ref, req_ref, tgt_ref):
    square = (TOK, TOK)
    lane = iota(square, 1)

    def column(values):
        return jnp.broadcast_to(values.astype(F32), square).T

    row = row_ref[...]
    owner = column(owner_ref[...])
    low, high = column(row & 127), column(row >> 7)
    onehot = owner == lane.astype(F32)
    onehot_f = onehot.astype(F32)
    onehot_b = onehot_f.astype(BF16)
    earlier = (lane < iota(square, 0)).astype(F32).astype(BF16)
    before = mm(earlier, onehot_b)
    slot = jnp.sum(before * onehot_f, axis=1, keepdims=True)
    tgt_ref[...] = (owner * SLOTS + slot).astype(jnp.int32)
    here = slot == lane.astype(F32)
    low = jnp.where(here, low, 0.0).astype(BF16)
    high = jnp.where(here, high, 0.0).astype(BF16)
    requests = mm_tn(onehot_b, low) + 128.0 * mm_tn(onehot_b, high)
    req_ref[...] = requests[:OWNERS].astype(jnp.int32)


def layer_kernel(
    lens_ref, got_ref, tgt_ref, weights_ref, gin_ref, gat_ref, ct_ref,
    out_ref, slots_ref, keep_ref, send_ref,
    wm, wo, dmx, sems,
):
    core = lax.axis_index("core")
    copies = []
    for half in range(2):
        for part in range(4):
            z = pl.ds(2 * part, 2)
            copies.append(
                pltpu.make_async_copy(
                    weights_ref.at[half, z, pl.ds(0, TOK), :],
                    wm.at[half, z],
                    sems.at[len(copies)],
                )
            )
    for half in range(2):
        copies.append(
            pltpu.make_async_copy(
                weights_ref.at[half, :, pl.ds(TOK, 32), :], wo.at[:, half], sems.at[len(copies)]
            )
        )
    for copy in copies:
        copy.start()

    pick = (tgt_ref[:, :1] == iota((TOK, OWNERS * SLOTS), 1)).astype(F32).astype(BF16)
    emb = mm(pick, got_ref[...])
    gin = gin_ref[...]
    gat = gat_ref[...]
    centered = emb - jnp.mean(emb, axis=1, keepdims=True)
    rstd = lax.rsqrt(jnp.mean(centered * centered, axis=1, keepdims=True) + 1e-05)
    xhat = centered * rstd
    normed = (xhat * gin).astype(BF16)

    position, other = iota((TOK, TOK), 0), iota((TOK, TOK), 1)
    seg_row = jnp.zeros((TOK, TOK), jnp.int32)
    seg_col = jnp.zeros((TOK, TOK), jnp.int32)
    end = 0
    for user in range(lens_ref.shape[1]):
        end = end + lens_ref[0, user]
        seg_row = seg_row + (position >= end).astype(jnp.int32)
        seg_col = seg_col + (other >= end).astype(jnp.int32)
    allowed = (seg_row == seg_col) & (other <= position)

    mixtures = []
    for half in range(2):
        mixture = jnp.zeros((TOK, D), F32)
        for part in range(4):
            copies[4 * half + part].wait()
            rows = wm[half, 2 * part : 2 * part + 2].reshape(2 * TOK, D)
            mixture = mixture + mm(normed[:, 256 * part : 256 * part + 256], rows)
        mixtures.append(mixture)
    mix0, mix1 = mixtures
    wm0, wm1 = wm[0].reshape(D, D), wm[1].reshape(D, D)

    sig0, sig1 = jax.nn.sigmoid(mix0), jax.nn.sigmoid(mix1)
    act0, act1 = (mix0 * sig0).astype(BF16), (mix1 * sig1).astype(BF16)
    slope0 = sig0 * (1.0 + mix0 * (1.0 - sig0))
    slope1 = sig1 * (1.0 + mix1 * (1.0 - sig1))
    gate_u = act0[:, :AW].astype(F32)

    heads = []
    attended = []
    for h in range(H):
        val = act0[:, AW + h * DH : AW + (h + 1) * DH]
        qry = act1[:, h * DH : (h + 1) * DH]
        key = act1[:, AW + h * DH : AW + (h + 1) * DH]
        score = mm_nt(qry, key) * DH ** (-0.5)
        sig = jax.nn.sigmoid(score)
        wgt = (jnp.where(allowed, score * sig, 0.0) / MAXLEN).astype(BF16)
        attended.append(mm(wgt, val).astype(BF16))
        slope = jnp.where(allowed, sig * (1.0 + score * (1.0 - sig)), 0.0) * (
            DH ** (-0.5) / MAXLEN
        )
        heads.append((val, qry, key, wgt, slope))
    att = jnp.concatenate(attended, axis=1).astype(F32)
    acent = att - jnp.mean(att, axis=1, keepdims=True)
    arstd = lax.rsqrt(jnp.mean(acent * acent, axis=1, keepdims=True) + 1e-05)
    ahat = acent * arstd
    scaled = ahat * gat
    gated = (scaled * gate_u).astype(BF16)

    copies[8].wait()
    copies[9].wait()
    w_out = wo[...].reshape(AW, D)
    ct = ct_ref[...]
    out_ref[...] = (emb + mm(gated, w_out)).astype(BF16)

    d_gated = mm_nt(ct, w_out).astype(BF16).astype(F32)
    d_gate = (d_gated * scaled).astype(BF16).astype(F32)
    d_ahat = d_gated * gate_u * gat
    d_att = arstd * (
        d_ahat
        - jnp.mean(d_ahat, axis=1, keepdims=True)
        - ahat * jnp.mean(d_ahat * ahat, axis=1, keepdims=True)
    )
    d_att = d_att.astype(BF16)
    d_val, d_qry, d_key = [], [], []
    for h in range(H):
        val, qry, key, wgt, slope = heads[h]
        d_head = d_att[:, h * DH : (h + 1) * DH]
        d_wgt = mm_nt(d_head, val).astype(BF16).astype(F32)
        d_val.append(mm_tn(wgt, d_head).astype(BF16))
        d_score = (d_wgt * slope).astype(BF16)
        d_qry.append(mm(d_score, key).astype(BF16))
        d_key.append(mm_tn(d_score, qry).astype(BF16))
    d_act0 = jnp.concatenate([d_gate] + [v.astype(F32) for v in d_val], axis=1)
    d_act1 = jnp.concatenate([v.astype(F32) for v in d_qry + d_key], axis=1)
    d_mix0 = (d_act0 * slope0).astype(BF16)
    d_mix1 = (d_act1 * slope1).astype(BF16)
    dmx[0] = d_mix0
    dmx[1] = d_mix1
    d_normed = (mm_nt(d_mix0, wm0) + mm_nt(d_mix1, wm1)).astype(BF16).astype(F32)
    d_xhat = d_normed * gin
    d_emb = (
        rstd
        * (
            d_xhat
            - jnp.mean(d_xhat, axis=1, keepdims=True)
            - xhat * jnp.mean(d_xhat * xhat, axis=1, keepdims=True)
        )
        + ct.astype(F32)
    ).astype(BF16)
    slots_ref[...] = mm_tn(pick, d_emb).astype(BF16)
    for side, dst in ((1 - core, send_ref), (core, keep_ref)):
        dst[:, 0:1024] = normed
        dst[:, 1024:2048] = dmx[side]
        dst[:, 2048:2560] = gated
        dst[:, 2560:FACT] = ct_ref[:, pl.ds(pl.multiple_of(side * AW, AW), AW)]


def grads_kernel(keep_ref, theirs_ref, out_ref, buf, sems):
    def both(first, last):
        return jnp.concatenate([keep_ref[:, first:last], theirs_ref[:, first:last]], axis=0)

    grad = mm_tn(both(2048, 2560), both(2560, FACT))
    for z in range(NZ):
        for p in range(XY):
            r, c = z * 64 + (p // 2) * 8, (p % 2) * 256
            part = grad[r : r + 8, c : c + 256]
            buf[z, p, :, 512:PCOLS] = jnp.concatenate(
                [part[:, :128], part[:, 128:]], axis=0
            ).astype(BF16)

    copies = []
    d_mix = both(1024, 2048)
    for z in range(NZ):
        grad = mm_tn(both(z * TOK, (z + 1) * TOK), d_mix)
        for p in range(XY):
            part = grad[8 * p : 8 * p + 8]
            buf[z, p, :, 0:512] = jnp.concatenate(
                [part[:, :512], part[:, 512:]], axis=0
            ).astype(BF16)
        copies.append(pltpu.make_async_copy(buf.at[z], out_ref.at[z], sems.at[z]))
        copies[-1].start()
    for copy in copies:
        copy.wait()


def pack_kernel(rows_ref, asked_ref, out_ref):
    used = OWNERS * CAP
    r, k = iota((used, OWNERS * SLOTS), 0), iota((used, OWNERS * SLOTS), 1)
    take = (r // CAP == k // SLOTS) & (r % CAP == k % SLOTS)
    out_ref[:used] = mm(take.astype(F32).astype(BF16), rows_ref[...]).astype(BF16)
    asked = asked_ref[...]
    owner = (iota((256, OWNERS), 0) // CAP == iota((256, OWNERS), 1)).astype(F32).astype(BF16)
    slot = iota((256, 128), 0) % CAP == iota((256, 128), 1)
    parts = []
    for part in (asked & 127, asked >> 7):
        spread = mm(owner, part.astype(F32).astype(BF16))
        column = jnp.sum(jnp.where(slot, spread, 0.0), axis=1, keepdims=True)
        parts.append(jnp.broadcast_to(column, (256, 128)).T[:PROWS])
    which = iota((PROWS, 256), 0)
    numbers = jnp.where(which == 0, parts[0], jnp.where(which == 1, parts[1], 0.0))
    out_ref[used:] = jnp.concatenate(
        [numbers.astype(BF16), jnp.zeros((PROWS, D - 256), BF16)], axis=1
    )


def table_kernel(rows_ref, out_ref, buf, total, sems, out_sems):
    used = OWNERS * CAP
    first = lax.axis_index("z") * 256
    copies = [
        pltpu.make_async_copy(rows_ref.at[z], buf.at[z], sems.at[z]) for z in range(NZ)
    ]
    for copy in copies:
        copy.start()
    picks = []
    for z in range(NZ):
        copies[z].wait()
        names = buf[z, used : used + PROWS, :256].astype(F32)
        number = (names[0:1] + 128.0 * names[1:2]).astype(jnp.int32)[:, :used] - first
        picks.append((iota((256, used), 0) == number).astype(F32).astype(BF16))
    outs = []
    for n in range(4):
        cols = slice(256 * n, 256 * n + 256)
        part = mm(picks[0], buf[0, :used, cols])
        for z in range(1, NZ):
            part = part + mm(picks[z], buf[z, :used, cols])
        total[:, cols] = part
        block = pl.ds(256 * n, 256)
        outs.append(
            pltpu.make_async_copy(total.at[:, block], out_ref.at[:, block], out_sems.at[n])
        )
        outs[-1].start()
    for copy in outs:
        copy.wait()


def square_kernel(sums_ref, out_ref):
    total = jnp.zeros((PROWS, PCOLS), F32)
    for i in range(OWNERS):
        part = sums_ref[i].astype(F32)
        total = total + part * part
    mix = jnp.sum(total[:, :512])
    out = jnp.sum(total[:, 512:])
    lane = iota((NZ, 8, 128), 2)
    out_ref[...] = jnp.where(lane == 0, mix, jnp.where(lane == 1, out, 0.0))


def scale_kernel(sums_ref, squares_ref, mix_ref, out_ref):
    total = jnp.sum(squares_ref[...], axis=0)[0:1]
    mix_sq, out_sq = total[:, 0:1], total[:, 1:2]
    mix_scale = jnp.minimum(1.0, 1.0 / jnp.sqrt(mix_sq / float(D * 4 * AW) + 1e-06))
    out_scale = jnp.minimum(1.0, 1.0 / jnp.sqrt(out_sq / float(D * AW) + 1e-06))
    for p in range(XY):
        for core in range(2):
            sums = sums_ref[p * 2 + core].astype(F32)
            mix, out = sums[:, :512] * mix_scale, sums[:, 512:] * out_scale
            r, c = p * 8, core * D
            mix_ref[r : r + 8, c : c + 512] = mix[:8]
            mix_ref[r : r + 8, c + 512 : c + 1024] = mix[8:]
            r, c = (p // 2) * 8, core * AW + (p % 2) * 256
            out_ref[r : r + 8, c : c + 128] = out[:8]
            out_ref[r : r + 8, c + 128 : c + 256] = out[8:]


def vmem():
    return pl.BlockSpec(memory_space=pltpu.VMEM)


def call(body, outs, args, specs=None, outs_specs=None, **kwargs):
    shapes = [jax.ShapeDtypeStruct(s, t) for s, t in outs]
    one = len(shapes) == 1
    return pl.pallas_call(
        body,
        out_shape=shapes[0] if one else shapes,
        in_specs=specs or [vmem()] * len(args),
        out_specs=outs_specs or (vmem() if one else [vmem()] * len(shapes)),
        **kwargs,
    )(*args)


def cost(us):
    return pl.CostEstimate(flops=0, bytes_accessed=int(us * 3.0e6), transcendentals=0)


def exchange(array, axes):
    return lax.all_to_all(array, axes, split_axis=0, concat_axis=0, tiled=True)


def shards(
    item_table, item_row, item_owner, user_lengths, w_mix, w_out, gain_in, gain_attn, cotangent
):
    anywhere = pl.BlockSpec(memory_space=pl.ANY)
    share = call(
        share_kernel,
        [((TOK + 32, D), BF16)],
        (w_mix, w_out),
        specs=[anywhere, anywhere],
        outs_specs=anywhere,
        scratch_shapes=[pltpu.SemaphoreType.DMA((2,))],
        compiler_params=pltpu.CompilerParams(vmem_limit_bytes=60 * MB),
    )
    weights = lax.all_gather(share, ("core", "z"), axis=0, tiled=True).reshape(2, NZ, 160, D)

    requests, target = call(
        plan_kernel,
        [((OWNERS, 128), jnp.int32), ((TOK, TOK), jnp.int32)],
        (item_owner.reshape(1, TOK), item_row.reshape(1, TOK)),
    )
    asked = exchange(requests, TABLE)
    wanted = asked[:, :SLOTS].reshape(OWNERS * SLOTS)
    found = item_table.at[wanted].get(mode="promise_in_bounds")
    got = exchange(found.reshape(OWNERS, SLOTS, D), TABLE)

    smem = pl.BlockSpec(memory_space=pltpu.SMEM)
    layer_out, grad_slots, keep, send = call(
        layer_kernel,
        [
            ((TOK, D), BF16),
            ((OWNERS * SLOTS, D), BF16),
            ((TOK, FACT), BF16),
            ((TOK, FACT), BF16),
        ],
        (
            user_lengths,
            got.reshape(OWNERS * SLOTS, D),
            target,
            weights,
            gain_in.reshape(1, D),
            gain_attn.reshape(1, AW),
            cotangent,
        ),
        specs=[smem, vmem(), vmem(), anywhere, vmem(), vmem(), vmem()],
        scratch_shapes=[
            pltpu.VMEM((2, NZ, TOK, D), BF16),
            pltpu.VMEM((NZ, 2, 32, D), BF16),
            pltpu.VMEM((2, TOK, D), BF16),
            pltpu.SemaphoreType.DMA((10,)),
        ],
        cost_estimate=cost(9),
        compiler_params=pltpu.CompilerParams(vmem_limit_bytes=60 * MB),
    )

    theirs = lax.ppermute(send, "core", [(0, 1), (1, 0)])
    grads = pl.pallas_call(
        grads_kernel,
        out_shape=jax.ShapeDtypeStruct((NZ, XY, PROWS, PCOLS), BF16),
        in_specs=[vmem(), vmem()],
        out_specs=anywhere,
        scratch_shapes=[
            pltpu.VMEM((NZ, XY, PROWS, PCOLS), BF16),
            pltpu.SemaphoreType.DMA((NZ,)),
        ],
        cost_estimate=cost(3),
        compiler_params=pltpu.CompilerParams(vmem_limit_bytes=30 * MB),
    )(keep, theirs)
    column = lax.psum_scatter(
        grads.reshape(NZ * XY * PROWS, PCOLS), "z", scatter_dimension=0, tiled=True
    )
    plane = exchange(column.reshape(XY, PROWS, PCOLS), ("x", "y"))
    whole = jnp.sum(plane.astype(F32), axis=0).astype(BF16)
    sums = exchange(jnp.broadcast_to(whole[None], (OWNERS, PROWS, PCOLS)), TABLE)

    received = exchange(grad_slots.reshape(OWNERS, SLOTS, D), TABLE)
    packed = call(
        pack_kernel,
        [((GROWS, D), BF16)],
        (received.reshape(OWNERS * SLOTS, D), asked),
        cost_estimate=cost(2),
        compiler_params=pltpu.CompilerParams(vmem_limit_bytes=16 * MB),
    )
    gathered = lax.all_gather(packed, "z", axis=0, tiled=True).reshape(NZ, GROWS, D)
    table_grad = call(
        table_kernel,
        [((256, D), F32)],
        (gathered,),
        specs=[anywhere],
        outs_specs=anywhere,
        scratch_shapes=[
            pltpu.VMEM((NZ, GROWS, D), BF16),
            pltpu.VMEM((256, D), F32),
            pltpu.SemaphoreType.DMA((NZ,)),
            pltpu.SemaphoreType.DMA((4,)),
        ],
        cost_estimate=cost(3),
        compiler_params=pltpu.CompilerParams(vmem_limit_bytes=60 * MB),
    )

    squares = call(
        square_kernel,
        [((NZ, 8, 128), F32)],
        (sums,),
        cost_estimate=cost(1),
        compiler_params=pltpu.CompilerParams(vmem_limit_bytes=16 * MB),
    )
    squares = exchange(squares, "z")
    mix_grad, out_grad = call(
        scale_kernel,
        [((TOK, 4 * AW), F32), ((64, D), F32)],
        (sums, squares),
        cost_estimate=cost(2),
        compiler_params=pltpu.CompilerParams(vmem_limit_bytes=16 * MB),
    )
    return (layer_out, table_grad, mix_grad, out_grad)


def solution(mesh):
    cube = Mesh(mesh.devices.reshape(4, 4, 2, 8), ALL)
    in_specs = (
        P(TABLE, None),
        P(ALL),
        P(ALL, None),
        P(ALL, None),
        P("z", None),
        P("z", None),
        P(),
        P(),
        P(ALL, None),
    )
    out_specs = (
        P(ALL, None),
        P(ALL, None),
        P("z", None),
        P("z", None),
    )
    return jax.shard_map(shards, mesh=cube, in_specs=in_specs, out_specs=out_specs, check_vma=False)
```

```python
import jax
import jax.numpy as jnp
from jax import lax
from jax.experimental import pallas as pl
from jax.experimental.pallas import tpu as pltpu
from jax.sharding import Mesh
from jax.sharding import PartitionSpec as P

H = 4
DH = 128
MAXLEN = 64
TOK = 128
D = 1024
AW = H * DH
OWNERS = 32
CAP = 6
SLOTS = 8
NZ = 8
XY = 16
PROWS = 16
PCOLS = 640
FACT = 3072
GROWS = OWNERS * CAP
TABLE = ("x", "y", "core")
ALL = ("x", "y", "core", "z")
F32 = jnp.float32
BF16 = jnp.bfloat16
MB = 1024 * 1024


def mm(a, b):
    return lax.dot_general(a, b, (((1,), (0,)), ((), ())), preferred_element_type=F32)


def mm_nt(a, b):
    return lax.dot_general(a, b, (((1,), (1,)), ((), ())), preferred_element_type=F32)


def mm_tn(a, b):
    return lax.dot_general(a, b, (((0,), (0,)), ((), ())), preferred_element_type=F32)


def iota(shape, dim):
    return lax.broadcasted_iota(jnp.int32, shape, dim)


def share_kernel(mix_ref, out_ref, share_ref):
    core = lax.axis_index("core")
    share_ref[:TOK] = mix_ref[:, pl.ds(pl.multiple_of(core * D, D), D)]
    share_ref[TOK:] = out_ref[pl.ds(pl.multiple_of(core * 32, 32), 32), :]


def plan_kernel(owner_ref, row_ref, req_ref, tgt_ref):
    square = (TOK, TOK)
    lane = iota(square, 1)

    def column(values):
        return jnp.broadcast_to(values.astype(F32), square).T

    row = row_ref[...]
    owner = column(owner_ref[...])
    low, high = column(row & 127), column(row >> 7)
    onehot = owner == lane.astype(F32)
    onehot_f = onehot.astype(F32)
    onehot_b = onehot_f.astype(BF16)
    earlier = (lane < iota(square, 0)).astype(F32).astype(BF16)
    before = mm(earlier, onehot_b)
    slot = jnp.sum(before * onehot_f, axis=1, keepdims=True)
    tgt_ref[...] = (owner * SLOTS + slot).astype(jnp.int32)
    here = slot == lane.astype(F32)
    low = jnp.where(here, low, 0.0).astype(BF16)
    high = jnp.where(here, high, 0.0).astype(BF16)
    requests = mm_tn(onehot_b, low) + 128.0 * mm_tn(onehot_b, high)
    req_ref[...] = requests[:OWNERS].astype(jnp.int32)


def layer_kernel(
    lens_ref, got_ref, tgt_ref, weights_ref, gin_ref, gat_ref, ct_ref, after_ref,
    out_ref, slots_ref, keep_ref, send_ref,
    wm, wo, dmx, sems,
):
    core = lax.axis_index("core")
    copies = []
    for half in range(2):
        for part in range(4):
            z = pl.ds(2 * part, 2)
            copies.append(
                pltpu.make_async_copy(
                    weights_ref.at[half, z, pl.ds(0, TOK), :],
                    wm.at[half, z],
                    sems.at[len(copies)],
                )
            )
    for half in range(2):
        copies.append(
            pltpu.make_async_copy(
                weights_ref.at[half, :, pl.ds(TOK, 32), :], wo.at[:, half], sems.at[len(copies)]
            )
        )
    for copy in copies:
        copy.start()

    pick = (tgt_ref[:, :1] == iota((TOK, OWNERS * SLOTS), 1)).astype(F32).astype(BF16)
    emb = mm(pick, got_ref[...])
    gin = gin_ref[...]
    gat = gat_ref[...]
    centered = emb - jnp.mean(emb, axis=1, keepdims=True)
    rstd = lax.rsqrt(jnp.mean(centered * centered, axis=1, keepdims=True) + 1e-05)
    xhat = centered * rstd
    normed = (xhat * gin).astype(BF16)

    position, other = iota((TOK, TOK), 0), iota((TOK, TOK), 1)
    seg_row = jnp.zeros((TOK, TOK), jnp.int32)
    seg_col = jnp.zeros((TOK, TOK), jnp.int32)
    end = 0
    for user in range(lens_ref.shape[1]):
        end = end + lens_ref[0, user]
        seg_row = seg_row + (position >= end).astype(jnp.int32)
        seg_col = seg_col + (other >= end).astype(jnp.int32)
    allowed = (seg_row == seg_col) & (other <= position)

    mixtures = []
    for half in range(2):
        mixture = jnp.zeros((TOK, D), F32)
        for part in range(4):
            copies[4 * half + part].wait()
            rows = wm[half, 2 * part : 2 * part + 2].reshape(2 * TOK, D)
            mixture = mixture + mm(normed[:, 256 * part : 256 * part + 256], rows)
        mixtures.append(mixture)
    mix0, mix1 = mixtures
    wm0, wm1 = wm[0].reshape(D, D), wm[1].reshape(D, D)

    sig0, sig1 = jax.nn.sigmoid(mix0), jax.nn.sigmoid(mix1)
    act0, act1 = (mix0 * sig0).astype(BF16), (mix1 * sig1).astype(BF16)
    slope0 = sig0 * (1.0 + mix0 * (1.0 - sig0))
    slope1 = sig1 * (1.0 + mix1 * (1.0 - sig1))
    gate_u = act0[:, :AW].astype(F32)

    heads = []
    attended = []
    for h in range(H):
        val = act0[:, AW + h * DH : AW + (h + 1) * DH]
        qry = act1[:, h * DH : (h + 1) * DH]
        key = act1[:, AW + h * DH : AW + (h + 1) * DH]
        score = mm_nt(qry, key) * DH ** (-0.5)
        sig = jax.nn.sigmoid(score)
        wgt = (jnp.where(allowed, score * sig, 0.0) / MAXLEN).astype(BF16)
        attended.append(mm(wgt, val).astype(BF16))
        slope = jnp.where(allowed, sig * (1.0 + score * (1.0 - sig)), 0.0) * (
            DH ** (-0.5) / MAXLEN
        )
        heads.append((val, qry, key, wgt, slope))
    att = jnp.concatenate(attended, axis=1).astype(F32)
    acent = att - jnp.mean(att, axis=1, keepdims=True)
    arstd = lax.rsqrt(jnp.mean(acent * acent, axis=1, keepdims=True) + 1e-05)
    ahat = acent * arstd
    scaled = ahat * gat
    gated = (scaled * gate_u).astype(BF16)

    copies[8].wait()
    copies[9].wait()
    w_out = wo[...].reshape(AW, D)
    ct = ct_ref[...]
    out_ref[...] = (emb + mm(gated, w_out)).astype(BF16)

    d_gated = mm_nt(ct, w_out).astype(BF16).astype(F32)
    d_gate = (d_gated * scaled).astype(BF16).astype(F32)
    d_ahat = d_gated * gate_u * gat
    d_att = arstd * (
        d_ahat
        - jnp.mean(d_ahat, axis=1, keepdims=True)
        - ahat * jnp.mean(d_ahat * ahat, axis=1, keepdims=True)
    )
    d_att = d_att.astype(BF16)
    d_val, d_qry, d_key = [], [], []
    for h in range(H):
        val, qry, key, wgt, slope = heads[h]
        d_head = d_att[:, h * DH : (h + 1) * DH]
        d_wgt = mm_nt(d_head, val).astype(BF16).astype(F32)
        d_val.append(mm_tn(wgt, d_head).astype(BF16))
        d_score = (d_wgt * slope).astype(BF16)
        d_qry.append(mm(d_score, key).astype(BF16))
        d_key.append(mm_tn(d_score, qry).astype(BF16))
    d_act0 = jnp.concatenate([d_gate] + [v.astype(F32) for v in d_val], axis=1)
    d_act1 = jnp.concatenate([v.astype(F32) for v in d_qry + d_key], axis=1)
    d_mix0 = (d_act0 * slope0).astype(BF16)
    d_mix1 = (d_act1 * slope1).astype(BF16)
    dmx[0] = d_mix0
    dmx[1] = d_mix1
    d_normed = (mm_nt(d_mix0, wm0) + mm_nt(d_mix1, wm1)).astype(BF16).astype(F32)
    d_xhat = d_normed * gin
    d_emb = (
        rstd
        * (
            d_xhat
            - jnp.mean(d_xhat, axis=1, keepdims=True)
            - xhat * jnp.mean(d_xhat * xhat, axis=1, keepdims=True)
        )
        + ct.astype(F32)
    ).astype(BF16)
    slots_ref[...] = mm_tn(pick, d_emb).astype(BF16)
    for side, dst in ((1 - core, send_ref), (core, keep_ref)):
        dst[:, 0:1024] = normed
        dst[:, 1024:2048] = dmx[side]
        dst[:, 2048:2560] = gated
        dst[:, 2560:FACT] = ct_ref[:, pl.ds(pl.multiple_of(side * AW, AW), AW)]


def grads_kernel(keep_ref, theirs_ref, out_ref, buf, sems):
    def both(first, last):
        return jnp.concatenate([keep_ref[:, first:last], theirs_ref[:, first:last]], axis=0)

    grad = mm_tn(both(2048, 2560), both(2560, FACT))
    for z in range(NZ):
        for p in range(XY):
            r, c = z * 64 + (p // 2) * 8, (p % 2) * 256
            part = grad[r : r + 8, c : c + 256]
            buf[z, p, :, 512:PCOLS] = jnp.concatenate(
                [part[:, :128], part[:, 128:]], axis=0
            ).astype(BF16)

    copies = []
    d_mix = both(1024, 2048)
    for z in range(NZ):
        grad = mm_tn(both(z * TOK, (z + 1) * TOK), d_mix)
        for p in range(XY):
            part = grad[8 * p : 8 * p + 8]
            buf[z, p, :, 0:512] = jnp.concatenate(
                [part[:, :512], part[:, 512:]], axis=0
            ).astype(BF16)
        copies.append(pltpu.make_async_copy(buf.at[z], out_ref.at[z], sems.at[z]))
        copies[-1].start()
    for copy in copies:
        copy.wait()


def pack_kernel(rows_ref, out_ref):
    r, k = iota((GROWS, OWNERS * SLOTS), 0), iota((GROWS, OWNERS * SLOTS), 1)
    take = (r // CAP) * SLOTS + r % CAP == k
    out_ref[...] = mm(take.astype(F32).astype(BF16), rows_ref[...]).astype(BF16)


def names_kernel(asked_ref, out_ref):
    first = lax.axis_index("z") * 256
    count = NZ * GROWS
    asked = asked_ref[...].reshape(NZ * OWNERS, 128)
    row, col = iota((count, NZ * OWNERS), 0), iota((count, NZ * OWNERS), 1)
    owner = (row // CAP == col).astype(F32).astype(BF16)
    lane = iota((count, 128), 1)
    spread = mm(owner, (asked & 127).astype(F32).astype(BF16)) + 128.0 * mm(
        owner, (asked >> 7).astype(F32).astype(BF16)
    )
    column = jnp.sum(
        jnp.where(iota((count, 128), 0) % CAP == lane, spread, 0.0), axis=1, keepdims=True
    )
    names = jnp.zeros((128, 128), F32)
    for line in range(count // 128):
        names = jnp.where(
            iota((128, 128), 1) == line, column[128 * line : 128 * line + 128], names
        )
    out_ref[...] = names.T[:PROWS].astype(jnp.int32) - first


def table_kernel(rows_ref, names_ref, after_ref, out_ref, buf, sems):
    half = NZ * GROWS // 2
    copies = [
        pltpu.make_async_copy(
            rows_ref.at[pl.ds(part * half, half), :], buf.at[part], sems.at[part]
        )
        for part in range(2)
    ]
    for copy in copies:
        copy.start()
    place = iota((256, 128), 0)
    lines = half // 128
    for part in range(2):
        pick = jnp.concatenate(
            [
                (place == names_ref[line : line + 1, :]).astype(F32).astype(BF16)
                for line in range(part * lines, (part + 1) * lines)
            ],
            axis=1,
        )
        copies[part].wait()
        total = mm(pick, buf[part])
        if part == 0:
            out_ref[...] = total
        else:
            out_ref[...] += total


def square_kernel(sums_ref, out_ref):
    total = jnp.zeros((PROWS, PCOLS), F32)
    for i in range(OWNERS):
        part = sums_ref[i].astype(F32)
        total = total + part * part
    mix = jnp.sum(total[:, :512])
    out = jnp.sum(total[:, 512:])
    lane = iota((NZ, 8, 128), 2)
    out_ref[...] = jnp.where(lane == 0, mix, jnp.where(lane == 1, out, 0.0))


def scale_kernel(sums_ref, squares_ref, mix_ref, out_ref):
    total = jnp.sum(squares_ref[...], axis=0)[0:1]
    mix_sq, out_sq = total[:, 0:1], total[:, 1:2]
    mix_scale = jnp.minimum(1.0, 1.0 / jnp.sqrt(mix_sq / float(D * 4 * AW) + 1e-06))
    out_scale = jnp.minimum(1.0, 1.0 / jnp.sqrt(out_sq / float(D * AW) + 1e-06))
    for p in range(XY):
        for core in range(2):
            sums = sums_ref[p * 2 + core].astype(F32)
            mix, out = sums[:, :512] * mix_scale, sums[:, 512:] * out_scale
            r, c = p * 8, core * D
            mix_ref[r : r + 8, c : c + 512] = mix[:8]
            mix_ref[r : r + 8, c + 512 : c + 1024] = mix[8:]
            r, c = (p // 2) * 8, core * AW + (p % 2) * 256
            out_ref[r : r + 8, c : c + 128] = out[:8]
            out_ref[r : r + 8, c + 128 : c + 256] = out[8:]


def vmem():
    return pl.BlockSpec(memory_space=pltpu.VMEM)


def call(body, outs, args, specs=None, outs_specs=None, **kwargs):
    shapes = [jax.ShapeDtypeStruct(s, t) for s, t in outs]
    one = len(shapes) == 1
    return pl.pallas_call(
        body,
        out_shape=shapes[0] if one else shapes,
        in_specs=specs or [vmem()] * len(args),
        out_specs=outs_specs or (vmem() if one else [vmem()] * len(shapes)),
        **kwargs,
    )(*args)


def cost(us):
    return pl.CostEstimate(flops=0, bytes_accessed=int(us * 3.0e6), transcendentals=0)


def exchange(array, axes):
    return lax.all_to_all(array, axes, split_axis=0, concat_axis=0, tiled=True)


def shards(
    item_table, item_row, item_owner, user_lengths, w_mix, w_out, gain_in, gain_attn, cotangent
):
    anywhere = pl.BlockSpec(memory_space=pl.ANY)
    pinned = pl.BlockSpec(memory_space=pltpu.HBM)
    share = call(share_kernel, [((TOK + 32, D), BF16)], (w_mix, w_out))
    weights = lax.all_gather(share, ("core", "z"), axis=0, tiled=True).reshape(2, NZ, 160, D)

    requests, target = call(
        plan_kernel,
        [((OWNERS, 128), jnp.int32), ((TOK, TOK), jnp.int32)],
        (item_owner.reshape(1, TOK), item_row.reshape(1, TOK)),
    )
    asked = exchange(requests, TABLE)
    names = call(
        names_kernel,
        [((PROWS, 128), jnp.int32)],
        (exchange(jnp.broadcast_to(asked[None], (NZ, OWNERS, 128)), "z"),),
        cost_estimate=cost(1),
    )
    wanted = asked[:, :SLOTS].reshape(OWNERS * SLOTS)
    found = item_table.at[wanted].get(mode="promise_in_bounds")
    got = exchange(found.reshape(OWNERS, SLOTS, D), TABLE)

    smem = pl.BlockSpec(memory_space=pltpu.SMEM)
    layer_out, grad_slots, keep, send = call(
        layer_kernel,
        [
            ((TOK, D), BF16),
            ((OWNERS * SLOTS, D), BF16),
            ((TOK, FACT), BF16),
            ((TOK, FACT), BF16),
        ],
        (
            user_lengths,
            got.reshape(OWNERS * SLOTS, D),
            target,
            weights,
            gain_in.reshape(1, D),
            gain_attn.reshape(1, AW),
            cotangent,
            names,
        ),
        specs=[smem, vmem(), vmem(), pinned, vmem(), vmem(), vmem(), anywhere],
        scratch_shapes=[
            pltpu.VMEM((2, NZ, TOK, D), BF16),
            pltpu.VMEM((NZ, 2, 32, D), BF16),
            pltpu.VMEM((2, TOK, D), BF16),
            pltpu.SemaphoreType.DMA((10,)),
        ],
        cost_estimate=cost(9),
        compiler_params=pltpu.CompilerParams(vmem_limit_bytes=32 * MB),
    )

    theirs = lax.ppermute(send, "core", [(0, 1), (1, 0)])
    grads = pl.pallas_call(
        grads_kernel,
        out_shape=jax.ShapeDtypeStruct((NZ, XY, PROWS, PCOLS), BF16),
        in_specs=[vmem(), vmem()],
        out_specs=anywhere,
        scratch_shapes=[
            pltpu.VMEM((NZ, XY, PROWS, PCOLS), BF16),
            pltpu.SemaphoreType.DMA((NZ,)),
        ],
        cost_estimate=cost(3),
        compiler_params=pltpu.CompilerParams(vmem_limit_bytes=30 * MB),
    )(keep, theirs)
    column = lax.psum_scatter(
        grads.reshape(NZ * XY * PROWS, PCOLS), "z", scatter_dimension=0, tiled=True
    )
    plane = exchange(column.reshape(XY, PROWS, PCOLS), ("x", "y"))
    whole = jnp.sum(plane.astype(F32), axis=0).astype(BF16)
    sums = exchange(jnp.broadcast_to(whole[None], (OWNERS, PROWS, PCOLS)), TABLE)

    received = exchange(grad_slots.reshape(OWNERS, SLOTS, D), TABLE)
    packed = call(
        pack_kernel,
        [((GROWS, D), BF16)],
        (received.reshape(OWNERS * SLOTS, D),),
        cost_estimate=cost(2),
        compiler_params=pltpu.CompilerParams(vmem_limit_bytes=16 * MB),
    )
    gathered = lax.all_gather(packed, "z", axis=0, tiled=True)
    squares = call(
        square_kernel,
        [((NZ, 8, 128), F32)],
        (sums,),
        cost_estimate=cost(1),
        compiler_params=pltpu.CompilerParams(vmem_limit_bytes=16 * MB),
    )
    squares = exchange(squares, "z")
    mix_grad, out_grad = call(
        scale_kernel,
        [((TOK, 4 * AW), F32), ((64, D), F32)],
        (sums, squares),
        cost_estimate=cost(2),
        compiler_params=pltpu.CompilerParams(vmem_limit_bytes=16 * MB),
    )
    table_grad = call(
        table_kernel,
        [((256, D), F32)],
        (gathered, names, out_grad),
        specs=[pinned, vmem(), anywhere],
        scratch_shapes=[
            pltpu.VMEM((2, NZ * GROWS // 2, D), BF16),
            pltpu.SemaphoreType.DMA((2,)),
        ],
        cost_estimate=cost(3),
        compiler_params=pltpu.CompilerParams(vmem_limit_bytes=60 * MB),
    )
    return (layer_out, table_grad, mix_grad, out_grad)


def solution(mesh):
    cube = Mesh(mesh.devices.reshape(4, 4, 2, 8), ALL)
    in_specs = (
        P(TABLE, None),
        P(ALL),
        P(ALL, None),
        P(ALL, None),
        P("z", None),
        P("z", None),
        P(),
        P(),
        P(ALL, None),
    )
    out_specs = (
        P(ALL, None),
        P(ALL, None),
        P("z", None),
        P("z", None),
    )
    return jax.shard_map(shards, mesh=cube, in_specs=in_specs, out_specs=out_specs, check_vma=False)
```

```python
import jax
import jax.numpy as jnp
from jax import lax
from jax.experimental import pallas as pl
from jax.experimental.pallas import tpu as pltpu
from jax.sharding import Mesh
from jax.sharding import PartitionSpec as P

H = 4
DH = 128
MAXLEN = 64
TOK = 128
D = 1024
AW = H * DH
OWNERS = 32
CAP = 6
SLOTS = 8
NZ = 8
XY = 16
PROWS = 16
PCOLS = 640
FACT = 3072
USED = OWNERS * CAP
LATE = 160
EARLY = USED - LATE
TABLE = ("x", "y", "core")
ALL = ("x", "y", "core", "z")
F32 = jnp.float32
BF16 = jnp.bfloat16
MB = 1024 * 1024


def mm(a, b):
    return lax.dot_general(a, b, (((1,), (0,)), ((), ())), preferred_element_type=F32)


def mm_nt(a, b):
    return lax.dot_general(a, b, (((1,), (1,)), ((), ())), preferred_element_type=F32)


def mm_tn(a, b):
    return lax.dot_general(a, b, (((0,), (0,)), ((), ())), preferred_element_type=F32)


def iota(shape, dim):
    return lax.broadcasted_iota(jnp.int32, shape, dim)


def share_kernel(mix_ref, out_ref, share_ref):
    core = lax.axis_index("core")
    share_ref[:TOK] = mix_ref[:, pl.ds(pl.multiple_of(core * D, D), D)]
    share_ref[TOK:] = out_ref[pl.ds(pl.multiple_of(core * 32, 32), 32), :]


def plan_kernel(owner_ref, row_ref, req_ref, tgt_ref):
    square = (TOK, TOK)
    lane = iota(square, 1)

    def column(values):
        return jnp.broadcast_to(values.astype(F32), square).T

    row = row_ref[...]
    owner = column(owner_ref[...])
    low, high = column(row & 127), column(row >> 7)
    onehot = owner == lane.astype(F32)
    onehot_f = onehot.astype(F32)
    onehot_b = onehot_f.astype(BF16)
    earlier = (lane < iota(square, 0)).astype(F32).astype(BF16)
    before = mm(earlier, onehot_b)
    slot = jnp.sum(before * onehot_f, axis=1, keepdims=True)
    tgt_ref[...] = (owner * SLOTS + slot).astype(jnp.int32)
    here = slot == lane.astype(F32)
    low = jnp.where(here, low, 0.0).astype(BF16)
    high = jnp.where(here, high, 0.0).astype(BF16)
    requests = mm_tn(onehot_b, low) + 128.0 * mm_tn(onehot_b, high)
    req_ref[...] = requests[:OWNERS].astype(jnp.int32)


def layer_kernel(
    lens_ref, got_ref, tgt_ref, weights_ref, gin_ref, gat_ref, ct_ref,
    out_ref, slots_ref, keep_ref, send_ref,
    wm, wo, dmx, sems,
):
    core = lax.axis_index("core")
    copies = []
    for half in range(2):
        for part in range(4):
            z = pl.ds(2 * part, 2)
            copies.append(
                pltpu.make_async_copy(
                    weights_ref.at[half, z, pl.ds(0, TOK), :],
                    wm.at[half, z],
                    sems.at[len(copies)],
                )
            )
    for half in range(2):
        copies.append(
            pltpu.make_async_copy(
                weights_ref.at[half, :, pl.ds(TOK, 32), :], wo.at[:, half], sems.at[len(copies)]
            )
        )
    for copy in copies:
        copy.start()

    pick = (tgt_ref[:, :1] == iota((TOK, OWNERS * SLOTS), 1)).astype(F32).astype(BF16)
    emb = mm(pick, got_ref[...])
    gin = gin_ref[...]
    gat = gat_ref[...]
    centered = emb - jnp.mean(emb, axis=1, keepdims=True)
    rstd = lax.rsqrt(jnp.mean(centered * centered, axis=1, keepdims=True) + 1e-05)
    xhat = centered * rstd
    normed = (xhat * gin).astype(BF16)

    position, other = iota((TOK, TOK), 0), iota((TOK, TOK), 1)
    seg_row = jnp.zeros((TOK, TOK), jnp.int32)
    seg_col = jnp.zeros((TOK, TOK), jnp.int32)
    end = 0
    for user in range(lens_ref.shape[1]):
        end = end + lens_ref[0, user]
        seg_row = seg_row + (position >= end).astype(jnp.int32)
        seg_col = seg_col + (other >= end).astype(jnp.int32)
    allowed = (seg_row == seg_col) & (other <= position)

    mixtures = []
    for half in range(2):
        mixture = jnp.zeros((TOK, D), F32)
        for part in range(4):
            copies[4 * half + part].wait()
            rows = wm[half, 2 * part : 2 * part + 2].reshape(2 * TOK, D)
            mixture = mixture + mm(normed[:, 256 * part : 256 * part + 256], rows)
        mixtures.append(mixture)
    mix0, mix1 = mixtures
    wm0, wm1 = wm[0].reshape(D, D), wm[1].reshape(D, D)

    sig0, sig1 = jax.nn.sigmoid(mix0), jax.nn.sigmoid(mix1)
    act0, act1 = (mix0 * sig0).astype(BF16), (mix1 * sig1).astype(BF16)
    slope0 = sig0 * (1.0 + mix0 * (1.0 - sig0))
    slope1 = sig1 * (1.0 + mix1 * (1.0 - sig1))
    gate_u = act0[:, :AW].astype(F32)

    heads = []
    attended = []
    for h in range(H):
        val = act0[:, AW + h * DH : AW + (h + 1) * DH]
        qry = act1[:, h * DH : (h + 1) * DH]
        key = act1[:, AW + h * DH : AW + (h + 1) * DH]
        score = mm_nt(qry, key) * DH ** (-0.5)
        sig = jax.nn.sigmoid(score)
        wgt = (jnp.where(allowed, score * sig, 0.0) / MAXLEN).astype(BF16)
        attended.append(mm(wgt, val).astype(BF16))
        slope = jnp.where(allowed, sig * (1.0 + score * (1.0 - sig)), 0.0) * (
            DH ** (-0.5) / MAXLEN
        )
        heads.append((val, qry, key, wgt, slope))
    att = jnp.concatenate(attended, axis=1).astype(F32)
    acent = att - jnp.mean(att, axis=1, keepdims=True)
    arstd = lax.rsqrt(jnp.mean(acent * acent, axis=1, keepdims=True) + 1e-05)
    ahat = acent * arstd
    scaled = ahat * gat
    gated = (scaled * gate_u).astype(BF16)

    copies[8].wait()
    copies[9].wait()
    w_out = wo[...].reshape(AW, D)
    ct = ct_ref[...]
    out_ref[...] = (emb + mm(gated, w_out)).astype(BF16)

    d_gated = mm_nt(ct, w_out).astype(BF16).astype(F32)
    d_gate = (d_gated * scaled).astype(BF16).astype(F32)
    d_ahat = d_gated * gate_u * gat
    d_att = arstd * (
        d_ahat
        - jnp.mean(d_ahat, axis=1, keepdims=True)
        - ahat * jnp.mean(d_ahat * ahat, axis=1, keepdims=True)
    )
    d_att = d_att.astype(BF16)
    d_val, d_qry, d_key = [], [], []
    for h in range(H):
        val, qry, key, wgt, slope = heads[h]
        d_head = d_att[:, h * DH : (h + 1) * DH]
        d_wgt = mm_nt(d_head, val).astype(BF16).astype(F32)
        d_val.append(mm_tn(wgt, d_head).astype(BF16))
        d_score = (d_wgt * slope).astype(BF16)
        d_qry.append(mm(d_score, key).astype(BF16))
        d_key.append(mm_tn(d_score, qry).astype(BF16))
    d_act0 = jnp.concatenate([d_gate] + [v.astype(F32) for v in d_val], axis=1)
    d_act1 = jnp.concatenate([v.astype(F32) for v in d_qry + d_key], axis=1)
    d_mix0 = (d_act0 * slope0).astype(BF16)
    d_mix1 = (d_act1 * slope1).astype(BF16)
    dmx[0] = d_mix0
    dmx[1] = d_mix1
    d_normed = (mm_nt(d_mix0, wm0) + mm_nt(d_mix1, wm1)).astype(BF16).astype(F32)
    d_xhat = d_normed * gin
    d_emb = (
        rstd
        * (
            d_xhat
            - jnp.mean(d_xhat, axis=1, keepdims=True)
            - xhat * jnp.mean(d_xhat * xhat, axis=1, keepdims=True)
        )
        + ct.astype(F32)
    ).astype(BF16)
    slots_ref[...] = mm_tn(pick, d_emb).astype(BF16)
    for side, dst in ((1 - core, send_ref), (core, keep_ref)):
        dst[:, 0:1024] = normed
        dst[:, 1024:2048] = dmx[side]
        dst[:, 2048:2560] = gated
        dst[:, 2560:FACT] = ct_ref[:, pl.ds(pl.multiple_of(side * AW, AW), AW)]


def grads_kernel(keep_ref, theirs_ref, out_ref, buf, sems):
    def both(first, last):
        return jnp.concatenate([keep_ref[:, first:last], theirs_ref[:, first:last]], axis=0)

    grad = mm_tn(both(2048, 2560), both(2560, FACT))
    for z in range(NZ):
        for p in range(XY):
            r, c = z * 64 + (p // 2) * 8, (p % 2) * 256
            part = grad[r : r + 8, c : c + 256]
            buf[z, p, :, 512:PCOLS] = jnp.concatenate(
                [part[:, :128], part[:, 128:]], axis=0
            ).astype(BF16)

    copies = []
    d_mix = both(1024, 2048)
    for z in range(NZ):
        grad = mm_tn(both(z * TOK, (z + 1) * TOK), d_mix)
        for p in range(XY):
            part = grad[8 * p : 8 * p + 8]
            buf[z, p, :, 0:512] = jnp.concatenate(
                [part[:, :512], part[:, 512:]], axis=0
            ).astype(BF16)
        copies.append(pltpu.make_async_copy(buf.at[z], out_ref.at[z], sems.at[z]))
        copies[-1].start()
    for copy in copies:
        copy.wait()


def pack_kernel(rows_ref, asked_ref, late_ref, early_ref):
    r, k = iota((USED, OWNERS * SLOTS), 0), iota((USED, OWNERS * SLOTS), 1)
    take = ((r // CAP) * SLOTS + r % CAP == k).astype(F32).astype(BF16)
    rows = mm(take, rows_ref[...]).astype(BF16)
    late_ref[...] = rows[:LATE]
    early_ref[:EARLY] = rows[LATE:]
    asked = asked_ref[...]
    owner = (iota((256, OWNERS), 0) // CAP == iota((256, OWNERS), 1)).astype(F32).astype(BF16)
    slot = iota((256, 128), 0) % CAP == iota((256, 128), 1)
    parts = []
    for part in (asked & 127, asked >> 7):
        spread = mm(owner, part.astype(F32).astype(BF16))
        column = jnp.sum(jnp.where(slot, spread, 0.0), axis=1, keepdims=True)
        parts.append(jnp.broadcast_to(column, (256, 128)).T[:PROWS])
    which = iota((PROWS, 256), 0)
    numbers = jnp.where(which == 0, parts[0], jnp.where(which == 1, parts[1], 0.0))
    early_ref[EARLY:] = jnp.concatenate(
        [numbers.astype(BF16), jnp.zeros((PROWS, D - 256), BF16)], axis=1
    )


def names_kernel(early_ref, out_ref):
    first = lax.axis_index("z") * 256
    count = NZ * USED
    parts = early_ref[:, EARLY:, :256].reshape(NZ * PROWS, 256)
    k, col = iota((count, 128), 0), iota((count, 128), 1)
    late = k < NZ * LATE
    source = jnp.where(late, k // LATE, (k - NZ * LATE) // EARLY)
    low, high = (
        mm((col == source * PROWS + i).astype(F32).astype(BF16), parts) for i in range(2)
    )
    k = iota((count, 256), 0)
    place = jnp.where(k < NZ * LATE, k % LATE, LATE + (k - NZ * LATE) % EARLY)
    column = jnp.sum(
        jnp.where(iota((count, 256), 1) == place, low + 128.0 * high, 0.0), axis=1, keepdims=True
    )
    names = jnp.zeros((128, 128), F32)
    for line in range(count // 128):
        names = jnp.where(
            iota((128, 128), 1) == line, column[128 * line : 128 * line + 128], names
        )
    out_ref[...] = names.T[:PROWS].astype(jnp.int32) - first


def table_kernel(late_ref, early_ref, names_ref, after_ref, out_ref, buf, early, total, sems):
    half = NZ * LATE // 2
    copies = [
        pltpu.make_async_copy(
            late_ref.at[pl.ds(part * half, half), :], buf.at[part], sems.at[part]
        )
        for part in range(2)
    ]
    copies.append(
        pltpu.make_async_copy(early_ref.at[:, pl.ds(0, EARLY), :], early, sems.at[2])
    )
    for copy in copies[::-1]:
        copy.start()
    place = iota((256, 128), 0)

    def picks(first, last):
        return jnp.concatenate(
            [
                (place == names_ref[line : line + 1, :]).astype(F32).astype(BF16)
                for line in range(first, last)
            ],
            axis=1,
        )

    lines = half // 128
    late_picks = [picks(part * lines, (part + 1) * lines) for part in range(2)]
    early_picks = picks(2 * lines, 2 * lines + NZ * EARLY // 128)
    copies[2].wait()
    total[...] = mm(early_picks, early[...].reshape(NZ * EARLY, D))
    copies[0].wait()
    total[...] += mm(late_picks[0], buf[0])
    copies[1].wait()
    outs = []
    for n in range(4):
        cols = slice(256 * n, 256 * n + 256)
        total[:, cols] += mm(late_picks[1], buf[1, :, cols])
        block = pl.ds(256 * n, 256)
        outs.append(
            pltpu.make_async_copy(total.at[:, block], out_ref.at[:, block], sems.at[3 + n])
        )
        outs[-1].start()
    for copy in outs:
        copy.wait()


def square_kernel(mine_ref, other_ref, out_ref):
    total = jnp.zeros((PROWS, PCOLS), F32)
    for sums_ref in (mine_ref, other_ref):
        for i in range(XY):
            part = sums_ref[i].astype(F32)
            total = total + part * part
    mix = jnp.sum(total[:, :512])
    out = jnp.sum(total[:, 512:])
    lane = iota((NZ, 8, 128), 2)
    out_ref[...] = jnp.where(lane == 0, mix, jnp.where(lane == 1, out, 0.0))


def scale_kernel(mine_ref, other_ref, squares_ref, mix_ref, out_ref):
    total = jnp.sum(squares_ref[...], axis=0)[0:1]
    mix_sq, out_sq = total[:, 0:1], total[:, 1:2]
    mix_scale = jnp.minimum(1.0, 1.0 / jnp.sqrt(mix_sq / float(D * 4 * AW) + 1e-06))
    out_scale = jnp.minimum(1.0, 1.0 / jnp.sqrt(out_sq / float(D * AW) + 1e-06))
    core = lax.axis_index("core")
    for side, sums_ref in ((core, mine_ref), (1 - core, other_ref)):
        for p in range(XY):
            sums = sums_ref[p].astype(F32)
            mix, out = sums[:, :512] * mix_scale, sums[:, 512:] * out_scale
            for part in range(2):
                r = p * 8
                c = pl.multiple_of(side * D + part * 512, 512)
                mix_ref[r : r + 8, pl.ds(c, 512)] = mix[8 * part : 8 * part + 8]
                r = (p // 2) * 8
                c = pl.multiple_of(side * AW + (p % 2) * 256 + part * 128, 128)
                out_ref[r : r + 8, pl.ds(c, 128)] = out[8 * part : 8 * part + 8]


def vmem():
    return pl.BlockSpec(memory_space=pltpu.VMEM)


def call(body, outs, args, specs=None, outs_specs=None, **kwargs):
    shapes = [jax.ShapeDtypeStruct(s, t) for s, t in outs]
    one = len(shapes) == 1
    return pl.pallas_call(
        body,
        out_shape=shapes[0] if one else shapes,
        in_specs=specs or [vmem()] * len(args),
        out_specs=outs_specs or (vmem() if one else [vmem()] * len(shapes)),
        **kwargs,
    )(*args)


def cost(us):
    return pl.CostEstimate(flops=0, bytes_accessed=int(us * 3.0e6), transcendentals=0)


def exchange(array, axes):
    return lax.all_to_all(array, axes, split_axis=0, concat_axis=0, tiled=True)


def shards(
    item_table, item_row, item_owner, user_lengths, w_mix, w_out, gain_in, gain_attn, cotangent
):
    anywhere = pl.BlockSpec(memory_space=pl.ANY)
    pinned = pl.BlockSpec(memory_space=pltpu.HBM)
    share = call(share_kernel, [((TOK + 32, D), BF16)], (w_mix, w_out))
    weights = lax.all_gather(share, ("core", "z"), axis=0, tiled=True).reshape(2, NZ, 160, D)

    requests, target = call(
        plan_kernel,
        [((OWNERS, 128), jnp.int32), ((TOK, TOK), jnp.int32)],
        (item_owner.reshape(1, TOK), item_row.reshape(1, TOK)),
    )
    asked = exchange(requests, TABLE)
    wanted = asked[:, :SLOTS].reshape(OWNERS * SLOTS)
    found = item_table.at[wanted].get(mode="promise_in_bounds")
    got = exchange(found.reshape(OWNERS, SLOTS, D), TABLE)

    smem = pl.BlockSpec(memory_space=pltpu.SMEM)
    layer_out, grad_slots, keep, send = call(
        layer_kernel,
        [
            ((TOK, D), BF16),
            ((OWNERS * SLOTS, D), BF16),
            ((TOK, FACT), BF16),
            ((TOK, FACT), BF16),
        ],
        (
            user_lengths,
            got.reshape(OWNERS * SLOTS, D),
            target,
            weights,
            gain_in.reshape(1, D),
            gain_attn.reshape(1, AW),
            cotangent,
        ),
        specs=[smem, vmem(), vmem(), pinned, vmem(), vmem(), vmem()],
        scratch_shapes=[
            pltpu.VMEM((2, NZ, TOK, D), BF16),
            pltpu.VMEM((NZ, 2, 32, D), BF16),
            pltpu.VMEM((2, TOK, D), BF16),
            pltpu.SemaphoreType.DMA((10,)),
        ],
        cost_estimate=cost(9),
        compiler_params=pltpu.CompilerParams(vmem_limit_bytes=32 * MB),
    )

    theirs = lax.ppermute(send, "core", [(0, 1), (1, 0)])
    grads = pl.pallas_call(
        grads_kernel,
        out_shape=jax.ShapeDtypeStruct((NZ, XY, PROWS, PCOLS), BF16),
        in_specs=[vmem(), vmem()],
        out_specs=anywhere,
        scratch_shapes=[
            pltpu.VMEM((NZ, XY, PROWS, PCOLS), BF16),
            pltpu.SemaphoreType.DMA((NZ,)),
        ],
        cost_estimate=cost(3),
        compiler_params=pltpu.CompilerParams(vmem_limit_bytes=30 * MB),
    )(keep, theirs)
    column = lax.psum_scatter(
        grads.reshape(NZ * XY * PROWS, PCOLS), "z", scatter_dimension=0, tiled=True
    )
    received = exchange(grad_slots.reshape(OWNERS, SLOTS, D), TABLE)
    late, early = call(
        pack_kernel,
        [((LATE, D), BF16), ((EARLY + PROWS, D), BF16)],
        (received.reshape(OWNERS * SLOTS, D), asked),
        cost_estimate=cost(2),
        compiler_params=pltpu.CompilerParams(vmem_limit_bytes=16 * MB),
    )
    late = lax.all_gather(late, "z", axis=0, tiled=True)
    early = exchange(jnp.broadcast_to(early[None], (NZ, EARLY + PROWS, D)), "z")
    column, early = lax.optimization_barrier((column, early))
    names = call(
        names_kernel,
        [((PROWS, 128), jnp.int32)],
        (early,),
        cost_estimate=cost(2),
        compiler_params=pltpu.CompilerParams(vmem_limit_bytes=16 * MB),
    )
    plane = exchange(column.reshape(XY, PROWS, PCOLS), ("x", "y"))
    whole = jnp.sum(plane.astype(F32), axis=0).astype(BF16)
    mine = exchange(jnp.broadcast_to(whole[None], (XY, PROWS, PCOLS)), ("x", "y"))
    other = lax.ppermute(mine, "core", [(0, 1), (1, 0)])

    squares = call(
        square_kernel,
        [((NZ, 8, 128), F32)],
        (mine, other),
        cost_estimate=cost(1),
        compiler_params=pltpu.CompilerParams(vmem_limit_bytes=16 * MB),
    )
    squares = exchange(squares, "z")
    mix_grad, out_grad = call(
        scale_kernel,
        [((TOK, 4 * AW), F32), ((64, D), F32)],
        (mine, other, squares),
        cost_estimate=cost(2),
        compiler_params=pltpu.CompilerParams(vmem_limit_bytes=16 * MB),
    )
    table_grad = call(
        table_kernel,
        [((256, D), F32)],
        (late, early, names, out_grad),
        specs=[pinned, pinned, vmem(), anywhere],
        outs_specs=anywhere,
        scratch_shapes=[
            pltpu.VMEM((2, NZ * LATE // 2, D), BF16),
            pltpu.VMEM((NZ, EARLY, D), BF16),
            pltpu.VMEM((256, D), F32),
            pltpu.SemaphoreType.DMA((7,)),
        ],
        cost_estimate=cost(3),
        compiler_params=pltpu.CompilerParams(vmem_limit_bytes=60 * MB),
    )
    return (layer_out, table_grad, mix_grad, out_grad)


def solution(mesh):
    cube = Mesh(mesh.devices.reshape(4, 4, 2, 8), ALL)
    in_specs = (
        P(TABLE, None),
        P(ALL),
        P(ALL, None),
        P(ALL, None),
        P("z", None),
        P("z", None),
        P(),
        P(),
        P(ALL, None),
    )
    out_specs = (
        P(ALL, None),
        P(ALL, None),
        P("z", None),
        P("z", None),
    )
    return jax.shard_map(shards, mesh=cube, in_specs=in_specs, out_specs=out_specs, check_vma=False)
```

```python
import jax
import jax.numpy as jnp
from jax import lax
from jax.experimental import pallas as pl
from jax.experimental.pallas import tpu as pltpu
from jax.sharding import Mesh
from jax.sharding import PartitionSpec as P

H = 4
DH = 128
MAXLEN = 64
TOK = 128
D = 1024
AW = H * DH
OWNERS = 32
CAP = 6
SLOTS = 8
NZ = 8
XY = 16
PROWS = 16
PCOLS = 640
FACT = 3072
USED = OWNERS * CAP
TABLE = ("x", "y", "core")
ALL = ("x", "y", "core", "z")
F32 = jnp.float32
BF16 = jnp.bfloat16
MB = 1024 * 1024


def mm(a, b):
    return lax.dot_general(a, b, (((1,), (0,)), ((), ())), preferred_element_type=F32)


def mm_nt(a, b):
    return lax.dot_general(a, b, (((1,), (1,)), ((), ())), preferred_element_type=F32)


def mm_tn(a, b):
    return lax.dot_general(a, b, (((0,), (0,)), ((), ())), preferred_element_type=F32)


def iota(shape, dim):
    return lax.broadcasted_iota(jnp.int32, shape, dim)


def share_kernel(mix_ref, out_ref, share_ref):
    core = lax.axis_index("core")
    share_ref[:TOK] = mix_ref[:, pl.ds(pl.multiple_of(core * D, D), D)]
    share_ref[TOK:] = out_ref[pl.ds(pl.multiple_of(core * 32, 32), 32), :]


def plan_kernel(owner_ref, row_ref, req_ref, tgt_ref):
    square = (TOK, TOK)
    lane = iota(square, 1)

    def column(values):
        return jnp.broadcast_to(values.astype(F32), square).T

    row = row_ref[...]
    owner = column(owner_ref[...])
    low, high = column(row & 127), column(row >> 7)
    onehot = owner == lane.astype(F32)
    onehot_f = onehot.astype(F32)
    onehot_b = onehot_f.astype(BF16)
    earlier = (lane < iota(square, 0)).astype(F32).astype(BF16)
    before = mm(earlier, onehot_b)
    slot = jnp.sum(before * onehot_f, axis=1, keepdims=True)
    tgt_ref[...] = (owner * SLOTS + slot).astype(jnp.int32)
    here = slot == lane.astype(F32)
    low = jnp.where(here, low, 0.0).astype(BF16)
    high = jnp.where(here, high, 0.0).astype(BF16)
    requests = mm_tn(onehot_b, low) + 128.0 * mm_tn(onehot_b, high)
    req_ref[...] = requests[:OWNERS].astype(jnp.int32)


def layer_kernel(
    lens_ref, got_ref, tgt_ref, weights_ref, gin_ref, gat_ref, ct_ref,
    out_ref, slots_ref, keep_ref, send_ref,
    wm, wo, dmx, sems,
):
    core = lax.axis_index("core")
    copies = []
    for half in range(2):
        for part in range(4):
            z = pl.ds(2 * part, 2)
            copies.append(
                pltpu.make_async_copy(
                    weights_ref.at[half, z, pl.ds(0, TOK), :],
                    wm.at[half, z],
                    sems.at[len(copies)],
                )
            )
    for half in range(2):
        copies.append(
            pltpu.make_async_copy(
                weights_ref.at[half, :, pl.ds(TOK, 32), :], wo.at[:, half], sems.at[len(copies)]
            )
        )
    for copy in copies:
        copy.start()

    pick = (tgt_ref[:, :1] == iota((TOK, OWNERS * SLOTS), 1)).astype(F32).astype(BF16)
    emb = mm(pick, got_ref[...])
    gin = gin_ref[...]
    gat = gat_ref[...]
    centered = emb - jnp.mean(emb, axis=1, keepdims=True)
    rstd = lax.rsqrt(jnp.mean(centered * centered, axis=1, keepdims=True) + 1e-05)
    xhat = centered * rstd
    normed = (xhat * gin).astype(BF16)

    position, other = iota((TOK, TOK), 0), iota((TOK, TOK), 1)
    seg_row = jnp.zeros((TOK, TOK), jnp.int32)
    seg_col = jnp.zeros((TOK, TOK), jnp.int32)
    end = 0
    for user in range(lens_ref.shape[1]):
        end = end + lens_ref[0, user]
        seg_row = seg_row + (position >= end).astype(jnp.int32)
        seg_col = seg_col + (other >= end).astype(jnp.int32)
    allowed = (seg_row == seg_col) & (other <= position)

    mixtures = []
    for half in range(2):
        mixture = jnp.zeros((TOK, D), F32)
        for part in range(4):
            copies[4 * half + part].wait()
            rows = wm[half, 2 * part : 2 * part + 2].reshape(2 * TOK, D)
            mixture = mixture + mm(normed[:, 256 * part : 256 * part + 256], rows)
        mixtures.append(mixture)
    mix0, mix1 = mixtures
    wm0, wm1 = wm[0].reshape(D, D), wm[1].reshape(D, D)

    sig0, sig1 = jax.nn.sigmoid(mix0), jax.nn.sigmoid(mix1)
    act0, act1 = (mix0 * sig0).astype(BF16), (mix1 * sig1).astype(BF16)
    slope0 = sig0 * (1.0 + mix0 * (1.0 - sig0))
    slope1 = sig1 * (1.0 + mix1 * (1.0 - sig1))
    gate_u = act0[:, :AW].astype(F32)

    heads = []
    attended = []
    for h in range(H):
        val = act0[:, AW + h * DH : AW + (h + 1) * DH]
        qry = act1[:, h * DH : (h + 1) * DH]
        key = act1[:, AW + h * DH : AW + (h + 1) * DH]
        score = mm_nt(qry, key) * DH ** (-0.5)
        sig = jax.nn.sigmoid(score)
        wgt = (jnp.where(allowed, score * sig, 0.0) / MAXLEN).astype(BF16)
        attended.append(mm(wgt, val).astype(BF16))
        slope = jnp.where(allowed, sig * (1.0 + score * (1.0 - sig)), 0.0) * (
            DH ** (-0.5) / MAXLEN
        )
        heads.append((val, qry, key, wgt, slope))
    att = jnp.concatenate(attended, axis=1).astype(F32)
    acent = att - jnp.mean(att, axis=1, keepdims=True)
    arstd = lax.rsqrt(jnp.mean(acent * acent, axis=1, keepdims=True) + 1e-05)
    ahat = acent * arstd
    scaled = ahat * gat
    gated = (scaled * gate_u).astype(BF16)

    copies[8].wait()
    copies[9].wait()
    w_out = wo[...].reshape(AW, D)
    ct = ct_ref[...]
    out_ref[...] = (emb + mm(gated, w_out)).astype(BF16)

    d_gated = mm_nt(ct, w_out).astype(BF16).astype(F32)
    d_gate = (d_gated * scaled).astype(BF16).astype(F32)
    d_ahat = d_gated * gate_u * gat
    d_att = arstd * (
        d_ahat
        - jnp.mean(d_ahat, axis=1, keepdims=True)
        - ahat * jnp.mean(d_ahat * ahat, axis=1, keepdims=True)
    )
    d_att = d_att.astype(BF16)
    d_val, d_qry, d_key = [], [], []
    for h in range(H):
        val, qry, key, wgt, slope = heads[h]
        d_head = d_att[:, h * DH : (h + 1) * DH]
        d_wgt = mm_nt(d_head, val).astype(BF16).astype(F32)
        d_val.append(mm_tn(wgt, d_head).astype(BF16))
        d_score = (d_wgt * slope).astype(BF16)
        d_qry.append(mm(d_score, key).astype(BF16))
        d_key.append(mm_tn(d_score, qry).astype(BF16))
    d_act0 = jnp.concatenate([d_gate] + [v.astype(F32) for v in d_val], axis=1)
    d_act1 = jnp.concatenate([v.astype(F32) for v in d_qry + d_key], axis=1)
    d_mix0 = (d_act0 * slope0).astype(BF16)
    d_mix1 = (d_act1 * slope1).astype(BF16)
    dmx[0] = d_mix0
    dmx[1] = d_mix1
    d_normed = (mm_nt(d_mix0, wm0) + mm_nt(d_mix1, wm1)).astype(BF16).astype(F32)
    d_xhat = d_normed * gin
    d_emb = (
        rstd
        * (
            d_xhat
            - jnp.mean(d_xhat, axis=1, keepdims=True)
            - xhat * jnp.mean(d_xhat * xhat, axis=1, keepdims=True)
        )
        + ct.astype(F32)
    ).astype(BF16)
    slots_ref[...] = mm_tn(pick, d_emb).astype(BF16)
    for side, dst in ((1 - core, send_ref), (core, keep_ref)):
        dst[:, 0:1024] = normed
        dst[:, 1024:2048] = dmx[side]
        dst[:, 2048:2560] = gated
        dst[:, 2560:FACT] = ct_ref[:, pl.ds(pl.multiple_of(side * AW, AW), AW)]


def grads_kernel(keep_ref, theirs_ref, mix_ref, out_ref, mix, out, sems):
    def both(first, last):
        return jnp.concatenate([keep_ref[:, first:last], theirs_ref[:, first:last]], axis=0)

    copies = []
    d_mix = both(1024, 2048)
    for z in range(NZ):
        grad = mm_tn(both(z * TOK, (z + 1) * TOK), d_mix)
        for p in range(XY):
            part = grad[8 * p : 8 * p + 8]
            mix[z, p] = jnp.concatenate([part[:, :512], part[:, 512:]], axis=0).astype(BF16)
        copies.append(pltpu.make_async_copy(mix.at[z], mix_ref.at[z], sems.at[z]))
        copies[-1].start()

    grad = mm_tn(both(2048, 2560), both(2560, FACT))
    for z in range(NZ):
        for p in range(XY):
            r, c = z * 64 + (p // 2) * 8, (p % 2) * 256
            part = grad[r : r + 8, c : c + 256]
            out[p, z * PROWS : (z + 1) * PROWS] = jnp.concatenate(
                [part[:, :128], part[:, 128:]], axis=0
            ).astype(BF16)
    copies.append(pltpu.make_async_copy(out, out_ref, sems.at[NZ]))
    copies[-1].start()
    for copy in copies:
        copy.wait()


def column_kernel(plane_ref, asked_ref, out_ref):
    total = jnp.sum(plane_ref[...].astype(F32), axis=0).astype(BF16)
    asked = asked_ref[...]
    low, high = ((part).astype(F32).astype(BF16) for part in (asked & 127, asked >> 7))
    for z in range(NZ):
        out_ref[z, :PROWS] = total[z * PROWS : (z + 1) * PROWS]
        out_ref[z, PROWS : PROWS + OWNERS] = low
        out_ref[z, PROWS + OWNERS :] = high


def pack_kernel(rows_ref, out_ref):
    r, k = iota((USED, OWNERS * SLOTS), 0), iota((USED, OWNERS * SLOTS), 1)
    take = (r // CAP) * SLOTS + r % CAP == k
    out_ref[...] = mm(take.astype(F32).astype(BF16), rows_ref[...]).astype(BF16)


def names_kernel(column_ref, out_ref):
    first = lax.axis_index("z") * 256
    count = NZ * USED
    low = column_ref[:, PROWS : PROWS + OWNERS].reshape(NZ * OWNERS, 128)
    high = column_ref[:, PROWS + OWNERS :].reshape(NZ * OWNERS, 128)
    row, col = iota((count, NZ * OWNERS), 0), iota((count, NZ * OWNERS), 1)
    owner = (row // CAP == col).astype(F32).astype(BF16)
    lane = iota((count, 128), 1)
    spread = mm(owner, low) + 128.0 * mm(owner, high)
    column = jnp.sum(
        jnp.where(iota((count, 128), 0) % CAP == lane, spread, 0.0), axis=1, keepdims=True
    )
    names = jnp.zeros((128, 128), F32)
    for line in range(count // 128):
        names = jnp.where(
            iota((128, 128), 1) == line, column[128 * line : 128 * line + 128], names
        )
    out_ref[...] = names.T[:PROWS].astype(jnp.int32) - first


def table_kernel(rows_ref, names_ref, after_ref, out_ref, buf, total, sems):
    half = NZ * USED // 2
    copies = [
        pltpu.make_async_copy(
            rows_ref.at[pl.ds(part * half, half), :], buf.at[part], sems.at[part]
        )
        for part in range(2)
    ]
    for copy in copies:
        copy.start()
    place = iota((256, 128), 0)
    lines = half // 128
    picks = [
        jnp.concatenate(
            [
                (place == names_ref[line : line + 1, :]).astype(F32).astype(BF16)
                for line in range(part * lines, (part + 1) * lines)
            ],
            axis=1,
        )
        for part in range(2)
    ]
    copies[0].wait()
    total[...] = mm(picks[0], buf[0])
    copies[1].wait()
    outs = []
    for n in range(4):
        cols = slice(256 * n, 256 * n + 256)
        total[:, cols] += mm(picks[1], buf[1, :, cols])
        block = pl.ds(256 * n, 256)
        outs.append(
            pltpu.make_async_copy(total.at[:, block], out_ref.at[:, block], sems.at[2 + n])
        )
        outs[-1].start()
    for copy in outs:
        copy.wait()


def square_kernel(mine_ref, other_ref, out_ref):
    total = jnp.zeros((PROWS, PCOLS), F32)
    for sums_ref in (mine_ref, other_ref):
        for i in range(XY):
            part = sums_ref[i].astype(F32)
            total = total + part * part
    mix = jnp.sum(total[:, :512])
    out = jnp.sum(total[:, 512:])
    lane = iota((NZ, 8, 128), 2)
    out_ref[...] = jnp.where(lane == 0, mix, jnp.where(lane == 1, out, 0.0))


def scale_kernel(mine_ref, other_ref, squares_ref, mix_ref, out_ref):
    total = jnp.sum(squares_ref[...], axis=0)[0:1]
    mix_sq, out_sq = total[:, 0:1], total[:, 1:2]
    mix_scale = jnp.minimum(1.0, 1.0 / jnp.sqrt(mix_sq / float(D * 4 * AW) + 1e-06))
    out_scale = jnp.minimum(1.0, 1.0 / jnp.sqrt(out_sq / float(D * AW) + 1e-06))
    core = lax.axis_index("core")
    for side, sums_ref in ((core, mine_ref), (1 - core, other_ref)):
        for p in range(XY):
            sums = sums_ref[p].astype(F32)
            mix, out = sums[:, :512] * mix_scale, sums[:, 512:] * out_scale
            for part in range(2):
                r = p * 8
                c = pl.multiple_of(side * D + part * 512, 512)
                mix_ref[r : r + 8, pl.ds(c, 512)] = mix[8 * part : 8 * part + 8]
                r = (p // 2) * 8
                c = pl.multiple_of(side * AW + (p % 2) * 256 + part * 128, 128)
                out_ref[r : r + 8, pl.ds(c, 128)] = out[8 * part : 8 * part + 8]


def vmem():
    return pl.BlockSpec(memory_space=pltpu.VMEM)


def call(body, outs, args, specs=None, outs_specs=None, **kwargs):
    shapes = [jax.ShapeDtypeStruct(s, t) for s, t in outs]
    one = len(shapes) == 1
    return pl.pallas_call(
        body,
        out_shape=shapes[0] if one else shapes,
        in_specs=specs or [vmem()] * len(args),
        out_specs=outs_specs or (vmem() if one else [vmem()] * len(shapes)),
        **kwargs,
    )(*args)


def cost(us):
    return pl.CostEstimate(flops=0, bytes_accessed=int(us * 3.0e6), transcendentals=0)


def exchange(array, axes):
    return lax.all_to_all(array, axes, split_axis=0, concat_axis=0, tiled=True)


def shards(
    item_table, item_row, item_owner, user_lengths, w_mix, w_out, gain_in, gain_attn, cotangent
):
    anywhere = pl.BlockSpec(memory_space=pl.ANY)
    pinned = pl.BlockSpec(memory_space=pltpu.HBM)
    share = call(share_kernel, [((TOK + 32, D), BF16)], (w_mix, w_out))
    weights = lax.all_gather(share, ("core", "z"), axis=0, tiled=True).reshape(2, NZ, 160, D)

    requests, target = call(
        plan_kernel,
        [((OWNERS, 128), jnp.int32), ((TOK, TOK), jnp.int32)],
        (item_owner.reshape(1, TOK), item_row.reshape(1, TOK)),
    )
    asked = exchange(requests, TABLE)
    wanted = asked[:, :SLOTS].reshape(OWNERS * SLOTS)
    found = item_table.at[wanted].get(mode="promise_in_bounds")
    got = exchange(found.reshape(OWNERS, SLOTS, D), TABLE)

    smem = pl.BlockSpec(memory_space=pltpu.SMEM)
    layer_out, grad_slots, keep, send = call(
        layer_kernel,
        [
            ((TOK, D), BF16),
            ((OWNERS * SLOTS, D), BF16),
            ((TOK, FACT), BF16),
            ((TOK, FACT), BF16),
        ],
        (
            user_lengths,
            got.reshape(OWNERS * SLOTS, D),
            target,
            weights,
            gain_in.reshape(1, D),
            gain_attn.reshape(1, AW),
            cotangent,
        ),
        specs=[smem, vmem(), vmem(), pinned, vmem(), vmem(), vmem()],
        scratch_shapes=[
            pltpu.VMEM((2, NZ, TOK, D), BF16),
            pltpu.VMEM((NZ, 2, 32, D), BF16),
            pltpu.VMEM((2, TOK, D), BF16),
            pltpu.SemaphoreType.DMA((10,)),
        ],
        cost_estimate=cost(9),
        compiler_params=pltpu.CompilerParams(vmem_limit_bytes=32 * MB),
    )

    theirs = lax.ppermute(send, "core", [(0, 1), (1, 0)])
    mix_part, out_part = call(
        grads_kernel,
        [((NZ, XY, PROWS, 512), BF16), ((XY, NZ * PROWS, 128), BF16)],
        (keep, theirs),
        outs_specs=[anywhere, anywhere],
        scratch_shapes=[
            pltpu.VMEM((NZ, XY, PROWS, 512), BF16),
            pltpu.VMEM((XY, NZ * PROWS, 128), BF16),
            pltpu.SemaphoreType.DMA((NZ + 1,)),
        ],
        cost_estimate=cost(3),
        compiler_params=pltpu.CompilerParams(vmem_limit_bytes=30 * MB),
    )
    mix_column = lax.psum_scatter(
        mix_part.reshape(NZ * XY * PROWS, 512), "z", scatter_dimension=0, tiled=True
    )

    received = exchange(grad_slots.reshape(OWNERS, SLOTS, D), TABLE)
    packed = call(
        pack_kernel,
        [((USED, D), BF16)],
        (received.reshape(OWNERS * SLOTS, D),),
        cost_estimate=cost(2),
        compiler_params=pltpu.CompilerParams(vmem_limit_bytes=16 * MB),
    )
    out_part, packed = lax.optimization_barrier((out_part, packed))
    gathered = lax.all_gather(packed, "z", axis=0, tiled=True)

    out_column = call(
        column_kernel,
        [((NZ, PROWS + 2 * OWNERS, 128), BF16)],
        (exchange(out_part, ("x", "y")), asked),
        cost_estimate=cost(1),
        compiler_params=pltpu.CompilerParams(vmem_limit_bytes=16 * MB),
    )
    out_column = exchange(out_column, "z")
    mix_column, out_column = lax.optimization_barrier((mix_column, out_column))
    names = call(
        names_kernel,
        [((PROWS, 128), jnp.int32)],
        (out_column,),
        cost_estimate=cost(2),
        compiler_params=pltpu.CompilerParams(vmem_limit_bytes=16 * MB),
    )
    mix_plane = exchange(mix_column.reshape(XY, PROWS, 512), ("x", "y"))
    whole = jnp.concatenate(
        [
            jnp.sum(mix_plane.astype(F32), axis=0),
            jnp.sum(out_column[:, :PROWS].astype(F32), axis=0),
        ],
        axis=1,
    ).astype(BF16)
    mine = exchange(jnp.broadcast_to(whole[None], (XY, PROWS, PCOLS)), ("x", "y"))
    other = lax.ppermute(mine, "core", [(0, 1), (1, 0)])

    squares = call(
        square_kernel,
        [((NZ, 8, 128), F32)],
        (mine, other),
        cost_estimate=cost(1),
        compiler_params=pltpu.CompilerParams(vmem_limit_bytes=16 * MB),
    )
    squares = exchange(squares, "z")
    mix_grad, out_grad = call(
        scale_kernel,
        [((TOK, 4 * AW), F32), ((64, D), F32)],
        (mine, other, squares),
        cost_estimate=cost(2),
        compiler_params=pltpu.CompilerParams(vmem_limit_bytes=16 * MB),
    )
    table_grad = call(
        table_kernel,
        [((256, D), F32)],
        (gathered, names, out_grad),
        specs=[pinned, vmem(), anywhere],
        outs_specs=anywhere,
        scratch_shapes=[
            pltpu.VMEM((2, NZ * USED // 2, D), BF16),
            pltpu.VMEM((256, D), F32),
            pltpu.SemaphoreType.DMA((6,)),
        ],
        cost_estimate=cost(3),
        compiler_params=pltpu.CompilerParams(vmem_limit_bytes=60 * MB),
    )
    return (layer_out, table_grad, mix_grad, out_grad)


def solution(mesh):
    cube = Mesh(mesh.devices.reshape(4, 4, 2, 8), ALL)
    in_specs = (
        P(TABLE, None),
        P(ALL),
        P(ALL, None),
        P(ALL, None),
        P("z", None),
        P("z", None),
        P(),
        P(),
        P(ALL, None),
    )
    out_specs = (
        P(ALL, None),
        P(ALL, None),
        P("z", None),
        P("z", None),
    )
    return jax.shard_map(shards, mesh=cube, in_specs=in_specs, out_specs=out_specs, check_vma=False)
```

```python
import jax
import jax.numpy as jnp
from jax import lax
from jax.experimental import pallas as pl
from jax.experimental.pallas import tpu as pltpu
from jax.sharding import Mesh
from jax.sharding import PartitionSpec as P

H = 4
DH = 128
MAXLEN = 64
TOK = 128
D = 1024
AW = H * DH
OWNERS = 32
CAP = 6
SLOTS = 8
NZ = 8
XY = 16
PROWS = 16
PCOLS = 640
FACT = 3072
USED = OWNERS * CAP
TABLE = ("x", "y", "core")
ALL = ("x", "y", "core", "z")
F32 = jnp.float32
BF16 = jnp.bfloat16
MB = 1024 * 1024


def mm(a, b):
    return lax.dot_general(a, b, (((1,), (0,)), ((), ())), preferred_element_type=F32)


def mm_nt(a, b):
    return lax.dot_general(a, b, (((1,), (1,)), ((), ())), preferred_element_type=F32)


def mm_tn(a, b):
    return lax.dot_general(a, b, (((0,), (0,)), ((), ())), preferred_element_type=F32)


def iota(shape, dim):
    return lax.broadcasted_iota(jnp.int32, shape, dim)


def share_kernel(mix_ref, out_ref, share_ref):
    core = lax.axis_index("core")
    share_ref[:TOK] = mix_ref[:, pl.ds(pl.multiple_of(core * D, D), D)]
    share_ref[TOK:] = out_ref[pl.ds(pl.multiple_of(core * 32, 32), 32), :]


def plan_kernel(owner_ref, row_ref, req_ref, tgt_ref):
    square = (TOK, TOK)
    lane = iota(square, 1)

    def column(values):
        return jnp.broadcast_to(values.astype(F32), square).T

    row = row_ref[...]
    owner = column(owner_ref[...])
    low, high = column(row & 127), column(row >> 7)
    onehot = owner == lane.astype(F32)
    onehot_f = onehot.astype(F32)
    onehot_b = onehot_f.astype(BF16)
    earlier = (lane < iota(square, 0)).astype(F32).astype(BF16)
    before = mm(earlier, onehot_b)
    slot = jnp.sum(before * onehot_f, axis=1, keepdims=True)
    tgt_ref[...] = (owner * SLOTS + slot).astype(jnp.int32)
    here = slot == lane.astype(F32)
    low = jnp.where(here, low, 0.0).astype(BF16)
    high = jnp.where(here, high, 0.0).astype(BF16)
    requests = mm_tn(onehot_b, low) + 128.0 * mm_tn(onehot_b, high)
    req_ref[...] = requests[:OWNERS].astype(jnp.int32)


def chosen(tgt_ref):
    return (tgt_ref[:, :1] == iota((TOK, OWNERS * SLOTS), 1)).astype(F32).astype(BF16)


def layer_kernel(
    lens_ref, got_ref, tgt_ref, weights_ref, gin_ref, gat_ref, ct_ref,
    out_ref, keep_ref, send_ref, dmx, xhat_ref, rstd_ref,
):
    core = lax.axis_index("core")
    emb = mm(chosen(tgt_ref), got_ref[...])
    gin = gin_ref[...]
    gat = gat_ref[...]
    centered = emb - jnp.mean(emb, axis=1, keepdims=True)
    rstd = lax.rsqrt(jnp.mean(centered * centered, axis=1, keepdims=True) + 1e-05)
    xhat = centered * rstd
    normed = (xhat * gin).astype(BF16)

    position, other = iota((TOK, TOK), 0), iota((TOK, TOK), 1)
    seg_row = jnp.zeros((TOK, TOK), jnp.int32)
    seg_col = jnp.zeros((TOK, TOK), jnp.int32)
    end = 0
    for user in range(lens_ref.shape[1]):
        end = end + lens_ref[0, user]
        seg_row = seg_row + (position >= end).astype(jnp.int32)
        seg_col = seg_col + (other >= end).astype(jnp.int32)
    allowed = (seg_row == seg_col) & (other <= position)

    mix0, mix1 = (
        mm(normed, weights_ref[half, :, :TOK, :].reshape(D, D)) for half in range(2)
    )

    sig0, sig1 = jax.nn.sigmoid(mix0), jax.nn.sigmoid(mix1)
    act0, act1 = (mix0 * sig0).astype(BF16), (mix1 * sig1).astype(BF16)
    slope0 = sig0 * (1.0 + mix0 * (1.0 - sig0))
    slope1 = sig1 * (1.0 + mix1 * (1.0 - sig1))
    gate_u = act0[:, :AW].astype(F32)

    heads = []
    attended = []
    for h in range(H):
        val = act0[:, AW + h * DH : AW + (h + 1) * DH]
        qry = act1[:, h * DH : (h + 1) * DH]
        key = act1[:, AW + h * DH : AW + (h + 1) * DH]
        score = mm_nt(qry, key) * DH ** (-0.5)
        sig = jax.nn.sigmoid(score)
        wgt = (jnp.where(allowed, score * sig, 0.0) / MAXLEN).astype(BF16)
        attended.append(mm(wgt, val).astype(BF16))
        slope = jnp.where(allowed, sig * (1.0 + score * (1.0 - sig)), 0.0) * (
            DH ** (-0.5) / MAXLEN
        )
        heads.append((val, qry, key, wgt, slope))
    att = jnp.concatenate(attended, axis=1).astype(F32)
    acent = att - jnp.mean(att, axis=1, keepdims=True)
    arstd = lax.rsqrt(jnp.mean(acent * acent, axis=1, keepdims=True) + 1e-05)
    ahat = acent * arstd
    scaled = ahat * gat
    gated = (scaled * gate_u).astype(BF16)

    w_out = jnp.stack([weights_ref[half, :, TOK:, :] for half in range(2)], axis=1)
    w_out = w_out.reshape(AW, D)
    ct = ct_ref[...]
    out_ref[...] = (emb + mm(gated, w_out)).astype(BF16)

    d_gated = mm_nt(ct, w_out).astype(BF16).astype(F32)
    d_gate = (d_gated * scaled).astype(BF16).astype(F32)
    d_ahat = d_gated * gate_u * gat
    d_att = arstd * (
        d_ahat
        - jnp.mean(d_ahat, axis=1, keepdims=True)
        - ahat * jnp.mean(d_ahat * ahat, axis=1, keepdims=True)
    )
    d_att = d_att.astype(BF16)
    d_val, d_qry, d_key = [], [], []
    for h in range(H):
        val, qry, key, wgt, slope = heads[h]
        d_head = d_att[:, h * DH : (h + 1) * DH]
        d_wgt = mm_nt(d_head, val).astype(BF16).astype(F32)
        d_val.append(mm_tn(wgt, d_head).astype(BF16))
        d_score = (d_wgt * slope).astype(BF16)
        d_qry.append(mm(d_score, key).astype(BF16))
        d_key.append(mm_tn(d_score, qry).astype(BF16))
    d_act0 = jnp.concatenate([d_gate] + [v.astype(F32) for v in d_val], axis=1)
    d_act1 = jnp.concatenate([v.astype(F32) for v in d_qry + d_key], axis=1)
    d_mix0 = (d_act0 * slope0).astype(BF16)
    d_mix1 = (d_act1 * slope1).astype(BF16)
    dmx[0] = d_mix0
    dmx[1] = d_mix1
    xhat_ref[...] = xhat
    rstd_ref[...] = jnp.broadcast_to(rstd, (TOK, TOK))
    for side, dst in ((1 - core, send_ref), (core, keep_ref)):
        dst[:, 0:1024] = normed
        dst[:, 1024:2048] = dmx[side]
        dst[:, 2048:2560] = gated
        dst[:, 2560:FACT] = ct_ref[:, pl.ds(pl.multiple_of(side * AW, AW), AW)]


def rows_kernel(tgt_ref, weights_ref, gin_ref, ct_ref, dmx, xhat_ref, rstd_ref, slots_ref):
    d_normed = mm_nt(dmx[0], weights_ref[0, :, :TOK, :].reshape(D, D))
    d_normed = d_normed + mm_nt(dmx[1], weights_ref[1, :, :TOK, :].reshape(D, D))
    d_xhat = d_normed.astype(BF16).astype(F32) * gin_ref[...]
    xhat = xhat_ref[...]
    d_emb = (
        rstd_ref[:, :1]
        * (
            d_xhat
            - jnp.mean(d_xhat, axis=1, keepdims=True)
            - xhat * jnp.mean(d_xhat * xhat, axis=1, keepdims=True)
        )
        + ct_ref[...].astype(F32)
    ).astype(BF16)
    slots_ref[...] = mm_tn(chosen(tgt_ref), d_emb).astype(BF16)


def grads_kernel(keep_ref, theirs_ref, out_ref, buf, sems):
    def both(first, last):
        return jnp.concatenate([keep_ref[:, first:last], theirs_ref[:, first:last]], axis=0)

    grad = mm_tn(both(2048, 2560), both(2560, FACT))
    for z in range(NZ):
        for p in range(XY):
            r, c = z * 64 + (p // 2) * 8, (p % 2) * 256
            part = grad[r : r + 8, c : c + 256]
            buf[z, p, :, 512:PCOLS] = jnp.concatenate(
                [part[:, :128], part[:, 128:]], axis=0
            ).astype(BF16)

    copies = []
    d_mix = both(1024, 2048)
    for z in range(NZ):
        grad = mm_tn(both(z * TOK, (z + 1) * TOK), d_mix)
        for p in range(XY):
            part = grad[8 * p : 8 * p + 8]
            buf[z, p, :, 0:512] = jnp.concatenate(
                [part[:, :512], part[:, 512:]], axis=0
            ).astype(BF16)
        copies.append(pltpu.make_async_copy(buf.at[z], out_ref.at[z], sems.at[z]))
        copies[-1].start()
    for copy in copies:
        copy.wait()


def pack_kernel(rows_ref, out_ref):
    r, k = iota((USED, OWNERS * SLOTS), 0), iota((USED, OWNERS * SLOTS), 1)
    take = (r // CAP) * SLOTS + r % CAP == k
    out_ref[...] = mm(take.astype(F32).astype(BF16), rows_ref[...]).astype(BF16)


def names_kernel(asked_ref, out_ref):
    first = lax.axis_index("z") * 256
    count = NZ * USED
    asked = asked_ref[...].reshape(NZ * OWNERS, 128)
    low, high = (part.astype(F32).astype(BF16) for part in (asked & 127, asked >> 7))
    row, col = iota((count, NZ * OWNERS), 0), iota((count, NZ * OWNERS), 1)
    owner = (row // CAP == col).astype(F32).astype(BF16)
    lane = iota((count, 128), 1)
    spread = mm(owner, low) + 128.0 * mm(owner, high)
    column = jnp.sum(
        jnp.where(iota((count, 128), 0) % CAP == lane, spread, 0.0), axis=1, keepdims=True
    )
    names = jnp.zeros((128, 128), F32)
    for line in range(count // 128):
        names = jnp.where(
            iota((128, 128), 1) == line, column[128 * line : 128 * line + 128], names
        )
    out_ref[...] = names.T[:PROWS].astype(jnp.int32) - first


def table_kernel(rows_ref, names_ref, after_ref, out_ref, buf, total, sems):
    half = NZ * USED // 2
    copies = [
        pltpu.make_async_copy(
            rows_ref.at[pl.ds(part * half, half), :], buf.at[part], sems.at[part]
        )
        for part in range(2)
    ]
    for copy in copies:
        copy.start()
    place = iota((256, 128), 0)
    lines = half // 128
    picks = [
        jnp.concatenate(
            [
                (place == names_ref[line : line + 1, :]).astype(F32).astype(BF16)
                for line in range(part * lines, (part + 1) * lines)
            ],
            axis=1,
        )
        for part in range(2)
    ]
    copies[0].wait()
    total[...] = mm(picks[0], buf[0])
    copies[1].wait()
    outs = []
    for n in range(4):
        cols = slice(256 * n, 256 * n + 256)
        total[:, cols] += mm(picks[1], buf[1, :, cols])
        block = pl.ds(256 * n, 256)
        outs.append(
            pltpu.make_async_copy(total.at[:, block], out_ref.at[:, block], sems.at[2 + n])
        )
        outs[-1].start()
    for copy in outs:
        copy.wait()


def square_kernel(mine_ref, other_ref, out_ref):
    total = jnp.zeros((PROWS, PCOLS), F32)
    for sums_ref in (mine_ref, other_ref):
        for i in range(XY):
            part = sums_ref[i].astype(F32)
            total = total + part * part
    mix = jnp.sum(total[:, :512])
    out = jnp.sum(total[:, 512:])
    lane = iota((NZ, 8, 128), 2)
    out_ref[...] = jnp.where(lane == 0, mix, jnp.where(lane == 1, out, 0.0))


def scale_kernel(mine_ref, other_ref, squares_ref, mix_ref, out_ref):
    total = jnp.sum(squares_ref[...], axis=0)[0:1]
    mix_sq, out_sq = total[:, 0:1], total[:, 1:2]
    mix_scale = jnp.minimum(1.0, 1.0 / jnp.sqrt(mix_sq / float(D * 4 * AW) + 1e-06))
    out_scale = jnp.minimum(1.0, 1.0 / jnp.sqrt(out_sq / float(D * AW) + 1e-06))
    core = lax.axis_index("core")
    for side, sums_ref in ((core, mine_ref), (1 - core, other_ref)):
        for p in range(XY):
            sums = sums_ref[p].astype(F32)
            mix, out = sums[:, :512] * mix_scale, sums[:, 512:] * out_scale
            for part in range(2):
                r = p * 8
                c = pl.multiple_of(side * D + part * 512, 512)
                mix_ref[r : r + 8, pl.ds(c, 512)] = mix[8 * part : 8 * part + 8]
                r = (p // 2) * 8
                c = pl.multiple_of(side * AW + (p % 2) * 256 + part * 128, 128)
                out_ref[r : r + 8, pl.ds(c, 128)] = out[8 * part : 8 * part + 8]


def vmem():
    return pl.BlockSpec(memory_space=pltpu.VMEM)


def call(body, outs, args, specs=None, outs_specs=None, **kwargs):
    shapes = [jax.ShapeDtypeStruct(s, t) for s, t in outs]
    one = len(shapes) == 1
    return pl.pallas_call(
        body,
        out_shape=shapes[0] if one else shapes,
        in_specs=specs or [vmem()] * len(args),
        out_specs=outs_specs or (vmem() if one else [vmem()] * len(shapes)),
        **kwargs,
    )(*args)


def cost(us):
    return pl.CostEstimate(flops=0, bytes_accessed=int(us * 3.0e6), transcendentals=0)


def exchange(array, axes):
    return lax.all_to_all(array, axes, split_axis=0, concat_axis=0, tiled=True)


def shards(
    item_table, item_row, item_owner, user_lengths, w_mix, w_out, gain_in, gain_attn, cotangent
):
    anywhere = pl.BlockSpec(memory_space=pl.ANY)
    pinned = pl.BlockSpec(memory_space=pltpu.HBM)
    share = call(share_kernel, [((TOK + 32, D), BF16)], (w_mix, w_out))
    weights = lax.all_gather(share, ("core", "z"), axis=0, tiled=True).reshape(2, NZ, 160, D)

    requests, target = call(
        plan_kernel,
        [((OWNERS, 128), jnp.int32), ((TOK, TOK), jnp.int32)],
        (item_owner.reshape(1, TOK), item_row.reshape(1, TOK)),
    )
    asked = exchange(requests, TABLE)
    wanted = asked[:, :SLOTS].reshape(OWNERS * SLOTS)
    found = item_table.at[wanted].get(mode="promise_in_bounds")
    got = exchange(found.reshape(OWNERS, SLOTS, D), TABLE)

    smem = pl.BlockSpec(memory_space=pltpu.SMEM)
    gin = gain_in.reshape(1, D)
    layer_out, keep, send, d_mix, xhat, rstd = call(
        layer_kernel,
        [
            ((TOK, D), BF16),
            ((TOK, FACT), BF16),
            ((TOK, FACT), BF16),
            ((2, TOK, D), BF16),
            ((TOK, D), F32),
            ((TOK, TOK), F32),
        ],
        (
            user_lengths,
            got.reshape(OWNERS * SLOTS, D),
            target,
            weights,
            gin,
            gain_attn.reshape(1, AW),
            cotangent,
        ),
        specs=[smem] + [vmem()] * 6,
        cost_estimate=cost(7),
        compiler_params=pltpu.CompilerParams(vmem_limit_bytes=32 * MB),
    )

    theirs = lax.ppermute(send, "core", [(0, 1), (1, 0)])
    grads = call(
        grads_kernel,
        [((NZ, XY, PROWS, PCOLS), BF16)],
        (keep, theirs),
        outs_specs=anywhere,
        scratch_shapes=[
            pltpu.VMEM((NZ, XY, PROWS, PCOLS), BF16),
            pltpu.SemaphoreType.DMA((NZ,)),
        ],
        cost_estimate=cost(3),
        compiler_params=pltpu.CompilerParams(vmem_limit_bytes=30 * MB),
    )
    grads, d_mix = lax.optimization_barrier((grads, d_mix))
    column = lax.psum_scatter(
        grads.reshape(NZ * XY * PROWS, PCOLS), "z", scatter_dimension=0, tiled=True
    )

    grad_slots = call(
        rows_kernel,
        [((OWNERS * SLOTS, D), BF16)],
        (target, weights, gin, cotangent, d_mix, xhat, rstd),
        cost_estimate=cost(3),
        compiler_params=pltpu.CompilerParams(vmem_limit_bytes=32 * MB),
    )
    received = exchange(grad_slots.reshape(OWNERS, SLOTS, D), TABLE)
    packed = call(
        pack_kernel,
        [((USED, D), BF16)],
        (received.reshape(OWNERS * SLOTS, D),),
        cost_estimate=cost(2),
        compiler_params=pltpu.CompilerParams(vmem_limit_bytes=16 * MB),
    )
    asked, packed = lax.optimization_barrier((asked, packed))
    gathered = lax.all_gather(packed, "z", axis=0, tiled=True)
    asked = exchange(jnp.broadcast_to(asked[None], (NZ, OWNERS, 128)), "z")
    names = call(
        names_kernel,
        [((PROWS, 128), jnp.int32)],
        (asked,),
        cost_estimate=cost(2),
        compiler_params=pltpu.CompilerParams(vmem_limit_bytes=16 * MB),
    )
    column, names = lax.optimization_barrier((column, names))
    plane = exchange(column.reshape(XY, PROWS, PCOLS), ("x", "y"))
    whole = jnp.sum(plane.astype(F32), axis=0).astype(BF16)
    mine = exchange(jnp.broadcast_to(whole[None], (XY, PROWS, PCOLS)), ("x", "y"))
    other = lax.ppermute(mine, "core", [(0, 1), (1, 0)])

    squares = call(
        square_kernel,
        [((NZ, 8, 128), F32)],
        (mine, other),
        cost_estimate=cost(1),
        compiler_params=pltpu.CompilerParams(vmem_limit_bytes=16 * MB),
    )
    squares = exchange(squares, "z")
    mix_grad, out_grad = call(
        scale_kernel,
        [((TOK, 4 * AW), F32), ((64, D), F32)],
        (mine, other, squares),
        cost_estimate=cost(2),
        compiler_params=pltpu.CompilerParams(vmem_limit_bytes=16 * MB),
    )
    table_grad = call(
        table_kernel,
        [((256, D), F32)],
        (gathered, names, out_grad),
        specs=[pinned, vmem(), anywhere],
        outs_specs=anywhere,
        scratch_shapes=[
            pltpu.VMEM((2, NZ * USED // 2, D), BF16),
            pltpu.VMEM((256, D), F32),
            pltpu.SemaphoreType.DMA((6,)),
        ],
        cost_estimate=cost(3),
        compiler_params=pltpu.CompilerParams(vmem_limit_bytes=60 * MB),
    )
    return (layer_out, table_grad, mix_grad, out_grad)


def solution(mesh):
    cube = Mesh(mesh.devices.reshape(4, 4, 2, 8), ALL)
    in_specs = (
        P(TABLE, None),
        P(ALL),
        P(ALL, None),
        P(ALL, None),
        P("z", None),
        P("z", None),
        P(),
        P(),
        P(ALL, None),
    )
    out_specs = (
        P(ALL, None),
        P(ALL, None),
        P("z", None),
        P("z", None),
    )
    return jax.shard_map(shards, mesh=cube, in_specs=in_specs, out_specs=out_specs, check_vma=False)
```

```python
import jax
import jax.numpy as jnp
from jax import lax
from jax.experimental import pallas as pl
from jax.experimental.pallas import tpu as pltpu
from jax.sharding import Mesh
from jax.sharding import PartitionSpec as P

H = 4
DH = 128
MAXLEN = 64
TOK = 128
D = 1024
AW = H * DH
OWNERS = 32
CAP = 6
SLOTS = 8
NZ = 8
XY = 16
PROWS = 16
PCOLS = 640
FACT = 3072
USED = OWNERS * CAP
TABLE = ("x", "y", "core")
ALL = ("x", "y", "core", "z")
F32 = jnp.float32
BF16 = jnp.bfloat16
MB = 1024 * 1024


def mm(a, b):
    return lax.dot_general(a, b, (((1,), (0,)), ((), ())), preferred_element_type=F32)


def mm_nt(a, b):
    return lax.dot_general(a, b, (((1,), (1,)), ((), ())), preferred_element_type=F32)


def mm_tn(a, b):
    return lax.dot_general(a, b, (((0,), (0,)), ((), ())), preferred_element_type=F32)


def iota(shape, dim):
    return lax.broadcasted_iota(jnp.int32, shape, dim)


def share_kernel(mix_ref, out_ref, share_ref, buf, sems):
    core = lax.axis_index("core")
    parts = (
        (mix_ref.at[:, pl.ds(pl.multiple_of(core * D, D), D)], pl.ds(0, TOK)),
        (out_ref.at[pl.ds(pl.multiple_of(core * 32, 32), 32), :], pl.ds(TOK, 32)),
    )
    inward, outward = [], []
    for i, (source, place) in enumerate(parts):
        inward.append(pltpu.make_async_copy(source, buf.at[place, :], sems.at[i]))
        outward.append(
            pltpu.make_async_copy(buf.at[place, :], share_ref.at[place, :], sems.at[2 + i])
        )
    for copy in inward:
        copy.start()
    for arrived, copy in zip(inward, outward):
        arrived.wait()
        copy.start()
    for copy in outward:
        copy.wait()


def plan_kernel(owner_ref, row_ref, req_ref, tgt_ref):
    square = (TOK, TOK)
    lane = iota(square, 1)

    def column(values):
        return jnp.broadcast_to(values.astype(F32), square).T

    row = row_ref[...]
    owner = column(owner_ref[...])
    low, high = column(row & 127), column(row >> 7)
    onehot = owner == lane.astype(F32)
    onehot_f = onehot.astype(F32)
    onehot_b = onehot_f.astype(BF16)
    earlier = (lane < iota(square, 0)).astype(F32).astype(BF16)
    before = mm(earlier, onehot_b)
    slot = jnp.sum(before * onehot_f, axis=1, keepdims=True)
    tgt_ref[...] = (owner * SLOTS + slot).astype(jnp.int32)
    here = slot == lane.astype(F32)
    low = jnp.where(here, low, 0.0).astype(BF16)
    high = jnp.where(here, high, 0.0).astype(BF16)
    requests = mm_tn(onehot_b, low) + 128.0 * mm_tn(onehot_b, high)
    req_ref[...] = requests[:OWNERS].astype(jnp.int32)


def chosen(tgt_ref):
    return (tgt_ref[:, :1] == iota((TOK, OWNERS * SLOTS), 1)).astype(F32).astype(BF16)


def layer_kernel(
    lens_ref, got_ref, tgt_ref, weights_ref, gin_ref, gat_ref, ct_ref,
    out_ref, keep_ref, send_ref, dmx, xhat_ref, rstd_ref,
):
    core = lax.axis_index("core")
    emb = mm(chosen(tgt_ref), got_ref[...])
    gin = gin_ref[...]
    gat = gat_ref[...]
    centered = emb - jnp.mean(emb, axis=1, keepdims=True)
    rstd = lax.rsqrt(jnp.mean(centered * centered, axis=1, keepdims=True) + 1e-05)
    xhat = centered * rstd
    normed = (xhat * gin).astype(BF16)

    position, other = iota((TOK, TOK), 0), iota((TOK, TOK), 1)
    seg_row = jnp.zeros((TOK, TOK), jnp.int32)
    seg_col = jnp.zeros((TOK, TOK), jnp.int32)
    end = 0
    for user in range(lens_ref.shape[1]):
        end = end + lens_ref[0, user]
        seg_row = seg_row + (position >= end).astype(jnp.int32)
        seg_col = seg_col + (other >= end).astype(jnp.int32)
    allowed = (seg_row == seg_col) & (other <= position)

    mix0, mix1 = (
        mm(normed, weights_ref[half, :, :TOK, :].reshape(D, D)) for half in range(2)
    )

    sig0, sig1 = jax.nn.sigmoid(mix0), jax.nn.sigmoid(mix1)
    act0, act1 = (mix0 * sig0).astype(BF16), (mix1 * sig1).astype(BF16)
    slope0 = sig0 * (1.0 + mix0 * (1.0 - sig0))
    slope1 = sig1 * (1.0 + mix1 * (1.0 - sig1))
    gate_u = act0[:, :AW].astype(F32)

    heads = []
    attended = []
    for h in range(H):
        val = act0[:, AW + h * DH : AW + (h + 1) * DH]
        qry = act1[:, h * DH : (h + 1) * DH]
        key = act1[:, AW + h * DH : AW + (h + 1) * DH]
        score = mm_nt(qry, key) * DH ** (-0.5)
        sig = jax.nn.sigmoid(score)
        wgt = (jnp.where(allowed, score * sig, 0.0) / MAXLEN).astype(BF16)
        attended.append(mm(wgt, val).astype(BF16))
        slope = jnp.where(allowed, sig * (1.0 + score * (1.0 - sig)), 0.0) * (
            DH ** (-0.5) / MAXLEN
        )
        heads.append((val, qry, key, wgt, slope))
    att = jnp.concatenate(attended, axis=1).astype(F32)
    acent = att - jnp.mean(att, axis=1, keepdims=True)
    arstd = lax.rsqrt(jnp.mean(acent * acent, axis=1, keepdims=True) + 1e-05)
    ahat = acent * arstd
    scaled = ahat * gat
    gated = (scaled * gate_u).astype(BF16)

    w_out = jnp.stack([weights_ref[half, :, TOK:, :] for half in range(2)], axis=1)
    w_out = w_out.reshape(AW, D)
    ct = ct_ref[...]
    out_ref[...] = (emb + mm(gated, w_out)).astype(BF16)

    d_gated = mm_nt(ct, w_out).astype(BF16).astype(F32)
    d_gate = (d_gated * scaled).astype(BF16).astype(F32)
    d_ahat = d_gated * gate_u * gat
    d_att = arstd * (
        d_ahat
        - jnp.mean(d_ahat, axis=1, keepdims=True)
        - ahat * jnp.mean(d_ahat * ahat, axis=1, keepdims=True)
    )
    d_att = d_att.astype(BF16)
    d_val, d_qry, d_key = [], [], []
    for h in range(H):
        val, qry, key, wgt, slope = heads[h]
        d_head = d_att[:, h * DH : (h + 1) * DH]
        d_wgt = mm_nt(d_head, val).astype(BF16).astype(F32)
        d_val.append(mm_tn(wgt, d_head).astype(BF16))
        d_score = (d_wgt * slope).astype(BF16)
        d_qry.append(mm(d_score, key).astype(BF16))
        d_key.append(mm_tn(d_score, qry).astype(BF16))
    d_act0 = jnp.concatenate([d_gate] + [v.astype(F32) for v in d_val], axis=1)
    d_act1 = jnp.concatenate([v.astype(F32) for v in d_qry + d_key], axis=1)
    d_mix0 = (d_act0 * slope0).astype(BF16)
    d_mix1 = (d_act1 * slope1).astype(BF16)
    dmx[0] = d_mix0
    dmx[1] = d_mix1
    xhat_ref[...] = xhat
    rstd_ref[...] = jnp.broadcast_to(rstd, (TOK, TOK))
    for side, dst in ((1 - core, send_ref), (core, keep_ref)):
        dst[:, 0:1024] = normed
        dst[:, 1024:2048] = dmx[side]
        dst[:, 2048:2560] = gated
        dst[:, 2560:FACT] = ct_ref[:, pl.ds(pl.multiple_of(side * AW, AW), AW)]


def rows_kernel(tgt_ref, weights_ref, gin_ref, ct_ref, dmx, xhat_ref, rstd_ref, slots_ref):
    d_normed = mm_nt(dmx[0], weights_ref[0, :, :TOK, :].reshape(D, D))
    d_normed = d_normed + mm_nt(dmx[1], weights_ref[1, :, :TOK, :].reshape(D, D))
    d_xhat = d_normed.astype(BF16).astype(F32) * gin_ref[...]
    xhat = xhat_ref[...]
    d_emb = (
        rstd_ref[:, :1]
        * (
            d_xhat
            - jnp.mean(d_xhat, axis=1, keepdims=True)
            - xhat * jnp.mean(d_xhat * xhat, axis=1, keepdims=True)
        )
        + ct_ref[...].astype(F32)
    ).astype(BF16)
    slots_ref[...] = mm_tn(chosen(tgt_ref), d_emb).astype(BF16)


def grads_kernel(keep_ref, theirs_ref, out_ref, buf, sems):
    def both(first, last):
        return jnp.concatenate([keep_ref[:, first:last], theirs_ref[:, first:last]], axis=0)

    grad = mm_tn(both(2048, 2560), both(2560, FACT))
    for z in range(NZ):
        for p in range(XY):
            r, c = z * 64 + (p // 2) * 8, (p % 2) * 256
            part = grad[r : r + 8, c : c + 256]
            buf[z, p, :, 512:PCOLS] = jnp.concatenate(
                [part[:, :128], part[:, 128:]], axis=0
            ).astype(BF16)

    copies = []
    d_mix = both(1024, 2048)
    for z in range(NZ):
        grad = mm_tn(both(z * TOK, (z + 1) * TOK), d_mix)
        for p in range(XY):
            part = grad[8 * p : 8 * p + 8]
            buf[z, p, :, 0:512] = jnp.concatenate(
                [part[:, :512], part[:, 512:]], axis=0
            ).astype(BF16)
        copies.append(pltpu.make_async_copy(buf.at[z], out_ref.at[z], sems.at[z]))
        copies[-1].start()
    for copy in copies:
        copy.wait()


def pack_kernel(rows_ref, out_ref):
    r, k = iota((USED, OWNERS * SLOTS), 0), iota((USED, OWNERS * SLOTS), 1)
    take = (r // CAP) * SLOTS + r % CAP == k
    out_ref[...] = mm(take.astype(F32).astype(BF16), rows_ref[...]).astype(BF16)


def names_kernel(asked_ref, out_ref):
    first = lax.axis_index("z") * 256
    count = NZ * USED
    asked = asked_ref[:, 8:].reshape(NZ * OWNERS, 128).astype(jnp.int32)
    low, high = (part.astype(F32).astype(BF16) for part in (asked & 127, asked >> 7))
    row, col = iota((count, NZ * OWNERS), 0), iota((count, NZ * OWNERS), 1)
    owner = (row // CAP == col).astype(F32).astype(BF16)
    lane = iota((count, 128), 1)
    spread = mm(owner, low) + 128.0 * mm(owner, high)
    column = jnp.sum(
        jnp.where(iota((count, 128), 0) % CAP == lane, spread, 0.0), axis=1, keepdims=True
    )
    names = jnp.zeros((128, 128), F32)
    for line in range(count // 128):
        names = jnp.where(
            iota((128, 128), 1) == line, column[128 * line : 128 * line + 128], names
        )
    out_ref[...] = names.T[:PROWS].astype(jnp.int32) - first


def table_kernel(rows_ref, names_ref, after_ref, out_ref, buf, total, sems):
    half = NZ * USED // 2
    copies = [
        pltpu.make_async_copy(
            rows_ref.at[pl.ds(part * half, half), :], buf.at[part], sems.at[part]
        )
        for part in range(2)
    ]
    for copy in copies:
        copy.start()
    place = iota((256, 128), 0)
    lines = half // 128
    picks = [
        jnp.concatenate(
            [
                (place == names_ref[line : line + 1, :]).astype(F32).astype(BF16)
                for line in range(part * lines, (part + 1) * lines)
            ],
            axis=1,
        )
        for part in range(2)
    ]
    copies[0].wait()
    total[...] = mm(picks[0], buf[0])
    copies[1].wait()
    outs = []
    for n in range(4):
        cols = slice(256 * n, 256 * n + 256)
        total[:, cols] += mm(picks[1], buf[1, :, cols])
        block = pl.ds(256 * n, 256)
        outs.append(
            pltpu.make_async_copy(total.at[:, block], out_ref.at[:, block], sems.at[2 + n])
        )
        outs[-1].start()
    for copy in outs:
        copy.wait()


def square_kernel(mine_ref, other_ref, asked_ref, out_ref):
    total = jnp.zeros((PROWS, PCOLS), F32)
    for sums_ref in (mine_ref, other_ref):
        for i in range(XY):
            part = sums_ref[i].astype(F32)
            total = total + part * part
    mix = jnp.sum(total[:, :512])
    out = jnp.sum(total[:, 512:])
    lane = iota((8, 128), 1)
    squares = jnp.where(lane == 0, mix, jnp.where(lane == 1, out, 0.0))
    asked = asked_ref[...].astype(F32)
    for z in range(NZ):
        out_ref[z, :8] = squares
        out_ref[z, 8:] = asked


def scale_kernel(mine_ref, other_ref, squares_ref, mix_ref, out_ref):
    total = jnp.sum(squares_ref[:, :8], axis=0)[0:1]
    mix_sq, out_sq = total[:, 0:1], total[:, 1:2]
    mix_scale = jnp.minimum(1.0, 1.0 / jnp.sqrt(mix_sq / float(D * 4 * AW) + 1e-06))
    out_scale = jnp.minimum(1.0, 1.0 / jnp.sqrt(out_sq / float(D * AW) + 1e-06))
    core = lax.axis_index("core")
    for side, sums_ref in ((core, mine_ref), (1 - core, other_ref)):
        for p in range(XY):
            sums = sums_ref[p].astype(F32)
            mix, out = sums[:, :512] * mix_scale, sums[:, 512:] * out_scale
            for part in range(2):
                r = p * 8
                c = pl.multiple_of(side * D + part * 512, 512)
                mix_ref[r : r + 8, pl.ds(c, 512)] = mix[8 * part : 8 * part + 8]
                r = (p // 2) * 8
                c = pl.multiple_of(side * AW + (p % 2) * 256 + part * 128, 128)
                out_ref[r : r + 8, pl.ds(c, 128)] = out[8 * part : 8 * part + 8]


def vmem():
    return pl.BlockSpec(memory_space=pltpu.VMEM)


def call(body, outs, args, specs=None, outs_specs=None, **kwargs):
    shapes = [jax.ShapeDtypeStruct(s, t) for s, t in outs]
    one = len(shapes) == 1
    return pl.pallas_call(
        body,
        out_shape=shapes[0] if one else shapes,
        in_specs=specs or [vmem()] * len(args),
        out_specs=outs_specs or (vmem() if one else [vmem()] * len(shapes)),
        **kwargs,
    )(*args)


def cost(us):
    return pl.CostEstimate(flops=0, bytes_accessed=int(us * 3.0e6), transcendentals=0)


def exchange(array, axes):
    return lax.all_to_all(array, axes, split_axis=0, concat_axis=0, tiled=True)


def shards(
    item_table, item_row, item_owner, user_lengths, w_mix, w_out, gain_in, gain_attn, cotangent
):
    anywhere = pl.BlockSpec(memory_space=pl.ANY)
    pinned = pl.BlockSpec(memory_space=pltpu.HBM)
    share = call(
        share_kernel,
        [((TOK + 32, D), BF16)],
        (w_mix, w_out),
        specs=[anywhere, anywhere],
        outs_specs=anywhere,
        scratch_shapes=[pltpu.VMEM((TOK + 32, D), BF16), pltpu.SemaphoreType.DMA((4,))],
        compiler_params=pltpu.CompilerParams(vmem_limit_bytes=60 * MB),
    )
    weights = lax.all_gather(share, ("core", "z"), axis=0, tiled=True).reshape(2, NZ, 160, D)

    requests, target = call(
        plan_kernel,
        [((OWNERS, 128), jnp.int32), ((TOK, TOK), jnp.int32)],
        (item_owner.reshape(1, TOK), item_row.reshape(1, TOK)),
    )
    asked = exchange(requests, TABLE)
    wanted = asked[:, :SLOTS].reshape(OWNERS * SLOTS)
    found = item_table.at[wanted].get(mode="promise_in_bounds")
    got = exchange(found.reshape(OWNERS, SLOTS, D), TABLE)

    smem = pl.BlockSpec(memory_space=pltpu.SMEM)
    gin = gain_in.reshape(1, D)
    layer_out, keep, send, d_mix, xhat, rstd = call(
        layer_kernel,
        [
            ((TOK, D), BF16),
            ((TOK, FACT), BF16),
            ((TOK, FACT), BF16),
            ((2, TOK, D), BF16),
            ((TOK, D), F32),
            ((TOK, TOK), F32),
        ],
        (
            user_lengths,
            got.reshape(OWNERS * SLOTS, D),
            target,
            weights,
            gin,
            gain_attn.reshape(1, AW),
            cotangent,
        ),
        specs=[smem] + [vmem()] * 6,
        cost_estimate=cost(7),
        compiler_params=pltpu.CompilerParams(vmem_limit_bytes=32 * MB),
    )

    theirs = lax.ppermute(send, "core", [(0, 1), (1, 0)])
    grads = call(
        grads_kernel,
        [((NZ, XY, PROWS, PCOLS), BF16)],
        (keep, theirs),
        outs_specs=anywhere,
        scratch_shapes=[
            pltpu.VMEM((NZ, XY, PROWS, PCOLS), BF16),
            pltpu.SemaphoreType.DMA((NZ,)),
        ],
        cost_estimate=cost(3),
        compiler_params=pltpu.CompilerParams(vmem_limit_bytes=30 * MB),
    )
    grads, d_mix = lax.optimization_barrier((grads, d_mix))
    column = lax.psum_scatter(
        grads.reshape(NZ * XY * PROWS, PCOLS), "z", scatter_dimension=0, tiled=True
    )

    grad_slots = call(
        rows_kernel,
        [((OWNERS * SLOTS, D), BF16)],
        (target, weights, gin, cotangent, d_mix, xhat, rstd),
        cost_estimate=cost(3),
        compiler_params=pltpu.CompilerParams(vmem_limit_bytes=32 * MB),
    )
    received = exchange(grad_slots.reshape(OWNERS, SLOTS, D), TABLE)
    packed = call(
        pack_kernel,
        [((USED, D), BF16)],
        (received.reshape(OWNERS * SLOTS, D),),
        cost_estimate=cost(2),
        compiler_params=pltpu.CompilerParams(vmem_limit_bytes=16 * MB),
    )
    gathered = lax.all_gather(packed, "z", axis=0, tiled=True)
    plane = exchange(column.reshape(XY, PROWS, PCOLS), ("x", "y"))
    whole = jnp.sum(plane.astype(F32), axis=0).astype(BF16)
    mine = exchange(jnp.broadcast_to(whole[None], (XY, PROWS, PCOLS)), ("x", "y"))
    other = lax.ppermute(mine, "core", [(0, 1), (1, 0)])

    squares = call(
        square_kernel,
        [((NZ, 8 + OWNERS, 128), F32)],
        (mine, other, asked),
        cost_estimate=cost(1),
        compiler_params=pltpu.CompilerParams(vmem_limit_bytes=16 * MB),
    )
    squares = exchange(squares, "z")
    mix_grad, out_grad = call(
        scale_kernel,
        [((TOK, 4 * AW), F32), ((64, D), F32)],
        (mine, other, squares),
        cost_estimate=cost(2),
        compiler_params=pltpu.CompilerParams(vmem_limit_bytes=16 * MB),
    )
    names = call(
        names_kernel,
        [((PROWS, 128), jnp.int32)],
        (squares,),
        cost_estimate=cost(1),
        compiler_params=pltpu.CompilerParams(vmem_limit_bytes=16 * MB),
    )
    table_grad = call(
        table_kernel,
        [((256, D), F32)],
        (gathered, names, out_grad),
        specs=[pinned, vmem(), anywhere],
        outs_specs=anywhere,
        scratch_shapes=[
            pltpu.VMEM((2, NZ * USED // 2, D), BF16),
            pltpu.VMEM((256, D), F32),
            pltpu.SemaphoreType.DMA((6,)),
        ],
        cost_estimate=cost(3),
        compiler_params=pltpu.CompilerParams(vmem_limit_bytes=60 * MB),
    )
    return (layer_out, table_grad, mix_grad, out_grad)


def solution(mesh):
    cube = Mesh(mesh.devices.reshape(4, 4, 2, 8), ALL)
    in_specs = (
        P(TABLE, None),
        P(ALL),
        P(ALL, None),
        P(ALL, None),
        P("z", None),
        P("z", None),
        P(),
        P(),
        P(ALL, None),
    )
    out_specs = (
        P(ALL, None),
        P(ALL, None),
        P("z", None),
        P("z", None),
    )
    return jax.shard_map(shards, mesh=cube, in_specs=in_specs, out_specs=out_specs, check_vma=False)
```

```python
import jax
import jax.numpy as jnp
from jax import lax
from jax.experimental import pallas as pl
from jax.experimental.pallas import tpu as pltpu
from jax.sharding import Mesh
from jax.sharding import PartitionSpec as P

H = 4
DH = 128
MAXLEN = 64
TOK = 128
D = 1024
AW = H * DH
OWNERS = 32
CAP = 6
SLOTS = 8
NZ = 8
XY = 16
PROWS = 16
PCOLS = 640
FACT = 3072
USED = OWNERS * CAP
TABLE = ("x", "y", "core")
ALL = ("x", "y", "core", "z")
F32 = jnp.float32
BF16 = jnp.bfloat16
MB = 1024 * 1024


def mm(a, b):
    return lax.dot_general(a, b, (((1,), (0,)), ((), ())), preferred_element_type=F32)


def mm_nt(a, b):
    return lax.dot_general(a, b, (((1,), (1,)), ((), ())), preferred_element_type=F32)


def mm_tn(a, b):
    return lax.dot_general(a, b, (((0,), (0,)), ((), ())), preferred_element_type=F32)


def iota(shape, dim):
    return lax.broadcasted_iota(jnp.int32, shape, dim)


def share_kernel(mix_ref, out_ref, share_ref, buf, sems):
    core = lax.axis_index("core")
    parts = (
        (mix_ref.at[:, pl.ds(pl.multiple_of(core * D, D), D)], pl.ds(0, TOK)),
        (out_ref.at[pl.ds(pl.multiple_of(core * 32, 32), 32), :], pl.ds(TOK, 32)),
    )
    inward, outward = [], []
    for i, (source, place) in enumerate(parts):
        inward.append(pltpu.make_async_copy(source, buf.at[place, :], sems.at[i]))
        outward.append(
            pltpu.make_async_copy(buf.at[place, :], share_ref.at[place, :], sems.at[2 + i])
        )
    for copy in inward:
        copy.start()
    for arrived, copy in zip(inward, outward):
        arrived.wait()
        copy.start()
    for copy in outward:
        copy.wait()


def plan_kernel(owner_ref, row_ref, req_ref, tgt_ref):
    square = (TOK, TOK)
    lane = iota(square, 1)

    def column(values):
        return jnp.broadcast_to(values.astype(F32), square).T

    row = row_ref[...]
    owner = column(owner_ref[...])
    low, high = column(row & 127), column(row >> 7)
    onehot = owner == lane.astype(F32)
    onehot_f = onehot.astype(F32)
    onehot_b = onehot_f.astype(BF16)
    earlier = (lane < iota(square, 0)).astype(F32).astype(BF16)
    before = mm(earlier, onehot_b)
    slot = jnp.sum(before * onehot_f, axis=1, keepdims=True)
    tgt_ref[...] = (owner * SLOTS + slot).astype(jnp.int32)
    here = slot == lane.astype(F32)
    low = jnp.where(here, low, 0.0).astype(BF16)
    high = jnp.where(here, high, 0.0).astype(BF16)
    requests = mm_tn(onehot_b, low) + 128.0 * mm_tn(onehot_b, high)
    req_ref[...] = requests[:OWNERS].astype(jnp.int32)


def chosen(tgt_ref):
    return (tgt_ref[:, :1] == iota((TOK, OWNERS * SLOTS), 1)).astype(F32).astype(BF16)


def layer_kernel(
    lens_ref, got_ref, tgt_ref, weights_ref, gin_ref, gat_ref, ct_ref,
    out_ref, keep_ref, send_ref, dmx, xhat_ref, rstd_ref,
):
    core = lax.axis_index("core")
    emb = mm(chosen(tgt_ref), got_ref[...])
    gin = gin_ref[...]
    gat = gat_ref[...]
    centered = emb - jnp.mean(emb, axis=1, keepdims=True)
    rstd = lax.rsqrt(jnp.mean(centered * centered, axis=1, keepdims=True) + 1e-05)
    xhat = centered * rstd
    normed = (xhat * gin).astype(BF16)

    position, other = iota((TOK, TOK), 0), iota((TOK, TOK), 1)
    seg_row = jnp.zeros((TOK, TOK), jnp.int32)
    seg_col = jnp.zeros((TOK, TOK), jnp.int32)
    end = 0
    for user in range(lens_ref.shape[1]):
        end = end + lens_ref[0, user]
        seg_row = seg_row + (position >= end).astype(jnp.int32)
        seg_col = seg_col + (other >= end).astype(jnp.int32)
    allowed = (seg_row == seg_col) & (other <= position)

    mix0, mix1 = (
        mm(normed, weights_ref[half, :, :TOK, :].reshape(D, D)) for half in range(2)
    )

    sig0, sig1 = jax.nn.sigmoid(mix0), jax.nn.sigmoid(mix1)
    act0, act1 = (mix0 * sig0).astype(BF16), (mix1 * sig1).astype(BF16)
    slope0 = sig0 * (1.0 + mix0 * (1.0 - sig0))
    slope1 = sig1 * (1.0 + mix1 * (1.0 - sig1))
    gate_u = act0[:, :AW].astype(F32)

    heads = []
    attended = []
    for h in range(H):
        val = act0[:, AW + h * DH : AW + (h + 1) * DH]
        qry = act1[:, h * DH : (h + 1) * DH]
        key = act1[:, AW + h * DH : AW + (h + 1) * DH]
        score = mm_nt(qry, key) * DH ** (-0.5)
        sig = jax.nn.sigmoid(score)
        wgt = (jnp.where(allowed, score * sig, 0.0) / MAXLEN).astype(BF16)
        attended.append(mm(wgt, val).astype(BF16))
        slope = jnp.where(allowed, sig * (1.0 + score * (1.0 - sig)), 0.0) * (
            DH ** (-0.5) / MAXLEN
        )
        heads.append((val, qry, key, wgt, slope))
    att = jnp.concatenate(attended, axis=1).astype(F32)
    acent = att - jnp.mean(att, axis=1, keepdims=True)
    arstd = lax.rsqrt(jnp.mean(acent * acent, axis=1, keepdims=True) + 1e-05)
    ahat = acent * arstd
    scaled = ahat * gat
    gated = (scaled * gate_u).astype(BF16)

    w_out = jnp.stack([weights_ref[half, :, TOK:, :] for half in range(2)], axis=1)
    w_out = w_out.reshape(AW, D)
    ct = ct_ref[...]
    out_ref[...] = (emb + mm(gated, w_out)).astype(BF16)

    d_gated = mm_nt(ct, w_out).astype(BF16).astype(F32)
    d_gate = (d_gated * scaled).astype(BF16).astype(F32)
    d_ahat = d_gated * gate_u * gat
    d_att = arstd * (
        d_ahat
        - jnp.mean(d_ahat, axis=1, keepdims=True)
        - ahat * jnp.mean(d_ahat * ahat, axis=1, keepdims=True)
    )
    d_att = d_att.astype(BF16)
    d_val, d_qry, d_key = [], [], []
    for h in range(H):
        val, qry, key, wgt, slope = heads[h]
        d_head = d_att[:, h * DH : (h + 1) * DH]
        d_wgt = mm_nt(d_head, val).astype(BF16).astype(F32)
        d_val.append(mm_tn(wgt, d_head).astype(BF16))
        d_score = (d_wgt * slope).astype(BF16)
        d_qry.append(mm(d_score, key).astype(BF16))
        d_key.append(mm_tn(d_score, qry).astype(BF16))
    d_act0 = jnp.concatenate([d_gate] + [v.astype(F32) for v in d_val], axis=1)
    d_act1 = jnp.concatenate([v.astype(F32) for v in d_qry + d_key], axis=1)
    d_mix0 = (d_act0 * slope0).astype(BF16)
    d_mix1 = (d_act1 * slope1).astype(BF16)
    dmx[0] = d_mix0
    dmx[1] = d_mix1
    xhat_ref[...] = xhat
    rstd_ref[...] = jnp.broadcast_to(rstd, (TOK, TOK))
    for side, dst in ((1 - core, send_ref), (core, keep_ref)):
        dst[:, 0:1024] = normed
        dst[:, 1024:2048] = dmx[side]
        dst[:, 2048:2560] = gated
        dst[:, 2560:FACT] = ct_ref[:, pl.ds(pl.multiple_of(side * AW, AW), AW)]


def rows_kernel(tgt_ref, weights_ref, gin_ref, ct_ref, dmx, xhat_ref, rstd_ref, slots_ref):
    d_normed = mm_nt(dmx[0], weights_ref[0, :, :TOK, :].reshape(D, D))
    d_normed = d_normed + mm_nt(dmx[1], weights_ref[1, :, :TOK, :].reshape(D, D))
    d_xhat = d_normed.astype(BF16).astype(F32) * gin_ref[...]
    xhat = xhat_ref[...]
    d_emb = (
        rstd_ref[:, :1]
        * (
            d_xhat
            - jnp.mean(d_xhat, axis=1, keepdims=True)
            - xhat * jnp.mean(d_xhat * xhat, axis=1, keepdims=True)
        )
        + ct_ref[...].astype(F32)
    ).astype(BF16)
    slots_ref[...] = mm_tn(chosen(tgt_ref), d_emb).astype(BF16)


def grads_kernel(keep_ref, theirs_ref, mix_ref, out_ref, mix, out, sems):
    def both(first, last):
        return jnp.concatenate([keep_ref[:, first:last], theirs_ref[:, first:last]], axis=0)

    copies = []
    d_mix = both(1024, 2048)
    for z in range(NZ):
        grad = mm_tn(both(z * TOK, (z + 1) * TOK), d_mix)
        for p in range(XY):
            part = grad[8 * p : 8 * p + 8]
            mix[z, p] = jnp.concatenate([part[:, :512], part[:, 512:]], axis=0).astype(BF16)
        copies.append(pltpu.make_async_copy(mix.at[z], mix_ref.at[z], sems.at[z]))
        copies[-1].start()

    grad = mm_tn(both(2048, 2560), both(2560, FACT))
    for z in range(NZ):
        for p in range(XY):
            r, c = z * 64 + (p // 2) * 8, (p % 2) * 256
            part = grad[r : r + 8, c : c + 256]
            out[p, z * PROWS : (z + 1) * PROWS] = jnp.concatenate(
                [part[:, :128], part[:, 128:]], axis=0
            ).astype(BF16)
    copies.append(pltpu.make_async_copy(out, out_ref, sems.at[NZ]))
    copies[-1].start()
    for copy in copies:
        copy.wait()


def column_kernel(plane_ref, asked_ref, out_ref):
    total = jnp.sum(plane_ref[...].astype(F32), axis=0).astype(BF16)
    asked = asked_ref[...]
    low, high = ((part).astype(F32).astype(BF16) for part in (asked & 127, asked >> 7))
    for z in range(NZ):
        out_ref[z, :PROWS] = total[z * PROWS : (z + 1) * PROWS]
        out_ref[z, PROWS : PROWS + OWNERS] = low
        out_ref[z, PROWS + OWNERS :] = high


def pack_kernel(rows_ref, out_ref):
    r, k = iota((USED, OWNERS * SLOTS), 0), iota((USED, OWNERS * SLOTS), 1)
    take = (r // CAP) * SLOTS + r % CAP == k
    out_ref[...] = mm(take.astype(F32).astype(BF16), rows_ref[...]).astype(BF16)


def names_kernel(column_ref, out_ref):
    first = lax.axis_index("z") * 256
    count = NZ * USED
    low = column_ref[:, PROWS : PROWS + OWNERS].reshape(NZ * OWNERS, 128)
    high = column_ref[:, PROWS + OWNERS :].reshape(NZ * OWNERS, 128)
    row, col = iota((count, NZ * OWNERS), 0), iota((count, NZ * OWNERS), 1)
    owner = (row // CAP == col).astype(F32).astype(BF16)
    lane = iota((count, 128), 1)
    spread = mm(owner, low) + 128.0 * mm(owner, high)
    column = jnp.sum(
        jnp.where(iota((count, 128), 0) % CAP == lane, spread, 0.0), axis=1, keepdims=True
    )
    names = jnp.zeros((128, 128), F32)
    for line in range(count // 128):
        names = jnp.where(
            iota((128, 128), 1) == line, column[128 * line : 128 * line + 128], names
        )
    out_ref[...] = names.T[:PROWS].astype(jnp.int32) - first


def table_kernel(rows_ref, names_ref, after_ref, out_ref, buf, total, sems):
    half = NZ * USED // 2
    copies = [
        pltpu.make_async_copy(
            rows_ref.at[pl.ds(part * half, half), :], buf.at[part], sems.at[part]
        )
        for part in range(2)
    ]
    for copy in copies:
        copy.start()
    place = iota((256, 128), 0)
    lines = half // 128
    picks = [
        jnp.concatenate(
            [
                (place == names_ref[line : line + 1, :]).astype(F32).astype(BF16)
                for line in range(part * lines, (part + 1) * lines)
            ],
            axis=1,
        )
        for part in range(2)
    ]
    copies[0].wait()
    total[...] = mm(picks[0], buf[0])
    copies[1].wait()
    outs = []
    for n in range(4):
        cols = slice(256 * n, 256 * n + 256)
        total[:, cols] += mm(picks[1], buf[1, :, cols])
        block = pl.ds(256 * n, 256)
        outs.append(
            pltpu.make_async_copy(total.at[:, block], out_ref.at[:, block], sems.at[2 + n])
        )
        outs[-1].start()
    for copy in outs:
        copy.wait()


def square_kernel(mine_ref, other_ref, out_ref):
    total = jnp.zeros((PROWS, PCOLS), F32)
    for sums_ref in (mine_ref, other_ref):
        for i in range(XY):
            part = sums_ref[i].astype(F32)
            total = total + part * part
    mix = jnp.sum(total[:, :512])
    out = jnp.sum(total[:, 512:])
    lane = iota((NZ, 8, 128), 2)
    out_ref[...] = jnp.where(lane == 0, mix, jnp.where(lane == 1, out, 0.0))


def scale_kernel(mine_ref, other_ref, squares_ref, mix_ref, out_ref):
    total = jnp.sum(squares_ref[...], axis=0)[0:1]
    mix_sq, out_sq = total[:, 0:1], total[:, 1:2]
    mix_scale = jnp.minimum(1.0, 1.0 / jnp.sqrt(mix_sq / float(D * 4 * AW) + 1e-06))
    out_scale = jnp.minimum(1.0, 1.0 / jnp.sqrt(out_sq / float(D * AW) + 1e-06))
    core = lax.axis_index("core")
    for side, sums_ref in ((core, mine_ref), (1 - core, other_ref)):
        for p in range(XY):
            sums = sums_ref[p].astype(F32)
            mix, out = sums[:, :512] * mix_scale, sums[:, 512:] * out_scale
            for part in range(2):
                r = p * 8
                c = pl.multiple_of(side * D + part * 512, 512)
                mix_ref[r : r + 8, pl.ds(c, 512)] = mix[8 * part : 8 * part + 8]
                r = (p // 2) * 8
                c = pl.multiple_of(side * AW + (p % 2) * 256 + part * 128, 128)
                out_ref[r : r + 8, pl.ds(c, 128)] = out[8 * part : 8 * part + 8]


def vmem():
    return pl.BlockSpec(memory_space=pltpu.VMEM)


def call(body, outs, args, specs=None, outs_specs=None, **kwargs):
    shapes = [jax.ShapeDtypeStruct(s, t) for s, t in outs]
    one = len(shapes) == 1
    return pl.pallas_call(
        body,
        out_shape=shapes[0] if one else shapes,
        in_specs=specs or [vmem()] * len(args),
        out_specs=outs_specs or (vmem() if one else [vmem()] * len(shapes)),
        **kwargs,
    )(*args)


def cost(us):
    return pl.CostEstimate(flops=0, bytes_accessed=int(us * 3.0e6), transcendentals=0)


def exchange(array, axes):
    return lax.all_to_all(array, axes, split_axis=0, concat_axis=0, tiled=True)


def shards(
    item_table, item_row, item_owner, user_lengths, w_mix, w_out, gain_in, gain_attn, cotangent
):
    anywhere = pl.BlockSpec(memory_space=pl.ANY)
    pinned = pl.BlockSpec(memory_space=pltpu.HBM)
    share = call(
        share_kernel,
        [((TOK + 32, D), BF16)],
        (w_mix, w_out),
        specs=[anywhere, anywhere],
        outs_specs=anywhere,
        scratch_shapes=[pltpu.VMEM((TOK + 32, D), BF16), pltpu.SemaphoreType.DMA((4,))],
        compiler_params=pltpu.CompilerParams(vmem_limit_bytes=60 * MB),
    )
    weights = lax.all_gather(share, ("core", "z"), axis=0, tiled=True).reshape(2, NZ, 160, D)

    requests, target = call(
        plan_kernel,
        [((OWNERS, 128), jnp.int32), ((TOK, TOK), jnp.int32)],
        (item_owner.reshape(1, TOK), item_row.reshape(1, TOK)),
    )
    asked = exchange(requests, TABLE)
    wanted = asked[:, :SLOTS].reshape(OWNERS * SLOTS)
    found = item_table.at[wanted].get(mode="promise_in_bounds")
    got = exchange(found.reshape(OWNERS, SLOTS, D), TABLE)

    smem = pl.BlockSpec(memory_space=pltpu.SMEM)
    gin = gain_in.reshape(1, D)
    layer_out, keep, send, d_mix, xhat, rstd = call(
        layer_kernel,
        [
            ((TOK, D), BF16),
            ((TOK, FACT), BF16),
            ((TOK, FACT), BF16),
            ((2, TOK, D), BF16),
            ((TOK, D), F32),
            ((TOK, TOK), F32),
        ],
        (
            user_lengths,
            got.reshape(OWNERS * SLOTS, D),
            target,
            weights,
            gin,
            gain_attn.reshape(1, AW),
            cotangent,
        ),
        specs=[smem] + [vmem()] * 6,
        cost_estimate=cost(7),
        compiler_params=pltpu.CompilerParams(vmem_limit_bytes=32 * MB),
    )

    theirs = lax.ppermute(send, "core", [(0, 1), (1, 0)])
    mix_part, out_part = call(
        grads_kernel,
        [((NZ, XY, PROWS, 512), BF16), ((XY, NZ * PROWS, 128), BF16)],
        (keep, theirs),
        outs_specs=[anywhere, anywhere],
        scratch_shapes=[
            pltpu.VMEM((NZ, XY, PROWS, 512), BF16),
            pltpu.VMEM((XY, NZ * PROWS, 128), BF16),
            pltpu.SemaphoreType.DMA((NZ + 1,)),
        ],
        cost_estimate=cost(3),
        compiler_params=pltpu.CompilerParams(vmem_limit_bytes=30 * MB),
    )
    mix_part, d_mix = lax.optimization_barrier((mix_part, d_mix))
    mix_column = lax.psum_scatter(
        mix_part.reshape(NZ * XY * PROWS, 512), "z", scatter_dimension=0, tiled=True
    )

    grad_slots = call(
        rows_kernel,
        [((OWNERS * SLOTS, D), BF16)],
        (target, weights, gin, cotangent, d_mix, xhat, rstd),
        cost_estimate=cost(3),
        compiler_params=pltpu.CompilerParams(vmem_limit_bytes=32 * MB),
    )
    received = exchange(grad_slots.reshape(OWNERS, SLOTS, D), TABLE)
    packed = call(
        pack_kernel,
        [((USED, D), BF16)],
        (received.reshape(OWNERS * SLOTS, D),),
        cost_estimate=cost(2),
        compiler_params=pltpu.CompilerParams(vmem_limit_bytes=16 * MB),
    )
    out_part, packed = lax.optimization_barrier((out_part, packed))
    gathered = lax.all_gather(packed, "z", axis=0, tiled=True)

    out_column = call(
        column_kernel,
        [((NZ, PROWS + 2 * OWNERS, 128), BF16)],
        (exchange(out_part, ("x", "y")), asked),
        cost_estimate=cost(1),
        compiler_params=pltpu.CompilerParams(vmem_limit_bytes=16 * MB),
    )
    out_column = exchange(out_column, "z")
    mix_column, out_column = lax.optimization_barrier((mix_column, out_column))
    names = call(
        names_kernel,
        [((PROWS, 128), jnp.int32)],
        (out_column,),
        cost_estimate=cost(2),
        compiler_params=pltpu.CompilerParams(vmem_limit_bytes=16 * MB),
    )
    mix_plane = exchange(mix_column.reshape(XY, PROWS, 512), ("x", "y"))
    whole = jnp.concatenate(
        [
            jnp.sum(mix_plane.astype(F32), axis=0),
            jnp.sum(out_column[:, :PROWS].astype(F32), axis=0),
        ],
        axis=1,
    ).astype(BF16)
    mine = exchange(jnp.broadcast_to(whole[None], (XY, PROWS, PCOLS)), ("x", "y"))
    other = lax.ppermute(mine, "core", [(0, 1), (1, 0)])

    squares = call(
        square_kernel,
        [((NZ, 8, 128), F32)],
        (mine, other),
        cost_estimate=cost(1),
        compiler_params=pltpu.CompilerParams(vmem_limit_bytes=16 * MB),
    )
    squares = exchange(squares, "z")
    mix_grad, out_grad = call(
        scale_kernel,
        [((TOK, 4 * AW), F32), ((64, D), F32)],
        (mine, other, squares),
        cost_estimate=cost(2),
        compiler_params=pltpu.CompilerParams(vmem_limit_bytes=16 * MB),
    )
    table_grad = call(
        table_kernel,
        [((256, D), F32)],
        (gathered, names, out_grad),
        specs=[pinned, vmem(), anywhere],
        outs_specs=anywhere,
        scratch_shapes=[
            pltpu.VMEM((2, NZ * USED // 2, D), BF16),
            pltpu.VMEM((256, D), F32),
            pltpu.SemaphoreType.DMA((6,)),
        ],
        cost_estimate=cost(3),
        compiler_params=pltpu.CompilerParams(vmem_limit_bytes=60 * MB),
    )
    return (layer_out, table_grad, mix_grad, out_grad)


def solution(mesh):
    cube = Mesh(mesh.devices.reshape(4, 4, 2, 8), ALL)
    in_specs = (
        P(TABLE, None),
        P(ALL),
        P(ALL, None),
        P(ALL, None),
        P("z", None),
        P("z", None),
        P(),
        P(),
        P(ALL, None),
    )
    out_specs = (
        P(ALL, None),
        P(ALL, None),
        P("z", None),
        P("z", None),
    )
    return jax.shard_map(shards, mesh=cube, in_specs=in_specs, out_specs=out_specs, check_vma=False)
```

```python
import jax
import jax.numpy as jnp
from jax import lax
from jax.experimental import pallas as pl
from jax.experimental.pallas import tpu as pltpu
from jax.sharding import Mesh
from jax.sharding import PartitionSpec as P

H = 4
DH = 128
MAXLEN = 64
TOK = 128
D = 1024
AW = H * DH
OWNERS = 32
CAP = 6
SLOTS = 8
NZ = 8
XY = 16
PROWS = 16
PCOLS = 640
FACT = 3072
USED = OWNERS * CAP
TABLE = ("x", "y", "core")
ALL = ("x", "y", "core", "z")
F32 = jnp.float32
BF16 = jnp.bfloat16
MB = 1024 * 1024


def mm(a, b):
    return lax.dot_general(a, b, (((1,), (0,)), ((), ())), preferred_element_type=F32)


def mm_nt(a, b):
    return lax.dot_general(a, b, (((1,), (1,)), ((), ())), preferred_element_type=F32)


def mm_tn(a, b):
    return lax.dot_general(a, b, (((0,), (0,)), ((), ())), preferred_element_type=F32)


def iota(shape, dim):
    return lax.broadcasted_iota(jnp.int32, shape, dim)


def share_kernel(mix_ref, out_ref, share_ref, buf, sems):
    core = lax.axis_index("core")
    parts = (
        (mix_ref.at[:, pl.ds(pl.multiple_of(core * D, D), D)], pl.ds(0, TOK)),
        (out_ref.at[pl.ds(pl.multiple_of(core * 32, 32), 32), :], pl.ds(TOK, 32)),
    )
    inward, outward = [], []
    for i, (source, place) in enumerate(parts):
        inward.append(pltpu.make_async_copy(source, buf.at[place, :], sems.at[i]))
        outward.append(
            pltpu.make_async_copy(buf.at[place, :], share_ref.at[place, :], sems.at[2 + i])
        )
    for copy in inward:
        copy.start()
    for arrived, copy in zip(inward, outward):
        arrived.wait()
        copy.start()
    for copy in outward:
        copy.wait()


def plan_kernel(owner_ref, row_ref, req_ref, tgt_ref):
    square = (TOK, TOK)
    lane = iota(square, 1)

    def column(values):
        return jnp.broadcast_to(values.astype(F32), square).T

    row = row_ref[...]
    owner = column(owner_ref[...])
    low, high = column(row & 127), column(row >> 7)
    onehot = owner == lane.astype(F32)
    onehot_f = onehot.astype(F32)
    onehot_b = onehot_f.astype(BF16)
    earlier = (lane < iota(square, 0)).astype(F32).astype(BF16)
    before = mm(earlier, onehot_b)
    slot = jnp.sum(before * onehot_f, axis=1, keepdims=True)
    tgt_ref[...] = (owner * SLOTS + slot).astype(jnp.int32)
    here = slot == lane.astype(F32)
    low = jnp.where(here, low, 0.0).astype(BF16)
    high = jnp.where(here, high, 0.0).astype(BF16)
    requests = mm_tn(onehot_b, low) + 128.0 * mm_tn(onehot_b, high)
    req_ref[...] = requests[:OWNERS].astype(jnp.int32)


def chosen(tgt_ref):
    return (tgt_ref[:, :1] == iota((TOK, OWNERS * SLOTS), 1)).astype(F32).astype(BF16)


def layer_kernel(
    lens_ref, got_ref, tgt_ref, weights_ref, gin_ref, gat_ref, ct_ref,
    out_ref, keep_ref, send_ref, dmx, xhat_ref, rstd_ref,
):
    core = lax.axis_index("core")
    emb = mm(chosen(tgt_ref), got_ref[...])
    gin = gin_ref[...]
    gat = gat_ref[...]
    centered = emb - jnp.mean(emb, axis=1, keepdims=True)
    rstd = lax.rsqrt(jnp.mean(centered * centered, axis=1, keepdims=True) + 1e-05)
    xhat = centered * rstd
    normed = (xhat * gin).astype(BF16)

    position, other = iota((TOK, TOK), 0), iota((TOK, TOK), 1)
    seg_row = jnp.zeros((TOK, TOK), jnp.int32)
    seg_col = jnp.zeros((TOK, TOK), jnp.int32)
    end = 0
    for user in range(lens_ref.shape[1]):
        end = end + lens_ref[0, user]
        seg_row = seg_row + (position >= end).astype(jnp.int32)
        seg_col = seg_col + (other >= end).astype(jnp.int32)
    allowed = (seg_row == seg_col) & (other <= position)

    mix0, mix1 = (
        mm(normed, weights_ref[half, :, :TOK, :].reshape(D, D)) for half in range(2)
    )

    sig0, sig1 = jax.nn.sigmoid(mix0), jax.nn.sigmoid(mix1)
    act0, act1 = (mix0 * sig0).astype(BF16), (mix1 * sig1).astype(BF16)
    slope0 = sig0 * (1.0 + mix0 * (1.0 - sig0))
    slope1 = sig1 * (1.0 + mix1 * (1.0 - sig1))
    gate_u = act0[:, :AW].astype(F32)

    heads = []
    attended = []
    for h in range(H):
        val = act0[:, AW + h * DH : AW + (h + 1) * DH]
        qry = act1[:, h * DH : (h + 1) * DH]
        key = act1[:, AW + h * DH : AW + (h + 1) * DH]
        score = mm_nt(qry, key) * DH ** (-0.5)
        sig = jax.nn.sigmoid(score)
        wgt = (jnp.where(allowed, score * sig, 0.0) / MAXLEN).astype(BF16)
        attended.append(mm(wgt, val).astype(BF16))
        slope = jnp.where(allowed, sig * (1.0 + score * (1.0 - sig)), 0.0) * (
            DH ** (-0.5) / MAXLEN
        )
        heads.append((val, qry, key, wgt, slope))
    att = jnp.concatenate(attended, axis=1).astype(F32)
    acent = att - jnp.mean(att, axis=1, keepdims=True)
    arstd = lax.rsqrt(jnp.mean(acent * acent, axis=1, keepdims=True) + 1e-05)
    ahat = acent * arstd
    scaled = ahat * gat
    gated = (scaled * gate_u).astype(BF16)

    w_out = jnp.stack([weights_ref[half, :, TOK:, :] for half in range(2)], axis=1)
    w_out = w_out.reshape(AW, D)
    ct = ct_ref[...]
    out_ref[...] = (emb + mm(gated, w_out)).astype(BF16)

    d_gated = mm_nt(ct, w_out).astype(BF16).astype(F32)
    d_gate = (d_gated * scaled).astype(BF16).astype(F32)
    d_ahat = d_gated * gate_u * gat
    d_att = arstd * (
        d_ahat
        - jnp.mean(d_ahat, axis=1, keepdims=True)
        - ahat * jnp.mean(d_ahat * ahat, axis=1, keepdims=True)
    )
    d_att = d_att.astype(BF16)
    d_val, d_qry, d_key = [], [], []
    for h in range(H):
        val, qry, key, wgt, slope = heads[h]
        d_head = d_att[:, h * DH : (h + 1) * DH]
        d_wgt = mm_nt(d_head, val).astype(BF16).astype(F32)
        d_val.append(mm_tn(wgt, d_head).astype(BF16))
        d_score = (d_wgt * slope).astype(BF16)
        d_qry.append(mm(d_score, key).astype(BF16))
        d_key.append(mm_tn(d_score, qry).astype(BF16))
    d_act0 = jnp.concatenate([d_gate] + [v.astype(F32) for v in d_val], axis=1)
    d_act1 = jnp.concatenate([v.astype(F32) for v in d_qry + d_key], axis=1)
    d_mix0 = (d_act0 * slope0).astype(BF16)
    d_mix1 = (d_act1 * slope1).astype(BF16)
    dmx[0] = d_mix0
    dmx[1] = d_mix1
    xhat_ref[...] = xhat
    rstd_ref[...] = jnp.broadcast_to(rstd, (TOK, TOK))
    for side, dst in ((1 - core, send_ref), (core, keep_ref)):
        dst[:, 0:1024] = normed
        dst[:, 1024:2048] = dmx[side]
        dst[:, 2048:2560] = gated
        dst[:, 2560:FACT] = ct_ref[:, pl.ds(pl.multiple_of(side * AW, AW), AW)]


def rows_kernel(tgt_ref, weights_ref, gin_ref, ct_ref, dmx, xhat_ref, rstd_ref, slots_ref):
    d_normed = mm_nt(dmx[0], weights_ref[0, :, :TOK, :].reshape(D, D))
    d_normed = d_normed + mm_nt(dmx[1], weights_ref[1, :, :TOK, :].reshape(D, D))
    d_xhat = d_normed.astype(BF16).astype(F32) * gin_ref[...]
    xhat = xhat_ref[...]
    d_emb = (
        rstd_ref[:, :1]
        * (
            d_xhat
            - jnp.mean(d_xhat, axis=1, keepdims=True)
            - xhat * jnp.mean(d_xhat * xhat, axis=1, keepdims=True)
        )
        + ct_ref[...].astype(F32)
    ).astype(BF16)
    slots_ref[...] = mm_tn(chosen(tgt_ref), d_emb).astype(BF16)


def grads_kernel(keep_ref, theirs_ref, mix_ref, out_ref, mix, out, sems):
    def both(first, last):
        return jnp.concatenate([keep_ref[:, first:last], theirs_ref[:, first:last]], axis=0)

    copies = []
    d_mix = both(1024, 2048)
    for z in range(NZ):
        grad = mm_tn(both(z * TOK, (z + 1) * TOK), d_mix)
        for p in range(XY):
            part = grad[8 * p : 8 * p + 8]
            mix[z, p] = jnp.concatenate([part[:, :512], part[:, 512:]], axis=0).astype(BF16)
        copies.append(pltpu.make_async_copy(mix.at[z], mix_ref.at[z], sems.at[z]))
        copies[-1].start()

    grad = mm_tn(both(2048, 2560), both(2560, FACT))
    for z in range(NZ):
        for p in range(XY):
            r, c = z * 64 + (p // 2) * 8, (p % 2) * 256
            part = grad[r : r + 8, c : c + 256]
            out[p, z * PROWS : (z + 1) * PROWS] = jnp.concatenate(
                [part[:, :128], part[:, 128:]], axis=0
            ).astype(BF16)
    copies.append(pltpu.make_async_copy(out, out_ref, sems.at[NZ]))
    copies[-1].start()
    for copy in copies:
        copy.wait()


def column_kernel(plane_ref, asked_ref, out_ref):
    total = jnp.sum(plane_ref[...].astype(F32), axis=0).astype(BF16)
    asked = asked_ref[...]
    low, high = ((part).astype(F32).astype(BF16) for part in (asked & 127, asked >> 7))
    for z in range(NZ):
        out_ref[z, :PROWS] = total[z * PROWS : (z + 1) * PROWS]
        out_ref[z, PROWS : PROWS + OWNERS] = low
        out_ref[z, PROWS + OWNERS :] = high


def pack_kernel(rows_ref, out_ref):
    r, k = iota((USED, OWNERS * SLOTS), 0), iota((USED, OWNERS * SLOTS), 1)
    take = (r // CAP) * SLOTS + r % CAP == k
    out_ref[...] = mm(take.astype(F32).astype(BF16), rows_ref[...]).astype(BF16)


def names_kernel(column_ref, out_ref):
    first = lax.axis_index("z") * 256
    count = NZ * USED
    low = column_ref[:, PROWS : PROWS + OWNERS].reshape(NZ * OWNERS, 128)
    high = column_ref[:, PROWS + OWNERS :].reshape(NZ * OWNERS, 128)
    row, col = iota((count, NZ * OWNERS), 0), iota((count, NZ * OWNERS), 1)
    owner = (row // CAP == col).astype(F32).astype(BF16)
    lane = iota((count, 128), 1)
    spread = mm(owner, low) + 128.0 * mm(owner, high)
    column = jnp.sum(
        jnp.where(iota((count, 128), 0) % CAP == lane, spread, 0.0), axis=1, keepdims=True
    )
    names = jnp.zeros((128, 128), F32)
    for line in range(count // 128):
        names = jnp.where(
            iota((128, 128), 1) == line, column[128 * line : 128 * line + 128], names
        )
    out_ref[...] = names.T[:PROWS].astype(jnp.int32) - first


def table_kernel(rows_ref, names_ref, out_ref, buf, total, sems):
    half = NZ * USED // 2
    copies = [
        pltpu.make_async_copy(
            rows_ref.at[pl.ds(part * half, half), :], buf.at[part], sems.at[part]
        )
        for part in range(2)
    ]
    for copy in copies:
        copy.start()
    place = iota((256, 128), 0)
    lines = half // 128
    picks = [
        jnp.concatenate(
            [
                (place == names_ref[line : line + 1, :]).astype(F32).astype(BF16)
                for line in range(part * lines, (part + 1) * lines)
            ],
            axis=1,
        )
        for part in range(2)
    ]
    copies[0].wait()
    total[...] = mm(picks[0], buf[0])
    copies[1].wait()
    outs = []
    for n in range(4):
        cols = slice(256 * n, 256 * n + 256)
        total[:, cols] += mm(picks[1], buf[1, :, cols])
        block = pl.ds(256 * n, 256)
        outs.append(
            pltpu.make_async_copy(total.at[:, block], out_ref.at[:, block], sems.at[2 + n])
        )
        outs[-1].start()
    for copy in outs:
        copy.wait()


def square_kernel(mine_ref, other_ref, out_ref):
    total = jnp.zeros((PROWS, PCOLS), F32)
    for sums_ref in (mine_ref, other_ref):
        for i in range(XY):
            part = sums_ref[i].astype(F32)
            total = total + part * part
    mix = jnp.sum(total[:, :512])
    out = jnp.sum(total[:, 512:])
    lane = iota((NZ, 8, 128), 2)
    out_ref[...] = jnp.where(lane == 0, mix, jnp.where(lane == 1, out, 0.0))


def scale_kernel(mine_ref, other_ref, squares_ref, mix_ref, out_ref):
    total = jnp.sum(squares_ref[...], axis=0)[0:1]
    mix_sq, out_sq = total[:, 0:1], total[:, 1:2]
    mix_scale = jnp.minimum(1.0, 1.0 / jnp.sqrt(mix_sq / float(D * 4 * AW) + 1e-06))
    out_scale = jnp.minimum(1.0, 1.0 / jnp.sqrt(out_sq / float(D * AW) + 1e-06))
    core = lax.axis_index("core")
    for side, sums_ref in ((core, mine_ref), (1 - core, other_ref)):
        for p in range(XY):
            sums = sums_ref[p].astype(F32)
            mix, out = sums[:, :512] * mix_scale, sums[:, 512:] * out_scale
            for part in range(2):
                r = p * 8
                c = pl.multiple_of(side * D + part * 512, 512)
                mix_ref[r : r + 8, pl.ds(c, 512)] = mix[8 * part : 8 * part + 8]
                r = (p // 2) * 8
                c = pl.multiple_of(side * AW + (p % 2) * 256 + part * 128, 128)
                out_ref[r : r + 8, pl.ds(c, 128)] = out[8 * part : 8 * part + 8]


def vmem():
    return pl.BlockSpec(memory_space=pltpu.VMEM)


def call(body, outs, args, specs=None, outs_specs=None, **kwargs):
    shapes = [jax.ShapeDtypeStruct(s, t) for s, t in outs]
    one = len(shapes) == 1
    return pl.pallas_call(
        body,
        out_shape=shapes[0] if one else shapes,
        in_specs=specs or [vmem()] * len(args),
        out_specs=outs_specs or (vmem() if one else [vmem()] * len(shapes)),
        **kwargs,
    )(*args)


def cost(us):
    return pl.CostEstimate(flops=0, bytes_accessed=int(us * 3.0e6), transcendentals=0)


def exchange(array, axes):
    return lax.all_to_all(array, axes, split_axis=0, concat_axis=0, tiled=True)


def shards(
    item_table, item_row, item_owner, user_lengths, w_mix, w_out, gain_in, gain_attn, cotangent
):
    anywhere = pl.BlockSpec(memory_space=pl.ANY)
    pinned = pl.BlockSpec(memory_space=pltpu.HBM)
    share = call(
        share_kernel,
        [((TOK + 32, D), BF16)],
        (w_mix, w_out),
        specs=[anywhere, anywhere],
        outs_specs=anywhere,
        scratch_shapes=[pltpu.VMEM((TOK + 32, D), BF16), pltpu.SemaphoreType.DMA((4,))],
        compiler_params=pltpu.CompilerParams(vmem_limit_bytes=60 * MB),
    )
    weights = lax.all_gather(share, ("core", "z"), axis=0, tiled=True).reshape(2, NZ, 160, D)

    requests, target = call(
        plan_kernel,
        [((OWNERS, 128), jnp.int32), ((TOK, TOK), jnp.int32)],
        (item_owner.reshape(1, TOK), item_row.reshape(1, TOK)),
    )
    asked = exchange(requests, TABLE)
    wanted = asked[:, :SLOTS].reshape(OWNERS * SLOTS)
    found = item_table.at[wanted].get(mode="promise_in_bounds")
    got = exchange(found.reshape(OWNERS, SLOTS, D), TABLE)

    smem = pl.BlockSpec(memory_space=pltpu.SMEM)
    gin = gain_in.reshape(1, D)
    layer_out, keep, send, d_mix, xhat, rstd = call(
        layer_kernel,
        [
            ((TOK, D), BF16),
            ((TOK, FACT), BF16),
            ((TOK, FACT), BF16),
            ((2, TOK, D), BF16),
            ((TOK, D), F32),
            ((TOK, TOK), F32),
        ],
        (
            user_lengths,
            got.reshape(OWNERS * SLOTS, D),
            target,
            weights,
            gin,
            gain_attn.reshape(1, AW),
            cotangent,
        ),
        specs=[smem] + [vmem()] * 6,
        cost_estimate=cost(7),
        compiler_params=pltpu.CompilerParams(vmem_limit_bytes=32 * MB),
    )

    theirs = lax.ppermute(send, "core", [(0, 1), (1, 0)])
    mix_part, out_part = call(
        grads_kernel,
        [((NZ, XY, PROWS, 512), BF16), ((XY, NZ * PROWS, 128), BF16)],
        (keep, theirs),
        outs_specs=[anywhere, anywhere],
        scratch_shapes=[
            pltpu.VMEM((NZ, XY, PROWS, 512), BF16),
            pltpu.VMEM((XY, NZ * PROWS, 128), BF16),
            pltpu.SemaphoreType.DMA((NZ + 1,)),
        ],
        cost_estimate=cost(3),
        compiler_params=pltpu.CompilerParams(vmem_limit_bytes=30 * MB),
    )
    mix_part, d_mix = lax.optimization_barrier((mix_part, d_mix))
    mix_column = lax.psum_scatter(
        mix_part.reshape(NZ * XY * PROWS, 512), "z", scatter_dimension=0, tiled=True
    )

    grad_slots = call(
        rows_kernel,
        [((OWNERS * SLOTS, D), BF16)],
        (target, weights, gin, cotangent, d_mix, xhat, rstd),
        cost_estimate=cost(3),
        compiler_params=pltpu.CompilerParams(vmem_limit_bytes=32 * MB),
    )
    received = exchange(grad_slots.reshape(OWNERS, SLOTS, D), TABLE)
    packed = call(
        pack_kernel,
        [((USED, D), BF16)],
        (received.reshape(OWNERS * SLOTS, D),),
        cost_estimate=cost(2),
        compiler_params=pltpu.CompilerParams(vmem_limit_bytes=16 * MB),
    )
    out_part, packed = lax.optimization_barrier((out_part, packed))
    gathered = lax.all_gather(packed, "z", axis=0, tiled=True)

    out_column = call(
        column_kernel,
        [((NZ, PROWS + 2 * OWNERS, 128), BF16)],
        (exchange(out_part, ("x", "y")), asked),
        cost_estimate=cost(1),
        compiler_params=pltpu.CompilerParams(vmem_limit_bytes=16 * MB),
    )
    out_column = exchange(out_column, "z")
    mix_column, out_column = lax.optimization_barrier((mix_column, out_column))
    names = call(
        names_kernel,
        [((PROWS, 128), jnp.int32)],
        (out_column,),
        cost_estimate=cost(2),
        compiler_params=pltpu.CompilerParams(vmem_limit_bytes=16 * MB),
    )
    mix_plane = exchange(mix_column.reshape(XY, PROWS, 512), ("x", "y"))
    whole = jnp.concatenate(
        [
            jnp.sum(mix_plane.astype(F32), axis=0),
            jnp.sum(out_column[:, :PROWS].astype(F32), axis=0),
        ],
        axis=1,
    ).astype(BF16)
    mine = exchange(jnp.broadcast_to(whole[None], (XY, PROWS, PCOLS)), ("x", "y"))
    other = lax.ppermute(mine, "core", [(0, 1), (1, 0)])

    squares = call(
        square_kernel,
        [((NZ, 8, 128), F32)],
        (mine, other),
        cost_estimate=cost(1),
        compiler_params=pltpu.CompilerParams(vmem_limit_bytes=16 * MB),
    )
    squares = exchange(squares, "z")
    table_grad = call(
        table_kernel,
        [((256, D), F32)],
        (gathered, names),
        specs=[pinned, vmem()],
        outs_specs=anywhere,
        scratch_shapes=[
            pltpu.VMEM((2, NZ * USED // 2, D), BF16),
            pltpu.VMEM((256, D), F32),
            pltpu.SemaphoreType.DMA((6,)),
        ],
        cost_estimate=cost(3),
        compiler_params=pltpu.CompilerParams(vmem_limit_bytes=60 * MB),
    )
    squares, table_grad = lax.optimization_barrier((squares, table_grad))
    mix_grad, out_grad = call(
        scale_kernel,
        [((TOK, 4 * AW), F32), ((64, D), F32)],
        (mine, other, squares),
        cost_estimate=cost(2),
        compiler_params=pltpu.CompilerParams(vmem_limit_bytes=16 * MB),
    )
    return (layer_out, table_grad, mix_grad, out_grad)


def solution(mesh):
    cube = Mesh(mesh.devices.reshape(4, 4, 2, 8), ALL)
    in_specs = (
        P(TABLE, None),
        P(ALL),
        P(ALL, None),
        P(ALL, None),
        P("z", None),
        P("z", None),
        P(),
        P(),
        P(ALL, None),
    )
    out_specs = (
        P(ALL, None),
        P(ALL, None),
        P("z", None),
        P("z", None),
    )
    return jax.shard_map(shards, mesh=cube, in_specs=in_specs, out_specs=out_specs, check_vma=False)
```

```python
import jax
import jax.numpy as jnp
from jax import lax
from jax.experimental import pallas as pl
from jax.experimental.pallas import tpu as pltpu
from jax.sharding import Mesh
from jax.sharding import PartitionSpec as P

H = 4
DH = 128
MAXLEN = 64
TOK = 128
D = 1024
AW = H * DH
OWNERS = 32
CAP = 6
SLOTS = 8
NZ = 8
XY = 16
PROWS = 16
PCOLS = 640
USED = OWNERS * CAP
TABLE = ("x", "y", "core")
ALL = ("x", "y", "core", "z")
F32 = jnp.float32
BF16 = jnp.bfloat16
MB = 1024 * 1024


def mm(a, b):
    return lax.dot_general(a, b, (((1,), (0,)), ((), ())), preferred_element_type=F32)


def mm_nt(a, b):
    return lax.dot_general(a, b, (((1,), (1,)), ((), ())), preferred_element_type=F32)


def mm_tn(a, b):
    return lax.dot_general(a, b, (((0,), (0,)), ((), ())), preferred_element_type=F32)


def iota(shape, dim):
    return lax.broadcasted_iota(jnp.int32, shape, dim)


def share_kernel(mix_ref, out_ref, share_ref, buf, sems):
    core = lax.axis_index("core")
    parts = (
        (mix_ref.at[:, pl.ds(pl.multiple_of(core * D, D), D)], pl.ds(0, TOK)),
        (out_ref.at[pl.ds(pl.multiple_of(core * 32, 32), 32), :], pl.ds(TOK, 32)),
    )
    inward, outward = [], []
    for i, (source, place) in enumerate(parts):
        inward.append(pltpu.make_async_copy(source, buf.at[place, :], sems.at[i]))
        outward.append(
            pltpu.make_async_copy(buf.at[place, :], share_ref.at[place, :], sems.at[2 + i])
        )
    for copy in inward:
        copy.start()
    for arrived, copy in zip(inward, outward):
        arrived.wait()
        copy.start()
    for copy in outward:
        copy.wait()


def plan_kernel(owner_ref, row_ref, req_ref, tgt_ref):
    square = (TOK, TOK)
    lane = iota(square, 1)

    def column(values):
        return jnp.broadcast_to(values.astype(F32), square).T

    row = row_ref[...]
    owner = column(owner_ref[...])
    low, high = column(row & 127), column(row >> 7)
    onehot = owner == lane.astype(F32)
    onehot_f = onehot.astype(F32)
    onehot_b = onehot_f.astype(BF16)
    earlier = (lane < iota(square, 0)).astype(F32).astype(BF16)
    before = mm(earlier, onehot_b)
    slot = jnp.sum(before * onehot_f, axis=1, keepdims=True)
    tgt_ref[...] = (owner * SLOTS + slot).astype(jnp.int32)
    here = slot == lane.astype(F32)
    low = jnp.where(here, low, 0.0).astype(BF16)
    high = jnp.where(here, high, 0.0).astype(BF16)
    requests = mm_tn(onehot_b, low) + 128.0 * mm_tn(onehot_b, high)
    req_ref[...] = requests[:OWNERS].astype(jnp.int32)


def chosen(tgt_ref):
    return (tgt_ref[:, :1] == iota((TOK, OWNERS * SLOTS), 1)).astype(F32).astype(BF16)


def layer_kernel(
    lens_ref, got_ref, tgt_ref, weights_ref, gin_ref, gat_ref, ct_ref,
    out_ref, keep_ref, send_ref, keep2_ref, send2_ref, dmx, xhat_ref, rstd_ref,
):
    core = lax.axis_index("core")
    emb = mm(chosen(tgt_ref), got_ref[...])
    gin = gin_ref[...]
    gat = gat_ref[...]
    centered = emb - jnp.mean(emb, axis=1, keepdims=True)
    rstd = lax.rsqrt(jnp.mean(centered * centered, axis=1, keepdims=True) + 1e-05)
    xhat = centered * rstd
    normed = (xhat * gin).astype(BF16)

    position, other = iota((TOK, TOK), 0), iota((TOK, TOK), 1)
    seg_row = jnp.zeros((TOK, TOK), jnp.int32)
    seg_col = jnp.zeros((TOK, TOK), jnp.int32)
    end = 0
    for user in range(lens_ref.shape[1]):
        end = end + lens_ref[0, user]
        seg_row = seg_row + (position >= end).astype(jnp.int32)
        seg_col = seg_col + (other >= end).astype(jnp.int32)
    allowed = (seg_row == seg_col) & (other <= position)

    mix0, mix1 = (
        mm(normed, weights_ref[half, :, :TOK, :].reshape(D, D)) for half in range(2)
    )

    sig0, sig1 = jax.nn.sigmoid(mix0), jax.nn.sigmoid(mix1)
    act0, act1 = (mix0 * sig0).astype(BF16), (mix1 * sig1).astype(BF16)
    slope0 = sig0 * (1.0 + mix0 * (1.0 - sig0))
    slope1 = sig1 * (1.0 + mix1 * (1.0 - sig1))
    gate_u = act0[:, :AW].astype(F32)

    heads = []
    attended = []
    for h in range(H):
        val = act0[:, AW + h * DH : AW + (h + 1) * DH]
        qry = act1[:, h * DH : (h + 1) * DH]
        key = act1[:, AW + h * DH : AW + (h + 1) * DH]
        score = mm_nt(qry, key) * DH ** (-0.5)
        sig = jax.nn.sigmoid(score)
        wgt = (jnp.where(allowed, score * sig, 0.0) / MAXLEN).astype(BF16)
        attended.append(mm(wgt, val).astype(BF16))
        slope = jnp.where(allowed, sig * (1.0 + score * (1.0 - sig)), 0.0) * (
            DH ** (-0.5) / MAXLEN
        )
        heads.append((val, qry, key, wgt, slope))
    att = jnp.concatenate(attended, axis=1).astype(F32)
    acent = att - jnp.mean(att, axis=1, keepdims=True)
    arstd = lax.rsqrt(jnp.mean(acent * acent, axis=1, keepdims=True) + 1e-05)
    ahat = acent * arstd
    scaled = ahat * gat
    gated = (scaled * gate_u).astype(BF16)

    w_out = jnp.stack([weights_ref[half, :, TOK:, :] for half in range(2)], axis=1)
    w_out = w_out.reshape(AW, D)
    ct = ct_ref[...]
    out_ref[...] = (emb + mm(gated, w_out)).astype(BF16)

    d_gated = mm_nt(ct, w_out).astype(BF16).astype(F32)
    d_gate = (d_gated * scaled).astype(BF16).astype(F32)
    d_ahat = d_gated * gate_u * gat
    d_att = arstd * (
        d_ahat
        - jnp.mean(d_ahat, axis=1, keepdims=True)
        - ahat * jnp.mean(d_ahat * ahat, axis=1, keepdims=True)
    )
    d_att = d_att.astype(BF16)
    d_val, d_qry, d_key = [], [], []
    for h in range(H):
        val, qry, key, wgt, slope = heads[h]
        d_head = d_att[:, h * DH : (h + 1) * DH]
        d_wgt = mm_nt(d_head, val).astype(BF16).astype(F32)
        d_val.append(mm_tn(wgt, d_head).astype(BF16))
        d_score = (d_wgt * slope).astype(BF16)
        d_qry.append(mm(d_score, key).astype(BF16))
        d_key.append(mm_tn(d_score, qry).astype(BF16))
    d_act0 = jnp.concatenate([d_gate] + [v.astype(F32) for v in d_val], axis=1)
    d_act1 = jnp.concatenate([v.astype(F32) for v in d_qry + d_key], axis=1)
    d_mix0 = (d_act0 * slope0).astype(BF16)
    d_mix1 = (d_act1 * slope1).astype(BF16)
    dmx[0] = d_mix0
    dmx[1] = d_mix1
    xhat_ref[...] = xhat
    rstd_ref[...] = jnp.broadcast_to(rstd, (TOK, TOK))
    for side, dst, dst2 in ((1 - core, send_ref, send2_ref), (core, keep_ref, keep2_ref)):
        dst[:, 0:1024] = normed
        dst[:, 1024:2048] = dmx[side]
        dst2[:, 0:512] = gated
        dst2[:, 512:1024] = ct_ref[:, pl.ds(pl.multiple_of(side * AW, AW), AW)]


def rows_kernel(tgt_ref, weights_ref, gin_ref, ct_ref, dmx, xhat_ref, rstd_ref, slots_ref):
    d_normed = mm_nt(dmx[0], weights_ref[0, :, :TOK, :].reshape(D, D))
    d_normed = d_normed + mm_nt(dmx[1], weights_ref[1, :, :TOK, :].reshape(D, D))
    d_xhat = d_normed.astype(BF16).astype(F32) * gin_ref[...]
    xhat = xhat_ref[...]
    d_emb = (
        rstd_ref[:, :1]
        * (
            d_xhat
            - jnp.mean(d_xhat, axis=1, keepdims=True)
            - xhat * jnp.mean(d_xhat * xhat, axis=1, keepdims=True)
        )
        + ct_ref[...].astype(F32)
    ).astype(BF16)
    slots_ref[...] = mm_tn(chosen(tgt_ref), d_emb).astype(BF16)


def both(keep_ref, theirs_ref, first, last):
    return jnp.concatenate([keep_ref[:, first:last], theirs_ref[:, first:last]], axis=0)


def mix_kernel(keep_ref, theirs_ref, mix_ref, mix, sems):
    copies = []
    d_mix = both(keep_ref, theirs_ref, 1024, 2048)
    for z in range(NZ):
        grad = mm_tn(both(keep_ref, theirs_ref, z * TOK, (z + 1) * TOK), d_mix)
        for p in range(XY):
            part = grad[8 * p : 8 * p + 8]
            mix[z, p] = jnp.concatenate([part[:, :512], part[:, 512:]], axis=0).astype(BF16)
        copies.append(pltpu.make_async_copy(mix.at[z], mix_ref.at[z], sems.at[z]))
        copies[-1].start()
    for copy in copies:
        copy.wait()


def out_kernel(keep_ref, theirs_ref, out):
    grad = mm_tn(both(keep_ref, theirs_ref, 0, 512), both(keep_ref, theirs_ref, 512, 1024))
    for z in range(NZ):
        for p in range(XY):
            r, c = z * 64 + (p // 2) * 8, (p % 2) * 256
            part = grad[r : r + 8, c : c + 256]
            out[p, z * PROWS : (z + 1) * PROWS] = jnp.concatenate(
                [part[:, :128], part[:, 128:]], axis=0
            ).astype(BF16)


def column_kernel(plane_ref, asked_ref, out_ref):
    total = jnp.sum(plane_ref[...].astype(F32), axis=0).astype(BF16)
    asked = asked_ref[...]
    low, high = ((part).astype(F32).astype(BF16) for part in (asked & 127, asked >> 7))
    for z in range(NZ):
        out_ref[z, :PROWS] = total[z * PROWS : (z + 1) * PROWS]
        out_ref[z, PROWS : PROWS + OWNERS] = low
        out_ref[z, PROWS + OWNERS :] = high


def pack_kernel(rows_ref, out_ref):
    r, k = iota((USED, OWNERS * SLOTS), 0), iota((USED, OWNERS * SLOTS), 1)
    take = (r // CAP) * SLOTS + r % CAP == k
    out_ref[...] = mm(take.astype(F32).astype(BF16), rows_ref[...]).astype(BF16)


def names_kernel(column_ref, out_ref):
    first = lax.axis_index("z") * 256
    count = NZ * USED
    low = column_ref[:, PROWS : PROWS + OWNERS].reshape(NZ * OWNERS, 128)
    high = column_ref[:, PROWS + OWNERS :].reshape(NZ * OWNERS, 128)
    row, col = iota((count, NZ * OWNERS), 0), iota((count, NZ * OWNERS), 1)
    owner = (row // CAP == col).astype(F32).astype(BF16)
    lane = iota((count, 128), 1)
    spread = mm(owner, low) + 128.0 * mm(owner, high)
    column = jnp.sum(
        jnp.where(iota((count, 128), 0) % CAP == lane, spread, 0.0), axis=1, keepdims=True
    )
    names = jnp.zeros((128, 128), F32)
    for line in range(count // 128):
        names = jnp.where(
            iota((128, 128), 1) == line, column[128 * line : 128 * line + 128], names
        )
    out_ref[...] = names.T[:PROWS].astype(jnp.int32) - first


def table_kernel(rows_ref, names_ref, out_ref, buf, total, sems):
    half = NZ * USED // 2
    copies = [
        pltpu.make_async_copy(
            rows_ref.at[pl.ds(part * half, half), :], buf.at[part], sems.at[part]
        )
        for part in range(2)
    ]
    for copy in copies:
        copy.start()
    place = iota((256, 128), 0)
    lines = half // 128
    picks = [
        jnp.concatenate(
            [
                (place == names_ref[line : line + 1, :]).astype(F32).astype(BF16)
                for line in range(part * lines, (part + 1) * lines)
            ],
            axis=1,
        )
        for part in range(2)
    ]
    copies[0].wait()
    total[...] = mm(picks[0], buf[0])
    copies[1].wait()
    outs = []
    for n in range(4):
        cols = slice(256 * n, 256 * n + 256)
        total[:, cols] += mm(picks[1], buf[1, :, cols])
        block = pl.ds(256 * n, 256)
        outs.append(
            pltpu.make_async_copy(total.at[:, block], out_ref.at[:, block], sems.at[2 + n])
        )
        outs[-1].start()
    for copy in outs:
        copy.wait()


def square_kernel(mine_ref, other_ref, out_ref):
    total = jnp.zeros((PROWS, PCOLS), F32)
    for sums_ref in (mine_ref, other_ref):
        for i in range(XY):
            part = sums_ref[i].astype(F32)
            total = total + part * part
    mix = jnp.sum(total[:, :512])
    out = jnp.sum(total[:, 512:])
    lane = iota((NZ, 8, 128), 2)
    out_ref[...] = jnp.where(lane == 0, mix, jnp.where(lane == 1, out, 0.0))


def scale_kernel(mine_ref, other_ref, squares_ref, mix_ref, out_ref):
    total = jnp.sum(squares_ref[...], axis=0)[0:1]
    mix_sq, out_sq = total[:, 0:1], total[:, 1:2]
    mix_scale = jnp.minimum(1.0, 1.0 / jnp.sqrt(mix_sq / float(D * 4 * AW) + 1e-06))
    out_scale = jnp.minimum(1.0, 1.0 / jnp.sqrt(out_sq / float(D * AW) + 1e-06))
    core = lax.axis_index("core")
    for side, sums_ref in ((core, mine_ref), (1 - core, other_ref)):
        for p in range(XY):
            sums = sums_ref[p].astype(F32)
            mix, out = sums[:, :512] * mix_scale, sums[:, 512:] * out_scale
            for part in range(2):
                r = p * 8
                c = pl.multiple_of(side * D + part * 512, 512)
                mix_ref[r : r + 8, pl.ds(c, 512)] = mix[8 * part : 8 * part + 8]
                r = (p // 2) * 8
                c = pl.multiple_of(side * AW + (p % 2) * 256 + part * 128, 128)
                out_ref[r : r + 8, pl.ds(c, 128)] = out[8 * part : 8 * part + 8]


def vmem():
    return pl.BlockSpec(memory_space=pltpu.VMEM)


def call(body, outs, args, specs=None, outs_specs=None, **kwargs):
    shapes = [jax.ShapeDtypeStruct(s, t) for s, t in outs]
    one = len(shapes) == 1
    return pl.pallas_call(
        body,
        out_shape=shapes[0] if one else shapes,
        in_specs=specs or [vmem()] * len(args),
        out_specs=outs_specs or (vmem() if one else [vmem()] * len(shapes)),
        **kwargs,
    )(*args)


def cost(us):
    return pl.CostEstimate(flops=0, bytes_accessed=int(us * 3.0e6), transcendentals=0)


def exchange(array, axes):
    return lax.all_to_all(array, axes, split_axis=0, concat_axis=0, tiled=True)


def shards(
    item_table, item_row, item_owner, user_lengths, w_mix, w_out, gain_in, gain_attn, cotangent
):
    anywhere = pl.BlockSpec(memory_space=pl.ANY)
    pinned = pl.BlockSpec(memory_space=pltpu.HBM)
    share = call(
        share_kernel,
        [((TOK + 32, D), BF16)],
        (w_mix, w_out),
        specs=[anywhere, anywhere],
        outs_specs=anywhere,
        scratch_shapes=[pltpu.VMEM((TOK + 32, D), BF16), pltpu.SemaphoreType.DMA((4,))],
        compiler_params=pltpu.CompilerParams(vmem_limit_bytes=60 * MB),
    )
    weights = lax.all_gather(share, ("core", "z"), axis=0, tiled=True).reshape(2, NZ, 160, D)

    requests, target = call(
        plan_kernel,
        [((OWNERS, 128), jnp.int32), ((TOK, TOK), jnp.int32)],
        (item_owner.reshape(1, TOK), item_row.reshape(1, TOK)),
    )
    asked = exchange(requests, TABLE)
    wanted = asked[:, :SLOTS].reshape(OWNERS * SLOTS)
    found = item_table.at[wanted].get(mode="promise_in_bounds")
    got = exchange(found.reshape(OWNERS, SLOTS, D), TABLE)

    smem = pl.BlockSpec(memory_space=pltpu.SMEM)
    gin = gain_in.reshape(1, D)
    layer_out, keep, send, keep2, send2, d_mix, xhat, rstd = call(
        layer_kernel,
        [
            ((TOK, D), BF16),
            ((TOK, 2 * D), BF16),
            ((TOK, 2 * D), BF16),
            ((TOK, D), BF16),
            ((TOK, D), BF16),
            ((2, TOK, D), BF16),
            ((TOK, D), F32),
            ((TOK, TOK), F32),
        ],
        (
            user_lengths,
            got.reshape(OWNERS * SLOTS, D),
            target,
            weights,
            gin,
            gain_attn.reshape(1, AW),
            cotangent,
        ),
        specs=[smem] + [vmem()] * 6,
        cost_estimate=cost(7),
        compiler_params=pltpu.CompilerParams(vmem_limit_bytes=32 * MB),
    )

    theirs = lax.ppermute(send, "core", [(0, 1), (1, 0)])
    mix_part = call(
        mix_kernel,
        [((NZ, XY, PROWS, 512), BF16)],
        (keep, theirs),
        outs_specs=anywhere,
        scratch_shapes=[
            pltpu.VMEM((NZ, XY, PROWS, 512), BF16),
            pltpu.SemaphoreType.DMA((NZ,)),
        ],
        cost_estimate=cost(3),
        compiler_params=pltpu.CompilerParams(vmem_limit_bytes=30 * MB),
    )
    mix_part, d_mix, send2 = lax.optimization_barrier((mix_part, d_mix, send2))
    mix_column = lax.psum_scatter(
        mix_part.reshape(NZ * XY * PROWS, 512), "z", scatter_dimension=0, tiled=True
    )

    grad_slots = call(
        rows_kernel,
        [((OWNERS * SLOTS, D), BF16)],
        (target, weights, gin, cotangent, d_mix, xhat, rstd),
        cost_estimate=cost(3),
        compiler_params=pltpu.CompilerParams(vmem_limit_bytes=32 * MB),
    )
    received = exchange(grad_slots.reshape(OWNERS, SLOTS, D), TABLE)
    packed = call(
        pack_kernel,
        [((USED, D), BF16)],
        (received.reshape(OWNERS * SLOTS, D),),
        cost_estimate=cost(2),
        compiler_params=pltpu.CompilerParams(vmem_limit_bytes=16 * MB),
    )
    out_part = call(
        out_kernel,
        [((XY, NZ * PROWS, 128), BF16)],
        (keep2, lax.ppermute(send2, "core", [(0, 1), (1, 0)])),
        cost_estimate=cost(1),
        compiler_params=pltpu.CompilerParams(vmem_limit_bytes=16 * MB),
    )
    out_part, packed = lax.optimization_barrier((out_part, packed))
    gathered = lax.all_gather(packed, "z", axis=0, tiled=True)

    out_column = call(
        column_kernel,
        [((NZ, PROWS + 2 * OWNERS, 128), BF16)],
        (exchange(out_part, ("x", "y")), asked),
        cost_estimate=cost(1),
        compiler_params=pltpu.CompilerParams(vmem_limit_bytes=16 * MB),
    )
    out_column = exchange(out_column, "z")
    mix_column, out_column = lax.optimization_barrier((mix_column, out_column))
    names = call(
        names_kernel,
        [((PROWS, 128), jnp.int32)],
        (out_column,),
        cost_estimate=cost(2),
        compiler_params=pltpu.CompilerParams(vmem_limit_bytes=16 * MB),
    )
    mix_plane = exchange(mix_column.reshape(XY, PROWS, 512), ("x", "y"))
    whole = jnp.concatenate(
        [
            jnp.sum(mix_plane.astype(F32), axis=0),
            jnp.sum(out_column[:, :PROWS].astype(F32), axis=0),
        ],
        axis=1,
    ).astype(BF16)
    mine = exchange(jnp.broadcast_to(whole[None], (XY, PROWS, PCOLS)), ("x", "y"))
    other = lax.ppermute(mine, "core", [(0, 1), (1, 0)])

    squares = call(
        square_kernel,
        [((NZ, 8, 128), F32)],
        (mine, other),
        cost_estimate=cost(1),
        compiler_params=pltpu.CompilerParams(vmem_limit_bytes=16 * MB),
    )
    squares = exchange(squares, "z")
    table_grad = call(
        table_kernel,
        [((256, D), F32)],
        (gathered, names),
        specs=[pinned, vmem()],
        outs_specs=anywhere,
        scratch_shapes=[
            pltpu.VMEM((2, NZ * USED // 2, D), BF16),
            pltpu.VMEM((256, D), F32),
            pltpu.SemaphoreType.DMA((6,)),
        ],
        cost_estimate=cost(3),
        compiler_params=pltpu.CompilerParams(vmem_limit_bytes=60 * MB),
    )
    squares, table_grad = lax.optimization_barrier((squares, table_grad))
    mix_grad, out_grad = call(
        scale_kernel,
        [((TOK, 4 * AW), F32), ((64, D), F32)],
        (mine, other, squares),
        cost_estimate=cost(2),
        compiler_params=pltpu.CompilerParams(vmem_limit_bytes=16 * MB),
    )
    return (layer_out, table_grad, mix_grad, out_grad)


def solution(mesh):
    cube = Mesh(mesh.devices.reshape(4, 4, 2, 8), ALL)
    in_specs = (
        P(TABLE, None),
        P(ALL),
        P(ALL, None),
        P(ALL, None),
        P("z", None),
        P("z", None),
        P(),
        P(),
        P(ALL, None),
    )
    out_specs = (
        P(ALL, None),
        P(ALL, None),
        P("z", None),
        P("z", None),
    )
    return jax.shard_map(shards, mesh=cube, in_specs=in_specs, out_specs=out_specs, check_vma=False)
```
